32 devices in a mesh: clus: 8 (over z, x), col: 4 (over y, core).
Axes of the slice: x: 2, y: 2, z: 4, core: 2. Of those that a mesh axis runs over, the one named last changes fastest.
Arguments:
- features: bfloat16 [3, 12288, 2048], P(None, 'clus', 'col'), may hold values from -12 to 12
- neighbours: int32 [3, 12288, 16], P(None, 'clus'), may hold values from 0 to 1535
- node_counts: int32 [3, 8], P(None, 'clus'), may hold values from 768 to 1536, as said below
- row_counts: int32 [8], replicated, may hold values from 1 to 512, 2048 in all
- master_weight: float32 [4096, 2048], P('clus', 'col'), may hold values from -0.125 to 0.125
- weight_first: float32 [4096, 2048], P('clus', 'col'), may hold values from -40 to 40
- weight_second: float32 [4096, 2048], P('clus', 'col'), may hold values from 184.32 to 737.28
- master_bias: float32 [2048], P('col'), may hold values from -1.75 to 1.75
- bias_first: float32 [2048], P('col'), may hold values from -64 to 64
- bias_second: float32 [2048], P('col'), may hold values from 442.368 to 1843.2
- out_grad: bfloat16 [3, 12288, 2048], P(None, 'clus', 'col'), may hold values from -6 to 6
Outputs:
- layer_out: bfloat16 [3, 12288, 2048], P(None, 'clus', 'col')
- feature_grad: bfloat16 [3, 12288, 2048], P(None, 'clus', 'col')
- weight_new: float32 [4096, 2048], P('clus', 'col')
- weight_first_new: float32 [4096, 2048], P('clus', 'col')
- weight_second_new: float32 [4096, 2048], P('clus', 'col')
- bias_new: float32 [2048], P('col')
- bias_first_new: float32 [2048], P('col')
- bias_second_new: float32 [2048], P('col')
The draws below stay inside these ranges and needn't reach their ends.
Inputs may be any that keep to these rules, and one draw needn't show every extreme that they name: `node_counts`: in every micro-batch some cluster has all 1536 slots live. `row_counts`: some owner holds exactly 512 rows.
All inputs are finite; a program needn't handle non-finite values.
Results may differ from the reference program's by a relative error of at most 0.0071.
Values may be sent and summed in bfloat16 or wider, within the bound.
A program may use at most 256 MiB of HBM per device.

```python
import math
import jax
import jax.numpy as jnp
import numpy as np
from jax import lax

D = 2048
NODE_DEV = 1536
MB = 3
NB = 16
STEP = 10
GROUPS = 8
NODES = 12288
CAP = 512
ROWS_ALL = 36864


def draw_node_counts(key, part):
    key = jax.random.fold_in(key, 7)
    first_key, second_key = jax.random.split(key)
    counts = jax.random.randint(first_key, (MB, GROUPS), NODE_DEV // 2, NODE_DEV + 1)
    fullest = jax.random.randint(second_key, (MB, 1), 0, GROUPS)
    places = jnp.arange(GROUPS, dtype=jnp.int32)[None, :]
    return jnp.where(places == fullest, NODE_DEV, counts).astype(jnp.int32)


def touch_ends(result, key, low, largest):
    longest = result.shape.index(max(result.shape))
    spots = []
    for shift in (0, 1):
        where = [jax.random.randint(jax.random.fold_in(key, axis), (), 0, length) for axis, length in enumerate(result.shape)]
        where[longest] = (where[longest] + shift) % result.shape[longest]
        spots.append(tuple(where))
    return result.at[spots[0]].set(low).at[spots[1]].set(largest)


def level_of(own_key, extent, cuts, low, largest):
    def one(dim, blocks):
        draws = jax.random.uniform(jax.random.fold_in(jax.random.fold_in(own_key, 6), dim), (blocks,), jnp.float32, low / len(cuts), largest / len(cuts))
        return jnp.repeat(jnp.exp(draws), extent[dim] // blocks).reshape((-1,) + (1,) * (len(extent) - dim - 1))

    factor_of = one(*cuts[0])
    for cut in cuts[1:]:
        factor_of = factor_of * one(*cut)
    return factor_of


def profile(count, total, limit, slope):
    portions = [(1 << 20) // math.isqrt(grade ** slope) + 1 for grade in range(2, count + 1)]
    spare, given = total - limit - (count - 1), [1] * (count - 1)
    while spare > 0:
        movable = [i for i in range(count - 1) if given[i] < limit]
        whole, budget = sum([portions[i] for i in movable]), spare
        for i in movable:
            addition = min(limit - given[i], max(1, budget * portions[i] // whole), spare)
            given[i] = given[i] + addition
            spare = spare - addition
    return np.array([limit] + given)


def ragged(own_key, number_of, total, reach, skew):
    if number_of == 2:
        one = jax.random.randint(own_key, (), max(1, total - reach), min(reach, total - 1) + 1)
        return jnp.stack([one, total - one])
    sizes = jnp.asarray(profile(number_of, total, reach, skew), jnp.int32)
    twos = (number_of - 1) // 2
    donor, receiver = sizes[1:1 + 2 * twos:2], sizes[2:2 + 2 * twos:2]
    slack = jnp.minimum(donor - 1, reach - receiver)
    moved = jax.random.randint(jax.random.fold_in(own_key, 1), (twos,), 0, 1 << 20) % (slack + 1)
    sizes = sizes.at[1:1 + 2 * twos:2].set(donor - moved).at[2:2 + 2 * twos:2].set(receiver + moved)
    return sizes[jax.random.permutation(jax.random.fold_in(own_key, 2), number_of)]


def centred(rng, dims, spread, limit, cuts=(), kind=jnp.bfloat16):
    level = level_of(rng, dims, cuts, -0.22, 0.18) if cuts else 1.0
    array = jax.random.normal(rng, dims, jnp.float32) * spread * level
    return jnp.minimum(jnp.maximum(array, -limit), limit).astype(kind)


def setup_inputs(seed: int = 0) -> dict:
    seeds = jax.random.split(jax.random.key(seed), 12)
    features = centred(seeds[0], (MB, NODES, D), 2.0, 12.0, ((1, 8), (2, 4)))
    neighbours = touch_ends(jax.random.randint(seeds[1], (MB, NODES, NB), 0, NODE_DEV), jax.random.fold_in(seeds[1], 1), 0, NODE_DEV - 1).astype(jnp.int32)
    node_counts = draw_node_counts(jax.random.fold_in(seeds[11], 71), 0)
    row_counts = ragged(seeds[3], GROUPS, D, CAP, 2).astype(jnp.int32)
    master_weight = centred(seeds[4], (GROUPS * CAP, D), D ** -0.5, 0.125, ((0, 8), (1, 4)), jnp.float32)
    weight_first = centred(seeds[5], (GROUPS * CAP, D), (0.033 * ROWS_ALL ** 0.5), 40.0, ((0, 8), (1, 4)), jnp.float32)
    weight_second = jnp.clip(jnp.exp(math.log(737.28) - 1.3862944 * jax.random.uniform(seeds[6], (GROUPS * CAP, D), jnp.float32) ** level_of(seeds[6], (GROUPS * CAP, D), ((0, 8), (1, 4)), -0.2, 0.2)), 184.32, 737.28)
    master_bias = centred(seeds[7], (D,), 0.3, 1.75, ((0, 4),), jnp.float32)
    bias_first = centred(seeds[8], (D,), (0.053 * ROWS_ALL ** 0.5), 64.0, ((0, 4),), jnp.float32)
    bias_second = jnp.clip(jnp.exp(math.log(1843.2) - 1.4271163 * jax.random.uniform(seeds[9], (D,), jnp.float32) ** level_of(seeds[9], (D,), ((0, 4),), -0.2, 0.2)), 442.368, 1843.2)
    out_grad = centred(seeds[10], (MB, NODES, D), 1.0, 6.0, ((1, 8), (2, 4)))
    return {"features": features, "neighbours": neighbours, "node_counts": node_counts, "row_counts": row_counts, "master_weight": master_weight, "weight_first": weight_first, "weight_second": weight_second, "master_bias": master_bias, "bias_first": bias_first, "bias_second": bias_second, "out_grad": out_grad}


HIGHEST = lax.Precision.HIGHEST
BETA_ONE = 0.9
BETA_TWO = 0.95
EPSILON = 1e-08
DECAY = 0.1
RATE_WEIGHT = 0.06
RATE_BIAS = 0.6
LAMBDA_DIAG = 1.0

@jax.custom_vjp
def low(v):
    return lax.optimization_barrier(v.astype(jnp.bfloat16)).astype(jnp.float32)

@jax.custom_vjp
def low_back(v):
    return v

def low_keep(v):
    return (low(v), None)

def low_pass(kept, grad):
    return (grad,)

def back_keep(v):
    return (v, None)

def back_low(kept, grad):
    return (low(grad),)
low.defvjp(low_keep, low_pass)
low_back.defvjp(back_keep, back_low)

def row_slots(row_counts):
    starts = jnp.cumsum(row_counts) - row_counts
    row_ids = jnp.arange(D, dtype=jnp.int32)
    owners = lax.optimization_barrier(jnp.sum((starts[None, :] <= row_ids[:, None]).astype(jnp.int32), axis=1)) - 1
    return (owners * CAP + row_ids - starts[owners]).astype(jnp.int32)

def slot_rows(row_counts):
    starts = jnp.cumsum(row_counts) - row_counts
    slot_ids = jnp.arange(GROUPS * CAP, dtype=jnp.int32)
    owners = slot_ids // CAP
    offsets = slot_ids % CAP
    row_ids = jnp.clip(starts[owners] + offsets, 0, D - 1).astype(jnp.int32)
    return (row_ids, (offsets < row_counts[owners]).astype(jnp.float32))

def cluster_forward(weight_low, bias_row, cluster):
    feature_rows, neighbour_rows, node_count = cluster
    positions = jnp.arange(NODE_DEV, dtype=jnp.int32)
    live_rows = (positions < node_count).astype(jnp.float32)
    counted = lax.optimization_barrier(jnp.sum((neighbour_rows[:, :, None] == positions[None, None, :]).astype(jnp.float32), axis=1))
    counted = counted * live_rows[:, None] * live_rows[None, :]
    degree = 1.0 + lax.optimization_barrier(jnp.sum(counted, axis=1))
    self_term = 1.0 + LAMBDA_DIAG * (1.0 + jnp.diagonal(counted))
    row_scale = live_rows / degree
    neighbour_sum = low_back(jnp.dot(counted, feature_rows, precision=HIGHEST))
    mixed_rows = low(low_back((neighbour_sum + self_term[:, None] * feature_rows) * row_scale[:, None]))
    preact = low_back(jnp.dot(mixed_rows, weight_low, precision=HIGHEST) + bias_row)
    return jax.nn.silu(preact) * live_rows[:, None]

def layer_forward(feature_values, weight, bias_row, neighbours, node_counts):
    feature_rows = feature_values.reshape(MB * GROUPS, NODE_DEV, D)
    neighbour_rows = neighbours.reshape(MB * GROUPS, NODE_DEV, NB)
    counts = node_counts.reshape(MB * GROUPS)
    weight_low = low(weight)
    cluster_step = jax.checkpoint(lambda cluster: cluster_forward(weight_low, bias_row, cluster))
    outputs = lax.map(cluster_step, (feature_rows, neighbour_rows, counts))
    return outputs.reshape(MB, GROUPS * NODE_DEV, D)

def adamw_update(current, first_moment, second_moment, gradient, step_rate):
    first_new = BETA_ONE * first_moment + (1.0 - BETA_ONE) * gradient
    second_new = BETA_TWO * second_moment + (1.0 - BETA_TWO) * gradient * gradient
    fixed_first = first_new / (1.0 - BETA_ONE ** STEP)
    fixed_second = second_new / (1.0 - BETA_TWO ** STEP)
    updated = current - step_rate * (fixed_first / (jnp.sqrt(fixed_second) + EPSILON) + DECAY * current)
    return (updated, first_new, second_new)

def reference(features, neighbours, node_counts, row_counts, master_weight, weight_first, weight_second, master_bias, bias_first, bias_second, out_grad):
    weight_rows = jnp.take(master_weight, row_slots(row_counts), axis=0)
    primal = features.astype(jnp.float32)

    def forward(feature_values, weight, bias_row):
        return layer_forward(feature_values, weight, bias_row, neighbours, node_counts)
    output, pullback = jax.vjp(forward, primal, weight_rows, master_bias)
    grad_features, grad_weight, grad_bias = pullback(out_grad.astype(jnp.float32))
    row_ids, live_slots = slot_rows(row_counts)
    slot_mask = live_slots[:, None]
    grad_slots = jnp.take(grad_weight, row_ids, axis=0) * slot_mask
    weight_new, first_new, second_new = adamw_update(master_weight, weight_first, weight_second, grad_slots, RATE_WEIGHT)
    bias_new, bias_first_new, bias_second_new = adamw_update(master_bias, bias_first, bias_second, grad_bias, RATE_BIAS)
    return (output.astype(jnp.bfloat16), grad_features.astype(jnp.bfloat16), weight_new * slot_mask, first_new * slot_mask, second_new * slot_mask, bias_new, bias_first_new, bias_second_new)
```

```python
import jax
import jax.numpy as jnp
from jax import lax
from jax.experimental import pallas as pl
from jax.experimental.pallas import tpu as pltpu
from jax.sharding import PartitionSpec as P

D = 2048
MB = 3
STEP = 10

BETA_ONE = 0.9
BETA_TWO = 0.95
EPSILON = 1e-08
DECAY = 0.1
RATE_WEIGHT = 0.06
RATE_BIAS = 0.6

LANES = 128
DIGIT_BITS = 5
DIGITS = 6


def adjacency_kernel(limit_ref, neighbour_ref, out_ref):
    limit = limit_ref[pl.program_id(0)]
    rows = neighbour_ref.shape[1]
    nodes = out_ref.shape[2]
    first_row = pl.program_id(1) * rows
    words = -(-(nodes // LANES) // DIGITS)
    table = neighbour_ref[0]
    row_ids = first_row + lax.broadcasted_iota(jnp.int32, table.shape, 0)
    valid = (table < limit) & (row_ids < limit)
    low = table & (LANES - 1)
    high = table >> 7
    digits = []
    for word in range(words):
        inside = valid & (high >= word * DIGITS) & (high < (word + 1) * DIGITS)
        shift = jnp.where(inside, (high - word * DIGITS) * DIGIT_BITS, 0)
        digits.append(jnp.where(inside, jnp.left_shift(1, shift), 0))
    lane = lax.broadcasted_iota(jnp.int32, (rows, LANES), 1)
    sums = [jnp.zeros((rows, LANES), jnp.int32) for _ in range(words)]
    for entry in range(table.shape[1]):
        hit = lane == low[:, entry : entry + 1]
        for word in range(words):
            sums[word] = sums[word] + jnp.where(hit, digits[word][:, entry : entry + 1], 0)
    own_row = first_row + lax.broadcasted_iota(jnp.int32, (rows, LANES), 0)
    for block in range(nodes // LANES):
        word, digit = block // DIGITS, block % DIGITS
        count = jnp.right_shift(sums[word], digit * DIGIT_BITS) & ((1 << DIGIT_BITS) - 1)
        count = jnp.where(lane + block * LANES == own_row, 2 * count + 2, count)
        out_ref[0, :, block * LANES : (block + 1) * LANES] = count.astype(jnp.float32).astype(
            jnp.bfloat16
        )


def adjacency(neighbours, limits):
    batches, nodes, entries = neighbours.shape
    rows = LANES
    return pl.pallas_call(
        adjacency_kernel,
        grid_spec=pltpu.PrefetchScalarGridSpec(
            num_scalar_prefetch=1,
            grid=(batches, nodes // rows),
            in_specs=[pl.BlockSpec((1, rows, entries), lambda b, r, limit: (b, r, 0))],
            out_specs=pl.BlockSpec((1, rows, nodes), lambda b, r, limit: (b, r, 0)),
        ),
        out_shape=jax.ShapeDtypeStruct((batches, nodes, nodes), jnp.bfloat16),
        cost_estimate=pl.CostEstimate(
            flops=batches * nodes * nodes * 12, bytes_accessed=batches * nodes * nodes * 2, transcendentals=0
        ),
        name="adjacency",
    )(limits, neighbours)


def adamw_update(current, first_moment, second_moment, gradient, step_rate):
    first_new = BETA_ONE * first_moment + (1.0 - BETA_ONE) * gradient
    second_new = BETA_TWO * second_moment + (1.0 - BETA_TWO) * gradient * gradient
    fixed_first = first_new / (1.0 - BETA_ONE**STEP)
    fixed_second = second_new / (1.0 - BETA_TWO**STEP)
    updated = current - step_rate * (
        fixed_first / (jnp.sqrt(fixed_second) + EPSILON) + DECAY * current
    )
    return (updated, first_new, second_new)


def flip(values, axis, bit):
    size = lax.axis_size(axis)
    return lax.ppermute(values, axis, [(i, i ^ bit) for i in range(size)])


def product(left, right):
    return jnp.dot(left, right, preferred_element_type=jnp.float32)


def product_back(left, right):
    return lax.dot_general(
        left, right, (((1,), (1,)), ((), ())), preferred_element_type=jnp.float32
    )


def product_rows(left, right):
    return lax.dot_general(
        left, right, (((0,), (0,)), ((), ())), preferred_element_type=jnp.float32
    )


def reduce_to_owners(grad_weight, starts, capacity):
    groups = lax.axis_size("clus")
    own = lax.axis_index("clus")
    half = grad_weight.shape[1] // 2
    side = (own & 1) == 0
    left, right = grad_weight[:, :half], grad_weight[:, half:]
    sent = jnp.where(side, right, left).astype(jnp.bfloat16)
    total = jnp.where(side, left, right) + flip(sent, "clus", 1).astype(jnp.float32)
    padded = jnp.concatenate([total, jnp.zeros((2 * capacity, half), jnp.float32)], axis=0)
    held = jnp.stack(
        [lax.dynamic_slice(padded, (starts[2 * q], 0), (2 * capacity, half)) for q in range(groups // 2)]
    )
    bit = 2
    while bit < groups:
        pairs = held.reshape(held.shape[0] // 2, 2, 2 * capacity, half)
        lower = (own & bit) == 0
        sent = jnp.where(lower, pairs[:, 1], pairs[:, 0]).astype(jnp.bfloat16)
        held = jnp.where(lower, pairs[:, 0], pairs[:, 1]) + flip(sent, "clus", bit).astype(jnp.float32)
        bit *= 2
    held = held[0]
    first = starts[own & ~1]
    mine = lax.dynamic_slice(held, (starts[own] - first, 0), (capacity, half))
    other = lax.dynamic_slice(held, (starts[own ^ 1] - first, 0), (capacity, half))
    got = flip(other.astype(jnp.bfloat16), "clus", 1).astype(jnp.float32)
    return jnp.where(
        side,
        jnp.concatenate([mine, got], axis=1),
        jnp.concatenate([got, mine], axis=1),
    )


def shards(
    features,
    neighbours,
    node_counts,
    row_counts,
    master_weight,
    weight_first,
    weight_second,
    master_bias,
    bias_first,
    bias_second,
    out_grad,
):
    groups = lax.axis_size("clus")
    capacity, width = master_weight.shape
    nodes = features.shape[1]
    own_group = lax.axis_index("clus")
    own_col = lax.axis_index("col")

    far = [flip(features[m], "col", 2) for m in range(MB)]
    slots = lax.all_gather(master_weight.astype(jnp.bfloat16), "clus", axis=0, tiled=True)

    owner_ids = jnp.arange(groups, dtype=jnp.int32)
    starts = jnp.sum(jnp.where(owner_ids[None, :] < owner_ids[:, None], row_counts[None, :], 0), axis=1)

    row_ids = jnp.arange(D, dtype=jnp.int32) ^ (own_col * width)
    reached = starts[None, :] <= row_ids[:, None]
    owners = jnp.sum(reached.astype(jnp.int32), axis=1) - 1
    start_of = jnp.max(jnp.where(reached, starts[None, :], 0), axis=1)
    weight = jnp.take(slots, owners * capacity + row_ids - start_of, axis=0).reshape(4, width, width)
    weight_mate = flip(jnp.concatenate([weight[1], weight[3]], axis=0), "col", 1)

    limits = node_counts[:, 0]
    matrix = adjacency(neighbours, limits)
    positions = jnp.arange(nodes, dtype=jnp.int32)
    grad_weight = [jnp.zeros((width, width), jnp.float32) for _ in range(4)]
    grad_bias = jnp.zeros((width,), jnp.float32)
    outputs, input_grads = [], []
    live, scale, mixed = [], [], []
    for m in range(MB):
        live_rows = (positions < limits[m]).astype(jnp.float32)
        degree = 1.0 + jnp.sum((neighbours[m] < limits[m]).astype(jnp.float32), axis=1) * live_rows
        live.append(live_rows[:, None])
        scale.append((live_rows / degree)[:, None])
        here = (product(matrix[m], features[m]) * scale[m]).astype(jnp.bfloat16)
        mixed.append([here, flip(here, "col", 1)])
    partial, pres = [], []
    for m in range(MB):
        there = (product(matrix[m], far[m]) * scale[m]).astype(jnp.bfloat16)
        mixed[m] += [there, flip(there, "col", 1)]
        preact = sum(product(mixed[m][b], weight[b]) for b in range(4)) + master_bias
        gate = jax.nn.sigmoid(preact)
        outputs.append((preact * gate * live[m]).astype(jnp.bfloat16))
        slope = gate * (1.0 + preact * (1.0 - gate))
        grad_pre = (out_grad[m].astype(jnp.float32) * live[m] * slope).astype(jnp.bfloat16)
        grad_mate = flip(grad_pre, "col", 1)
        pres.append((grad_pre, grad_mate))
        away = (
            product_back(grad_pre, weight[2]) + product_back(grad_mate, weight_mate[width:])
        ).astype(jnp.bfloat16)
        partial.append(flip(away, "col", 2))
        for b in range(4):
            grad_weight[b] = grad_weight[b] + product_rows(mixed[m][b], grad_pre)
        grad_bias = grad_bias + jnp.sum(grad_pre.astype(jnp.float32), axis=0)

    bit = 1
    while bit < groups:
        grad_bias = grad_bias + flip(grad_bias, "clus", bit)
        bit *= 2
    ordered = [
        sum(jnp.where((own_col ^ d) == b, grad_weight[d], 0.0) for d in range(4)) for b in range(4)
    ]
    grad_slots = reduce_to_owners(jnp.concatenate(ordered, axis=0), starts, capacity)

    for m in range(MB):
        grad_pre, grad_mate = pres[m]
        grad_mixed = (
            product_back(grad_pre, weight[0])
            + product_back(grad_mate, weight_mate[:width])
            + partial[m].astype(jnp.float32)
        ).astype(jnp.bfloat16)
        grad_sum = (grad_mixed.astype(jnp.float32) * scale[m]).astype(jnp.bfloat16)
        input_grads.append(product_rows(matrix[m], grad_sum).astype(jnp.bfloat16))

    slot_mask = (jnp.arange(capacity, dtype=jnp.int32) < row_counts[own_group]).astype(jnp.float32)[:, None]
    weight_new, first_new, second_new = adamw_update(
        master_weight, weight_first, weight_second, grad_slots, RATE_WEIGHT
    )
    bias_new, bias_first_new, bias_second_new = adamw_update(
        master_bias, bias_first, bias_second, grad_bias, RATE_BIAS
    )
    return (
        jnp.stack(outputs),
        jnp.stack(input_grads),
        jnp.where(slot_mask > 0, weight_new, 0.0),
        jnp.where(slot_mask > 0, first_new, 0.0),
        jnp.where(slot_mask > 0, second_new, 0.0),
        bias_new,
        bias_first_new,
        bias_second_new,
    )


def solution(mesh):
    in_specs = (
        P(None, "clus", "col"),
        P(None, "clus", None),
        P(None, "clus"),
        P(),
        P("clus", "col"),
        P("clus", "col"),
        P("clus", "col"),
        P("col"),
        P("col"),
        P("col"),
        P(None, "clus", "col"),
    )
    out_specs = (
        P(None, "clus", "col"),
        P(None, "clus", "col"),
        P("clus", "col"),
        P("clus", "col"),
        P("clus", "col"),
        P("col"),
        P("col"),
        P("col"),
    )
    return jax.shard_map(shards, mesh=mesh, in_specs=in_specs, out_specs=out_specs, check_vma=False)
```

```python
import functools

import jax
import jax.numpy as jnp
from jax import lax
from jax.experimental import pallas as pl
from jax.experimental.pallas import tpu as pltpu
from jax.sharding import PartitionSpec as P

D = 2048
MB = 3
STEP = 10

BETA_ONE = 0.9
BETA_TWO = 0.95
EPSILON = 1e-08
DECAY = 0.1
RATE_WEIGHT = 0.06
RATE_BIAS = 0.6

LANES = 128
DIGIT_BITS = 5
DIGITS = 6
STRIP = 32
SUBLANES = 8
TILE = 256
VMEM_BYTES = 48 * 1024 * 1024

GROUP, COLUMN, LIMITS = 0, 1, 2
STARTS = LIMITS + MB

F32, BF16 = jnp.float32, jnp.bfloat16


def launch(name, body, table, ins, outs, grid=(1,), after=(), alias=None, scratch=()):
    arrays = [array for array, _, _ in ins]
    in_specs = [
        pl.BlockSpec(memory_space=pl.ANY) if block is None else pl.BlockSpec(block, lambda *a, f=index: f(*a[:-1]))
        for _, block, index in ins
    ]
    unread = ([alias[0]] if alias else []) + list(after)
    out_specs = [pl.BlockSpec(block, lambda *a, f=index: f(*a[:-1])) for _, _, block, index in outs]

    def kernel(table_ref, *refs):
        kept = refs[: len(ins)] + refs[len(ins) + len(unread) :]
        body(table_ref, *kept)

    return pl.pallas_call(
        kernel,
        grid_spec=pltpu.PrefetchScalarGridSpec(
            num_scalar_prefetch=1,
            grid=grid,
            in_specs=in_specs + [pl.BlockSpec(memory_space=pl.ANY)] * len(unread),
            out_specs=out_specs,
            scratch_shapes=list(scratch),
        ),
        out_shape=[jax.ShapeDtypeStruct(shape, kind) for shape, kind, _, _ in outs],
        input_output_aliases={1 + len(ins): alias[1]} if alias else {},
        compiler_params=pltpu.CompilerParams(vmem_limit_bytes=VMEM_BYTES),
        cost_estimate=pl.CostEstimate(flops=1, bytes_accessed=1, transcendentals=0),
        name=name,
    )(table, *arrays, *unread)


def flip(values, axis, bit):
    size = lax.axis_size(axis)
    return lax.ppermute(values, axis, [(i, i ^ bit) for i in range(size)])


def product(left, right):
    return jnp.dot(left, right, preferred_element_type=F32)


def product_back(left, right):
    return lax.dot_general(left, right, (((1,), (1,)), ((), ())), preferred_element_type=F32)


def product_rows(left, right):
    return lax.dot_general(left, right, (((0,), (0,)), ((), ())), preferred_element_type=F32)


def put_rows(ref, first, rows):
    base = pl.multiple_of((first // SUBLANES) * SUBLANES, SUBLANES)
    offset = first - base
    spare = jnp.zeros((SUBLANES, rows.shape[1]), rows.dtype)
    moved = pltpu.roll(jnp.concatenate([rows, spare], axis=0), offset, 0)
    head = ref[pl.ds(base, SUBLANES), :]
    row_ids = lax.broadcasted_iota(jnp.int32, head.shape, 0)
    ref[pl.ds(base, SUBLANES), :] = jnp.where(row_ids < offset, head, moved[:SUBLANES])
    ref[pl.ds(pl.multiple_of(base + SUBLANES, SUBLANES), rows.shape[0]), :] = moved[SUBLANES:]


def take_rows(ref, first, count):
    base = pl.multiple_of((first // SUBLANES) * SUBLANES, SUBLANES)
    length = count + SUBLANES
    moved = pltpu.roll(ref[pl.ds(base, length), :], lax.rem(length - (first - base), length), 0)
    return moved[:count]


def pick_kernel(table_ref, source_ref, out_ref):
    out_ref[...] = source_ref[0]


def pick(table, stacked, m, after=()):
    _, rows, width = stacked.shape
    return launch(
        f"pick{m}", pick_kernel, table,
        [(stacked, (1, rows // 4, width), lambda i: (m, i, 0))],
        [((rows, width), stacked.dtype, (rows // 4, width), lambda i: (i, 0))],
        grid=(4,), after=after,
    )[0]


def gather_kernel(m, table_ref, neighbour_ref, feature_ref, matrix_ref, scale_ref, mixed_ref):
    limit = table_ref[LIMITS + m]
    tile, nodes = matrix_ref.shape
    words = -(-(nodes // LANES) // DIGITS)
    lane = lax.broadcasted_iota(jnp.int32, (STRIP, LANES), 1)
    for strip in range(tile // STRIP):
        rows = pl.ds(strip * STRIP, STRIP)
        first_row = pl.program_id(0) * tile + strip * STRIP
        entries = neighbour_ref[0, rows, :]
        row_ids = first_row + lax.broadcasted_iota(jnp.int32, entries.shape, 0)
        valid = (entries < limit) & (row_ids < limit)
        low = entries & (LANES - 1)
        high = entries >> 7
        digits = []
        for word in range(words):
            inside = valid & (high >= word * DIGITS) & (high < (word + 1) * DIGITS)
            shift = jnp.where(inside, (high - word * DIGITS) * DIGIT_BITS, 0)
            digits.append(jnp.where(inside, jnp.left_shift(1, shift), 0))
        sums = [jnp.zeros((STRIP, LANES), jnp.int32) for _ in range(words)]
        for entry in range(entries.shape[1]):
            hit = lane == low[:, entry : entry + 1]
            for word in range(words):
                sums[word] = sums[word] + jnp.where(hit, digits[word][:, entry : entry + 1], 0)
        own_row = first_row + lax.broadcasted_iota(jnp.int32, (STRIP, LANES), 0)
        for block in range(nodes // LANES):
            word, digit = block // DIGITS, block % DIGITS
            count = jnp.right_shift(sums[word], digit * DIGIT_BITS) & ((1 << DIGIT_BITS) - 1)
            count = jnp.where(lane + block * LANES == own_row, 2 * count + 2, count)
            matrix_ref[rows, block * LANES : (block + 1) * LANES] = count.astype(F32).astype(BF16)
        degree = 1.0 + jnp.sum(valid.astype(F32), axis=1, keepdims=True)
        scale_ref[rows, :] = (row_ids[:, :1] < limit).astype(F32) / degree
    mixed_ref[...] = (product(matrix_ref[...], feature_ref[0]) * scale_ref[...]).astype(BF16)


def gather(table, m, neighbours, features, after=()):
    _, nodes, entries = neighbours.shape
    width = features.shape[2]
    return launch(
        f"gather{m}", functools.partial(gather_kernel, m), table,
        [
            (neighbours, (1, TILE, entries), lambda i: (m, i, 0)),
            (features, (1, nodes, width), lambda i: (m, 0, 0)),
        ],
        [
            ((nodes, nodes), BF16, (TILE, nodes), lambda i: (i, 0)),
            ((nodes, 1), F32, (TILE, 1), lambda i: (i, 0)),
            ((nodes, width), BF16, (TILE, width), lambda i: (i, 0)),
        ],
        grid=(nodes // TILE,), after=after,
    )


def mix_kernel(table_ref, matrix_ref, scale_ref, feature_ref, mixed_ref):
    mixed_ref[...] = (product(matrix_ref[...], feature_ref[...]) * scale_ref[...]).astype(BF16)


def mix(table, m, matrix, scale, far, after=()):
    nodes, width = far.shape
    return launch(
        f"mix{m}", mix_kernel, table,
        [
            (matrix, (TILE, nodes), lambda i: (i, 0)),
            (scale, (TILE, 1), lambda i: (i, 0)),
            (far, (nodes, width), lambda i: (0, 0)),
        ],
        [((nodes, width), BF16, (TILE, width), lambda i: (i, 0))],
        grid=(nodes // TILE,), after=after,
    )[0]


def place_kernel(groups, table_ref, slots_ref, weight_ref, mate_ref, rows_ref):
    owner = pl.program_id(0)

    @pl.when(owner == 0)
    def _():
        rows_ref[...] = jnp.zeros_like(rows_ref)

    put_rows(rows_ref, table_ref[STARTS + owner], slots_ref[...].astype(F32))

    @pl.when(owner == groups - 1)
    def _():
        width = weight_ref.shape[2]
        for block in range(weight_ref.shape[0]):
            source = pl.multiple_of((table_ref[COLUMN] ^ block) * width, width)
            rows = rows_ref[pl.ds(source, width), :].astype(BF16)
            weight_ref[block] = rows
            if block % 2:
                mate_ref[block // 2] = rows


def place(table, slots, groups, after=()):
    capacity, width = slots.shape[0] // groups, slots.shape[1]
    blocks = D // width
    return launch(
        "place", functools.partial(place_kernel, groups), table,
        [(slots, (capacity, width), lambda i: (i, 0))],
        [
            ((blocks, width, width), BF16, (blocks, width, width), lambda i: (0, 0, 0)),
            ((blocks // 2, width, width), BF16, (blocks // 2, width, width), lambda i: (0, 0, 0)),
        ],
        grid=(groups,), after=after, scratch=[pltpu.VMEM((D + capacity + SUBLANES, width), F32)],
    )


def layer_kernel(m, table_ref, *refs):
    mixed_refs, (weight_ref, bias_ref, grad_ref, out_ref, pre_ref, sum_ref) = refs[:4], refs[4:]
    tile = out_ref.shape[1]
    preact = bias_ref[...]
    for block in range(4):
        preact = preact + product(mixed_refs[block][...], weight_ref[block])
    first_row = pl.program_id(0) * tile
    row_ids = first_row + lax.broadcasted_iota(jnp.int32, preact.shape, 0)
    live = row_ids < table_ref[LIMITS + m]
    gate = jax.nn.sigmoid(preact)
    out_ref[0] = jnp.where(live, preact * gate, 0.0).astype(BF16)
    slope = gate * (1.0 + preact * (1.0 - gate))
    grad_pre = jnp.where(live, grad_ref[0].astype(F32) * slope, 0.0).astype(BF16)
    pre_ref[...] = grad_pre

    @pl.when(pl.program_id(0) == 0)
    def _():
        sum_ref[...] = jnp.zeros_like(sum_ref)

    sum_ref[...] += jnp.sum(grad_pre.astype(F32), axis=0, keepdims=True)


def layer(table, m, mixed, weight, bias, out_grad, outputs, after=()):
    nodes, width = mixed[0].shape
    return launch(
        f"layer{m}", functools.partial(layer_kernel, m), table,
        [(part, (TILE, width), lambda i: (i, 0)) for part in mixed]
        + [
            (weight, weight.shape, lambda i: (0, 0, 0)),
            (bias, (1, width), lambda i: (0, 0)),
            (out_grad, (1, TILE, width), lambda i: (m, i, 0)),
        ],
        [
            ((MB, nodes, width), BF16, (1, TILE, width), lambda i: (m, i, 0)),
            ((nodes, width), BF16, (TILE, width), lambda i: (i, 0)),
            ((1, width), F32, (1, width), lambda i: (0, 0)),
        ],
        grid=(nodes // TILE,), after=after, alias=None if outputs is None else (outputs, 0),
    )


def back_kernel(chunks, table_ref, here_ref, mate_ref, weight_ref, weight_mate_ref, *out_refs):
    own_ref, away_refs = out_refs[0], out_refs[1:]
    here, mate = here_ref[...], mate_ref[...]
    away = (product_back(here, weight_ref[2]) + product_back(mate, weight_mate_ref[1])).astype(BF16)
    step = away.shape[1] // chunks
    for chunk in range(chunks):
        away_refs[chunk][...] = away[:, chunk * step : (chunk + 1) * step]
    own_ref[...] = product_back(here, weight_ref[0]) + product_back(mate, weight_mate_ref[0])


def back(table, m, here, mate, weight, weight_mate, chunks, after=()):
    nodes, width = here.shape
    step = width // chunks
    return launch(
        f"back{m}", functools.partial(back_kernel, chunks), table,
        [
            (here, (TILE, width), lambda i: (i, 0)),
            (mate, (TILE, width), lambda i: (i, 0)),
            (weight, weight.shape, lambda i: (0, 0, 0)),
            (weight_mate, weight_mate.shape, lambda i: (0, 0, 0)),
        ],
        [((nodes, width), F32, (TILE, width), lambda i: (i, 0))]
        + [((nodes, step), BF16, (TILE, step), lambda i: (i, 0)) for _ in range(chunks)],
        grid=(nodes // TILE,), after=after,
    )


def scatter_kernel(table_ref, own_ref, got_ref, scale_ref, matrix_ref, out_ref, sum_ref):
    @pl.when(pl.program_id(0) == 0)
    def _():
        grad_mixed = (own_ref[...] + got_ref[...].astype(F32)).astype(BF16)
        sum_ref[...] = (grad_mixed.astype(F32) * scale_ref[...]).astype(BF16)

    out_ref[0] = product_rows(matrix_ref[...], sum_ref[...]).astype(BF16)


def scatter(table, m, chunk, own, got, scale, matrix, grads, after=()):
    nodes, width = own.shape
    step = got.shape[1]
    return launch(
        f"scatter{m}_{chunk}", scatter_kernel, table,
        [
            (own, (nodes, step), lambda i: (0, chunk)),
            (got, (nodes, step), lambda i: (0, 0)),
            (scale, (nodes, 1), lambda i: (0, 0)),
            (matrix, (nodes, TILE), lambda i: (0, i)),
        ],
        [((MB, nodes, width), BF16, (1, TILE, step), lambda i: (m, i, chunk))],
        grid=(nodes // TILE,), after=after, alias=None if grads is None else (grads, 0),
        scratch=[pltpu.VMEM((nodes, step), BF16)],
    )[0]


def weight_kernel(parts, table_ref, *refs):
    blocks = len(refs[: MB * 4]) // MB
    mixed_refs, pre_refs = refs[: MB * blocks], refs[MB * blocks : MB * blocks + MB]
    bias_refs = refs[MB * blocks + MB : MB * blocks + 2 * MB]
    keep_refs, sent_refs = refs[MB * blocks + 2 * MB :][:2], refs[MB * blocks + 2 * MB + 2 : -2]
    bias_out_ref, total_ref = refs[-2:]
    step = pl.program_id(0)

    for m in range(MB):

        @pl.when(step // parts == m)
        def _(m=m):
            for block in range(blocks):
                term = product_rows(mixed_refs[m * blocks + block][...], pre_refs[m][...])
                if m == 0:
                    term = jnp.where(step == 0, term, total_ref[block] + term)
                else:
                    term = total_ref[block] + term
                total_ref[block] = term

    @pl.when(step == parts * MB - 1)
    def _():
        bias_out_ref[...] = sum(ref[...] for ref in bias_refs)
        width = total_ref.shape[1]
        quarter = width // 4
        upper = (table_ref[GROUP] & 1) == 1
        for block in range(blocks):
            rows = pl.ds(pl.multiple_of((table_ref[COLUMN] ^ block) * width, width), width)
            for chunk in range(2):
                low = total_ref[block, :, chunk * quarter : (chunk + 1) * quarter]
                high = total_ref[block, :, (2 + chunk) * quarter : (3 + chunk) * quarter]
                keep_refs[chunk][rows, :] = jnp.where(upper, high, low)
                sent_refs[chunk][rows, :] = jnp.where(upper, low, high).astype(BF16)


def weight_gradient(table, mixed, pres, biases, after=()):
    nodes, width = pres[0].shape
    parts = 2
    rows, quarter = nodes // parts, width // 4
    blocks = len(mixed[0])

    def turn(m):
        return lambda i: (jnp.clip(i - m * parts, 0, parts - 1), 0)

    whole = lambda i: (0, 0)
    return launch(
        "weight", functools.partial(weight_kernel, parts), table,
        [(mixed[m][b], (rows, width), turn(m)) for m in range(MB) for b in range(blocks)]
        + [(pres[m], (rows, width), turn(m)) for m in range(MB)]
        + [(bias, (1, width), whole) for bias in biases],
        [((D, quarter), F32, (D, quarter), whole)] * 2
        + [((D, quarter), BF16, (D, quarter), whole)] * 2
        + [((1, width), F32, (1, width), whole)],
        grid=(parts * MB,), after=after, scratch=[pltpu.VMEM((blocks, width, width), F32)],
    )


def pairs_kernel(capacity, table_ref, keep_ref, got_ref, bias_ref, bias_got_ref, held_ref, sent_ref, bias_out_ref, total_ref):
    rows = keep_ref.shape[0]
    total_ref[:rows, :] = keep_ref[...] + got_ref[...].astype(F32)
    total_ref[rows:, :] = jnp.zeros((2 * capacity + SUBLANES, keep_ref.shape[1]), F32)
    bit = (table_ref[GROUP] >> 1) & 1
    for j in range(held_ref.shape[0]):
        kept, gone = 2 * j + bit, 2 * j + 1 - bit
        held_ref[j] = take_rows(total_ref, table_ref[STARTS + 2 * kept], 2 * capacity)
        sent_ref[j] = take_rows(total_ref, table_ref[STARTS + 2 * gone], 2 * capacity).astype(BF16)
    bias_out_ref[...] = bias_ref[...] + bias_got_ref[...]


def pairs(table, name, keep, got, bias, bias_got, groups, capacity, after=()):
    rows, width = keep.shape
    count = groups // 4
    shape = (count, 2 * capacity, width)
    flat, deep = (lambda i: (0, 0)), (lambda i: (0, 0, 0))
    return launch(
        name, functools.partial(pairs_kernel, capacity), table,
        [(array, array.shape, flat) for array in (keep, got, bias, bias_got)],
        [(shape, F32, shape, deep), (shape, BF16, shape, deep), (bias.shape, F32, bias.shape, flat)],
        after=after, scratch=[pltpu.VMEM((rows + 2 * capacity + SUBLANES, width), F32)],
    )


def halve_kernel(level, table_ref, held_ref, got_ref, bias_ref, bias_got_ref, out_ref, sent_ref, bias_out_ref):
    bit = (table_ref[GROUP] >> level) & 1
    for j in range(out_ref.shape[0]):
        kept, gone = 2 * j + bit, 2 * j + 1 - bit
        out_ref[j] = held_ref[kept] + got_ref[kept].astype(F32)
        sent_ref[j] = (held_ref[gone] + got_ref[gone].astype(F32)).astype(BF16)
    bias_out_ref[...] = bias_ref[...] + bias_got_ref[...]


def halve(table, name, level, held, got, bias, bias_got, after=()):
    shape = (held.shape[0] // 2,) + held.shape[1:]
    flat, deep = (lambda i: (0, 0)), (lambda i: (0, 0, 0))
    return launch(
        name, functools.partial(halve_kernel, level), table,
        [(held, held.shape, deep), (got, got.shape, deep), (bias, bias.shape, flat), (bias_got, bias.shape, flat)],
        [(shape, F32, shape, deep), (shape, BF16, shape, deep), (bias.shape, F32, bias.shape, flat)],
        after=after,
    )


def part_kernel(capacity, table_ref, held_ref, got_ref, bias_ref, bias_got_ref, own_ref, sent_ref, bias_out_ref, total_ref):
    rows = held_ref.shape[1]
    total_ref[:rows, :] = held_ref[0] + got_ref[0].astype(F32)
    total_ref[rows:, :] = jnp.zeros((SUBLANES, held_ref.shape[2]), F32)
    own = table_ref[GROUP]
    first = table_ref[STARTS + (own & ~1)]
    own_ref[...] = take_rows(total_ref, table_ref[STARTS + own] - first, capacity)
    sent_ref[...] = take_rows(total_ref, table_ref[STARTS + (own ^ 1)] - first, capacity).astype(BF16)
    bias_out_ref[...] = bias_ref[...] + bias_got_ref[...]


def part(table, name, held, got, bias, bias_got, capacity, after=()):
    shape = (capacity, held.shape[2])
    flat, deep = (lambda i: (0, 0)), (lambda i: (0, 0, 0))
    return launch(
        name, functools.partial(part_kernel, capacity), table,
        [(held, held.shape, deep), (got, got.shape, deep), (bias, bias.shape, flat), (bias_got, bias.shape, flat)],
        [(shape, F32, shape, flat), (shape, BF16, shape, flat), (bias.shape, F32, bias.shape, flat)],
        after=after, scratch=[pltpu.VMEM((held.shape[1] + SUBLANES, held.shape[2]), F32)],
    )


def adamw_update(current, first_moment, second_moment, gradient, step_rate):
    first_new = BETA_ONE * first_moment + (1.0 - BETA_ONE) * gradient
    second_new = BETA_TWO * second_moment + (1.0 - BETA_TWO) * gradient * gradient
    fixed_first = first_new / (1.0 - BETA_ONE**STEP)
    fixed_second = second_new / (1.0 - BETA_TWO**STEP)
    updated = current - step_rate * (
        fixed_first / (jnp.sqrt(fixed_second) + EPSILON) + DECAY * current
    )
    return (updated, first_new, second_new)


def adamw_kernel(groups, table_ref, *refs):
    own_refs, got_refs, (bias_grad_ref, *states), outs = refs[:2], refs[2:4], refs[4:11], refs[11:]
    weights, biases = states[:3], states[3:]
    rows, width = weights[0].shape
    quarter = width // 4
    own = table_ref[GROUP]
    row_ids = pl.program_id(0) * rows + lax.broadcasted_iota(jnp.int32, (rows, quarter), 0)
    used = row_ids < table_ref[STARTS + groups + own]
    for block in range(4):
        mine = (own & 1) == block // 2
        gradient = jnp.where(mine, own_refs[block % 2][...], got_refs[block % 2][...].astype(F32))
        columns = slice(block * quarter, (block + 1) * quarter)
        results = adamw_update(*(ref[:, columns] for ref in weights), gradient, RATE_WEIGHT)
        for out_ref, result in zip(outs[:3], results):
            out_ref[:, columns] = jnp.where(used, result, 0.0)
    results = adamw_update(*(ref[...] for ref in biases), bias_grad_ref[...], RATE_BIAS)
    for out_ref, result in zip(outs[3:], results):
        out_ref[...] = result


def adamw(table, groups, own, got, bias_grad, weights, biases, after=()):
    capacity, width = weights[0].shape
    steps = 4 if capacity % 64 == 0 and capacity >= 256 else 1
    rows, quarter = capacity // steps, width // 4
    down, fixed = (lambda i: (i, 0)), (lambda i: (0, 0))
    return launch(
        "adamw", functools.partial(adamw_kernel, groups), table,
        [(array, (rows, quarter), down) for array in (*own, *got)]
        + [(bias_grad, (1, width), fixed)]
        + [(array, (rows, width), down) for array in weights]
        + [(array, (1, width), fixed) for array in biases],
        [((capacity, width), F32, (rows, width), down)] * 3 + [((1, width), F32, (1, width), fixed)] * 3,
        grid=(steps,), after=after,
    )


def shards(
    features,
    neighbours,
    node_counts,
    row_counts,
    master_weight,
    weight_first,
    weight_second,
    master_bias,
    bias_first,
    bias_second,
    out_grad,
):
    groups = lax.axis_size("clus")
    capacity, width = master_weight.shape
    owner_ids = jnp.arange(groups, dtype=jnp.int32)
    starts = jnp.sum(jnp.where(owner_ids[None, :] < owner_ids[:, None], row_counts[None, :], 0), axis=1)
    table = jnp.concatenate(
        [
            jnp.stack([lax.axis_index("clus"), lax.axis_index("col")]).astype(jnp.int32),
            node_counts[:, 0],
            starts.astype(jnp.int32),
            row_counts,
        ]
    )
    bias_row, bias_first_row, bias_second_row = (
        array.reshape(1, width) for array in (master_bias, bias_first, bias_second)
    )

    picked = []
    for m in range(MB):
        picked.append(pick(table, features, m, picked[-1:]))
    far = [flip(part_, "col", 2) for part_ in picked]
    slots = lax.all_gather(master_weight.astype(BF16), "clus", axis=0, tiled=True)

    matrix, scale, mixed = [], [], []
    last = picked[-1]
    for m in range(MB):
        matrix_m, scale_m, here = gather(table, m, neighbours, features, [last])
        matrix.append(matrix_m)
        scale.append(scale_m)
        mixed.append([here, flip(here, "col", 1)])
        last = here

    def aggregate(m):
        nonlocal last
        last = there = mix(table, m, matrix[m], scale[m], far[m], [last])
        mixed[m] += [there, flip(there, "col", 1)]

    outputs, input_grads = None, None
    pres, mates, biases, own, away = [], [], [], [], []

    def forward(m):
        nonlocal last, outputs
        outputs, grad_pre, bias_sum = layer(table, m, mixed[m], weight, bias_row, out_grad, outputs, [last])
        pres.append(grad_pre)
        mates.append(flip(grad_pre, "col", 1))
        biases.append(bias_sum)
        last = grad_pre

    def backward(m, chunks):
        nonlocal last
        own_m, *away_m = back(table, m, pres[m], mates[m], weight, weight_mate, chunks, [last])
        own.append(own_m)
        away.append([flip(chunk, "col", 2) for chunk in away_m])
        last = own_m

    def finish(m):
        nonlocal last, input_grads
        for chunk, got in enumerate(away[m]):
            last = input_grads = scatter(table, m, chunk, own[m], got, scale[m], matrix[m], input_grads, [last])

    aggregate(0)
    aggregate(1)
    weight, for_mate = place(table, slots, groups, [last])
    weight_mate = flip(for_mate, "col", 1)
    last = for_mate
    forward(0)
    forward(1)
    backward(0, 1)
    backward(1, 1)
    aggregate(2)
    forward(2)
    backward(2, 2)
    *held, bias_sum = weight_gradient(table, mixed, pres, biases, [last])
    keep, sent = held[:2], held[2:]
    last = bias_sum
    got = [flip(chunk, "clus", 1) for chunk in sent]
    bias_got = flip(bias_sum, "clus", 1)
    finish(0)

    held = [None, None]
    zero = jnp.zeros_like(bias_sum)
    level, bit = 1, 2
    while bit < groups:
        for chunk in range(2):
            here, there = (bias_sum, bias_got) if chunk == 0 else (zero, zero)
            if level == 1:
                held[chunk], out, total = pairs(
                    table, f"pairs{chunk}", keep[chunk], got[chunk], here, there, groups, capacity, [last]
                )
            else:
                held[chunk], out, total = halve(
                    table, f"halve{level}_{chunk}", level, held[chunk], got[chunk], here, there, [last]
                )
            last = out
            got[chunk] = flip(out, "clus", bit)
            if chunk == 0:
                new_sum, new_got = total, flip(total, "clus", bit)
        bias_sum, bias_got = new_sum, new_got
        level, bit = level + 1, 2 * bit
    finish(1)
    mine, other = [], []
    for chunk in range(2):
        here, there = (bias_sum, bias_got) if chunk == 0 else (zero, zero)
        own_rows, out, total = part(
            table, f"part{chunk}", held[chunk], got[chunk], here, there, capacity, [last]
        )
        last = out
        mine.append(own_rows)
        other.append(flip(out, "clus", 1))
        if chunk == 0:
            bias_total = total
    updated = adamw(
        table, groups, mine, other, bias_total,
        (master_weight, weight_first, weight_second), (bias_row, bias_first_row, bias_second_row), [last],
    )
    last = updated[0]
    finish(2)
    return (outputs, input_grads, *updated[:3], *(row.reshape(width) for row in updated[3:]))


def solution(mesh):
    in_specs = (
        P(None, "clus", "col"),
        P(None, "clus", None),
        P(None, "clus"),
        P(),
        P("clus", "col"),
        P("clus", "col"),
        P("clus", "col"),
        P("col"),
        P("col"),
        P("col"),
        P(None, "clus", "col"),
    )
    out_specs = (
        P(None, "clus", "col"),
        P(None, "clus", "col"),
        P("clus", "col"),
        P("clus", "col"),
        P("clus", "col"),
        P("col"),
        P("col"),
        P("col"),
    )
    return jax.shard_map(shards, mesh=mesh, in_specs=in_specs, out_specs=out_specs, check_vma=False)
```

```python
import functools

import jax
import jax.numpy as jnp
from jax import lax
from jax.experimental import pallas as pl
from jax.experimental.pallas import tpu as pltpu
from jax.sharding import PartitionSpec as P

D = 2048
MB = 3
STEP = 10

BETA_ONE = 0.9
BETA_TWO = 0.95
EPSILON = 1e-08
DECAY = 0.1
RATE_WEIGHT = 0.06
RATE_BIAS = 0.6

LANES = 128
DIGIT_BITS = 5
DIGITS = 6
STRIP = 32
SUBLANES = 8
TILE = 256
WIDE = 512
VMEM_BYTES = 48 * 1024 * 1024

GROUP, COLUMN, LIMITS = 0, 1, 2
STARTS = LIMITS + MB

FRONT_ID, MIX_ID, BACK_ID, SUM_ID = 1, 2, 2 + MB, 2 + 2 * MB

F32, BF16 = jnp.float32, jnp.bfloat16


def launch(name, body, table, ins, outs, grid=(1,), after=(), alias=None, scratch=(), barrier=None):
    def spec(block, index):
        if block is None:
            return pl.BlockSpec(memory_space=pl.ANY)
        return pl.BlockSpec(block, lambda *a: index(*a[:-1]))

    unread = ([alias[0]] if alias else []) + [array for array in after if alias is None or array is not alias[0]]

    def kernel(table_ref, *refs):
        body(table_ref, *refs[: len(ins)], *refs[len(ins) + len(unread) :])

    call = functools.partial(
        pl.pallas_call,
        kernel,
        grid_spec=pltpu.PrefetchScalarGridSpec(
            num_scalar_prefetch=1,
            grid=grid,
            in_specs=[spec(block, index) for _, block, index in ins]
            + [pl.BlockSpec(memory_space=pl.ANY)] * len(unread),
            out_specs=[spec(block, index) for _, _, block, index in outs],
            scratch_shapes=list(scratch),
        ),
        out_shape=[jax.ShapeDtypeStruct(shape, kind) for shape, kind, _, _ in outs],
        input_output_aliases={1 + len(ins): alias[1]} if alias else {},
        compiler_params=pltpu.CompilerParams(
            vmem_limit_bytes=VMEM_BYTES, collective_id=barrier, has_side_effects=barrier is not None
        ),
        cost_estimate=pl.CostEstimate(flops=1, bytes_accessed=1, transcendentals=0),
        name=name,
    )
    operands = (table, *(array for array, _, _ in ins), *unread)
    if barrier == FRONT_ID:
        return call()(*operands)
    if barrier == SUM_ID:
        return call()(*operands)
    if barrier is not None and barrier >= BACK_ID:
        return call()(*operands)
    if barrier is not None:
        return call()(*operands)
    return call()(*operands)


def flip(values, axis, bit):
    size = lax.axis_size(axis)
    return lax.ppermute(values, axis, [(i, i ^ bit) for i in range(size)])


def partner(index, bit):
    return index + bit * (1 - 2 * ((index // bit) % 2))


def product(left, right):
    return jnp.dot(left, right, preferred_element_type=F32)


def product_back(left, right):
    return lax.dot_general(left, right, (((1,), (1,)), ((), ())), preferred_element_type=F32)


def product_rows(left, right):
    return lax.dot_general(left, right, (((0,), (0,)), ((), ())), preferred_element_type=F32)


def scaled(values, scale):
    return values * jnp.concatenate([scale] * (values.shape[1] // LANES), axis=1)


def put_rows(ref, first, rows):
    base = pl.multiple_of((first // SUBLANES) * SUBLANES, SUBLANES)
    offset = first - base
    spare = jnp.zeros((SUBLANES, rows.shape[1]), rows.dtype)
    moved = pltpu.roll(jnp.concatenate([rows, spare], axis=0), offset, 0)
    head = ref[pl.ds(base, SUBLANES), :]
    row_ids = lax.broadcasted_iota(jnp.int32, head.shape, 0)
    ref[pl.ds(base, SUBLANES), :] = jnp.where(row_ids < offset, head, moved[:SUBLANES])
    ref[pl.ds(pl.multiple_of(base + SUBLANES, SUBLANES), rows.shape[0]), :] = moved[SUBLANES:]


def take_rows(ref, first, count, largest):
    bit = 1 << (largest.bit_length() - 1)
    rows = ref[: count + 2 * bit, :]
    while bit:
        length = count + max(bit, SUBLANES)
        moved = rows[bit : bit + length] if bit >= SUBLANES else pltpu.roll(rows, length - bit, 0)
        chosen = (jnp.broadcast_to(first, (length, rows.shape[1])) & bit) != 0
        rows = jnp.where(chosen, moved, rows[:length])
        bit //= 2
    return rows[:count]


def pick_kernel(m, table_ref, source_ref, out_ref, semaphore):
    copy = pltpu.make_async_copy(source_ref.at[m], out_ref, semaphore)
    copy.start()
    copy.wait()


def pick(table, stacked, m, after=()):
    return launch(
        f"pick{m}", functools.partial(pick_kernel, m), table,
        [(stacked, None, None)], [(stacked.shape[1:], stacked.dtype, None, None)],
        after=after, scratch=[pltpu.SemaphoreType.DMA],
    )[0]


def count_tile(limit, first, neighbour_ref, matrix_ref, scale_ref, lanes):
    nodes = matrix_ref.shape[1]
    words = -(-(nodes // LANES) // DIGITS)
    entries = neighbour_ref[0, :, lanes]
    node_ids = first + lax.broadcasted_iota(jnp.int32, entries.shape, 1)
    valid = (entries < limit) & (node_ids < limit)
    low = entries & (LANES - 1)
    high = entries >> 7
    digits = []
    for word in range(words):
        inside = valid & (high >= word * DIGITS) & (high < (word + 1) * DIGITS)
        shift = jnp.where(inside, (high - word * DIGITS) * DIGIT_BITS, 0)
        digits.append(jnp.where(inside, jnp.left_shift(1, shift), 0))
    for strip in range(LANES // STRIP):
        row_ids = strip * STRIP + lax.broadcasted_iota(jnp.int32, (STRIP, LANES), 0)
        sums = [jnp.zeros((STRIP, LANES), jnp.int32) for _ in range(words)]
        for entry in range(entries.shape[0]):
            hit = row_ids == low[entry : entry + 1, :]
            for word in range(words):
                sums[word] = sums[word] + jnp.where(hit, digits[word][entry : entry + 1, :], 0)
        for block in range(nodes // LANES):
            word, digit = block // DIGITS, block % DIGITS
            count = jnp.right_shift(sums[word], digit * DIGIT_BITS) & ((1 << DIGIT_BITS) - 1)
            rows = slice(block * LANES + strip * STRIP, block * LANES + (strip + 1) * STRIP)
            matrix_ref[0, rows, lanes] = count.astype(F32).astype(BF16)
    rows = pl.ds(pl.multiple_of(first, LANES), LANES)
    square = matrix_ref[0, rows, lanes].astype(F32)
    on_diagonal = lax.broadcasted_iota(jnp.int32, square.shape, 0) == lax.broadcasted_iota(jnp.int32, square.shape, 1)
    matrix_ref[0, rows, lanes] = jnp.where(on_diagonal, 2.0 * square + 2.0, square).astype(BF16)
    degree = 1.0 + jnp.sum(valid.astype(F32), axis=0, keepdims=True)
    factor = (node_ids[:1] < limit).astype(F32) / degree
    scale_ref[0, lanes, :] = jnp.transpose(jnp.broadcast_to(factor, (LANES, LANES)))


def front_kernel(
    groups, total, table_ref, master_ref, neighbour_ref, feature_ref, matrix_ref, scale_ref, mixed_ref, slots_ref,
    block_ref, local_semaphore, line_send, line_receive, pair_send, pair_receive,
):
    batch, tile_id = pl.program_id(0), pl.program_id(1)
    tiles = pl.num_programs(1)
    step = batch * tiles + tile_id
    own = lax.axis_index("clus")
    place, side = own // 2, own % 2
    pairs = groups // 2
    other = partner(own, 1)

    def line_copy(direction, hop):
        origin = place - hop if direction == 0 else place + hop
        target = place + 1 if direction == 0 else place - 1
        slot = origin * 2 + side
        return pltpu.make_async_remote_copy(
            src_ref=block_ref if hop == 0 else slots_ref.at[slot],
            dst_ref=slots_ref.at[slot],
            send_sem=line_send.at[direction, hop],
            recv_sem=line_receive.at[direction, hop],
            device_id={"clus": target * 2 + side},
            device_id_type=pl.DeviceIdType.MESH,
        )

    def sends(direction, hop):
        if direction == 0:
            return (place - hop >= 0) & (place + 1 < pairs)
        return (place + hop < pairs) & (place - 1 >= 0)

    def arrives(direction, hop):
        return place - 1 - hop >= 0 if direction == 0 else place + 1 + hop < pairs

    def arrival(direction, hop):
        origin = place - 1 - hop if direction == 0 else place + 1 + hop
        slot = slots_ref.at[origin * 2 + side]
        return pltpu.make_async_remote_copy(
            src_ref=slot,
            dst_ref=slot,
            send_sem=line_send.at[direction, hop],
            recv_sem=line_receive.at[direction, hop],
            device_id={"clus": other},
            device_id_type=pl.DeviceIdType.MESH,
        )

    def pair_copy(direction, hop):
        origin = place - 1 - hop if direction == 0 else place + 1 + hop
        number = 0 if hop < 0 else 1 + 2 * hop + direction
        slot = own if hop < 0 else origin * 2 + side
        return pltpu.make_async_remote_copy(
            src_ref=block_ref if hop < 0 else slots_ref.at[slot],
            dst_ref=slots_ref.at[slot],
            send_sem=pair_send.at[number],
            recv_sem=pair_receive.at[number],
            device_id={"clus": other},
            device_id_type=pl.DeviceIdType.MESH,
        )

    def pair_arrival(direction, hop):
        origin = place - 1 - hop if direction == 0 else place + 1 + hop
        number = 0 if hop < 0 else 1 + 2 * hop + direction
        slot = slots_ref.at[other if hop < 0 else origin * 2 + 1 - side]
        return pltpu.make_async_remote_copy(
            src_ref=slot,
            dst_ref=slot,
            send_sem=pair_send.at[number],
            recv_sem=pair_receive.at[number],
            device_id={"clus": other},
            device_id_type=pl.DeviceIdType.MESH,
        )

    local_copy = pltpu.make_async_copy(block_ref, slots_ref.at[own], local_semaphore)
    hops = pairs - 1

    @pl.when(step == 0)
    def _():
        barrier = pltpu.get_barrier_semaphore()

        def greet(index):
            pl.semaphore_signal(barrier, inc=1, device_id={"clus": index}, device_id_type=pl.DeviceIdType.MESH)

        greet(other)

        @pl.when(place + 1 < pairs)
        def _():
            greet(own + 2)

        @pl.when(place - 1 >= 0)
        def _():
            greet(own - 2)

        pl.semaphore_wait(barrier, 1 + jnp.where(place + 1 < pairs, 1, 0) + jnp.where(place - 1 >= 0, 1, 0))
        block_ref[...] = master_ref[...].astype(BF16)
        local_copy.start()
        for direction in range(2):
            pl.when(sends(direction, 0))(line_copy(direction, 0).start)
        pair_copy(0, -1).start()

    limit = table_ref[LIMITS + batch]
    tile = mixed_ref.shape[1]
    for part in range(tile // LANES):
        first = tile_id * tile + part * LANES
        count_tile(limit, first, neighbour_ref, matrix_ref, scale_ref, slice(part * LANES, (part + 1) * LANES))
    mixed_ref[0] = scaled(product_rows(matrix_ref[0], feature_ref[0]), scale_ref[0]).astype(BF16)

    for hop in range(hops):
        when = min(total - 1, ((hop + 1) * total) // hops)

        @pl.when(step == when)
        def _(hop=hop):
            for direction in range(2):

                @pl.when(arrives(direction, hop))
                def _(direction=direction):
                    arrival(direction, hop).wait_recv()
                    pair_copy(direction, hop).start()

                if hop + 1 < hops:
                    pl.when(sends(direction, hop + 1))(line_copy(direction, hop + 1).start)

    @pl.when(step == total - 1)
    def _():
        local_copy.wait()
        pair_copy(0, -1).wait_send()
        pair_arrival(0, -1).wait_recv()
        for hop in range(hops):
            for direction in range(2):
                pl.when(sends(direction, hop))(line_copy(direction, hop).wait_send)

                @pl.when(arrives(direction, hop))
                def _(direction=direction, hop=hop):
                    pair_copy(direction, hop).wait_send()
                    pair_arrival(direction, hop).wait_recv()


def front(table, groups, master, neighbours, features, after=()):
    _, entries, nodes = neighbours.shape
    capacity, width = master.shape
    hops = groups // 2 - 1
    steps = MB * (nodes // TILE)
    return launch(
        "front", functools.partial(front_kernel, groups, steps), table,
        [
            (master, (capacity, width), lambda b, i: (0, 0)),
            (neighbours, (1, entries, TILE), lambda b, i: (b, 0, i)),
            (features, (1, nodes, width), lambda b, i: (b, 0, 0)),
        ],
        [
            ((MB, nodes, nodes), BF16, (1, nodes, TILE), lambda b, i: (b, 0, i)),
            ((MB, nodes, LANES), F32, (1, TILE, LANES), lambda b, i: (b, i, 0)),
            ((MB, nodes, width), BF16, (1, TILE, width), lambda b, i: (b, i, 0)),
            ((groups, capacity, width), BF16, None, None),
        ],
        grid=(MB, nodes // TILE), after=after, barrier=FRONT_ID,
        scratch=[
            pltpu.VMEM((capacity, width), BF16),
            pltpu.SemaphoreType.DMA,
            pltpu.SemaphoreType.DMA((2, hops)),
            pltpu.SemaphoreType.DMA((2, hops)),
            pltpu.SemaphoreType.DMA((1 + 2 * hops,)),
            pltpu.SemaphoreType.DMA((1 + 2 * hops,)),
        ],
    )


def greet_mate(mate):
    barrier = pltpu.get_barrier_semaphore()
    pl.semaphore_signal(barrier, inc=1, device_id={"col": mate}, device_id_type=pl.DeviceIdType.MESH)
    pl.semaphore_wait(barrier, 1)


def mix_kernel(
    m, steps, table_ref, matrix_ref, scale_ref, far_ref, here_ref, there_ref, here_mate_ref, there_mate_ref,
    buffer_ref, send, receive,
):
    step = pl.program_id(0)
    tile = there_ref.shape[0]
    mate = partner(lax.axis_index("col"), 1)

    def copy(number):
        rows = pl.ds((number - 1) * tile, tile)
        return pltpu.make_async_remote_copy(
            src_ref=here_ref.at[m] if number == 0 else buffer_ref.at[rows],
            dst_ref=here_mate_ref if number == 0 else there_mate_ref.at[rows],
            send_sem=send.at[number],
            recv_sem=receive.at[number],
            device_id={"col": mate},
            device_id_type=pl.DeviceIdType.MESH,
        )

    @pl.when(step == 0)
    def _():
        greet_mate(mate)
        copy(0).start()

    result = scaled(product_rows(matrix_ref[0], far_ref[...]), scale_ref[0]).astype(BF16)
    there_ref[...] = result
    for number in range(1, steps + 1):

        @pl.when(step == number - 1)
        def _(number=number):
            buffer_ref[(number - 1) * tile : number * tile, :] = result
            copy(number).start()

    @pl.when(step == steps - 1)
    def _():
        for number in range(steps + 1):
            copy(number).wait()


def mix(table, m, matrix, scale, far, here, after=()):
    nodes, width = far.shape
    steps = nodes // WIDE
    shape = (nodes, width)
    return launch(
        f"mix{m}", functools.partial(mix_kernel, m, steps), table,
        [
            (matrix, (1, nodes, WIDE), lambda i: (m, 0, i)),
            (scale, (1, WIDE, LANES), lambda i: (m, i, 0)),
            (far, shape, lambda i: (0, 0)),
            (here, None, None),
        ],
        [
            (shape, BF16, (WIDE, width), lambda i: (i, 0)),
            (shape, BF16, None, None),
            (shape, BF16, None, None),
        ],
        grid=(steps,), after=after, barrier=MIX_ID + m,
        scratch=[
            pltpu.VMEM(shape, BF16),
            pltpu.SemaphoreType.DMA((steps + 1,)),
            pltpu.SemaphoreType.DMA((steps + 1,)),
        ],
    )


def place_kernel(groups, table_ref, slots_ref, weight_ref, mate_ref, rows_ref):
    owner = pl.program_id(0)

    @pl.when(owner == 0)
    def _():
        rows_ref[...] = jnp.zeros_like(rows_ref)

    put_rows(rows_ref, table_ref[STARTS + owner], slots_ref[0].astype(F32))

    @pl.when(owner == groups - 1)
    def _():
        width = weight_ref.shape[2]
        for block in range(weight_ref.shape[0]):
            source = pl.multiple_of((table_ref[COLUMN] ^ block) * width, width)
            rows = rows_ref[pl.ds(source, width), :].astype(BF16)
            weight_ref[block] = rows
            if block % 2:
                mate_ref[block // 2] = rows


def place(table, slots, after=()):
    groups, capacity, width = slots.shape
    blocks = D // width
    return launch(
        "place", functools.partial(place_kernel, groups), table,
        [(slots, (1, capacity, width), lambda i: (i, 0, 0))],
        [
            ((blocks, width, width), BF16, (blocks, width, width), lambda i: (0, 0, 0)),
            ((blocks // 2, width, width), BF16, (blocks // 2, width, width), lambda i: (0, 0, 0)),
        ],
        grid=(groups,), after=after, scratch=[pltpu.VMEM((D + capacity + SUBLANES, width), F32)],
    )


def layer_kernel(m, table_ref, *refs):
    mixed_refs, (weight_ref, bias_ref, grad_ref, out_ref, pre_ref, sum_ref) = refs[:4], refs[4:]
    tile = out_ref.shape[1]
    preact = bias_ref[...]
    for block in range(4):
        mixed = mixed_refs[block][0] if block == 0 else mixed_refs[block][...]
        preact = preact + product(mixed, weight_ref[block])
    first_row = pl.program_id(0) * tile
    row_ids = first_row + lax.broadcasted_iota(jnp.int32, preact.shape, 0)
    live = row_ids < table_ref[LIMITS + m]
    gate = jax.nn.sigmoid(preact)
    out_ref[0] = jnp.where(live, preact * gate, 0.0).astype(BF16)
    slope = gate * (1.0 + preact * (1.0 - gate))
    grad_pre = jnp.where(live, grad_ref[0].astype(F32) * slope, 0.0).astype(BF16)
    pre_ref[...] = grad_pre

    @pl.when(pl.program_id(0) == 0)
    def _():
        sum_ref[...] = jnp.zeros_like(sum_ref)

    sum_ref[...] += jnp.sum(grad_pre.astype(F32), axis=0, keepdims=True)


def layer(table, m, here, mixed, weight, bias, out_grad, outputs, after=()):
    _, nodes, width = here.shape
    return launch(
        f"layer{m}", functools.partial(layer_kernel, m), table,
        [(here, (1, TILE, width), lambda i: (m, i, 0))]
        + [(part, (TILE, width), lambda i: (i, 0)) for part in mixed]
        + [
            (weight, weight.shape, lambda i: (0, 0, 0)),
            (bias, (1, width), lambda i: (0, 0)),
            (out_grad, (1, TILE, width), lambda i: (m, i, 0)),
        ],
        [
            ((MB, nodes, width), BF16, (1, TILE, width), lambda i: (m, i, 0)),
            ((nodes, width), BF16, (TILE, width), lambda i: (i, 0)),
            ((1, width), F32, (1, width), lambda i: (0, 0)),
        ],
        grid=(nodes // TILE,), after=after, alias=None if outputs is None else (outputs, 0),
    )


def back_kernel(chunks, table_ref, here_hbm, for_mate_hbm, here_ref, weight_ref, *refs):
    own_ref, away_refs = refs[0], refs[1 : 1 + chunks]
    mate_ref, mate_weight_ref, own_total, away_total, send, receive = refs[1 + chunks :]
    half, step = pl.program_id(0), pl.program_id(1)
    tile = here_ref.shape[0]
    mate = partner(lax.axis_index("col"), 1)
    rows = pl.ds(pl.multiple_of(step * tile, tile), tile)

    def copy(number):
        return pltpu.make_async_remote_copy(
            src_ref=(here_hbm, for_mate_hbm)[number],
            dst_ref=(mate_ref, mate_weight_ref)[number],
            send_sem=send.at[number],
            recv_sem=receive.at[number],
            device_id={"col": mate},
            device_id_type=pl.DeviceIdType.MESH,
        )

    @pl.when((half == 0) & (step == 0))
    def _():
        greet_mate(mate)
        copy(1).start()
        copy(0).start()

    @pl.when(half == 0)
    def _():
        here = here_ref[...]
        away_total[rows, :] = product_back(here, weight_ref[2])
        own_total[rows, :] = product_back(here, weight_ref[0])

    @pl.when((half == 1) & (step == 0))
    def _():
        copy(1).wait()
        copy(0).wait()

    @pl.when(half == 1)
    def _():
        mate_rows = mate_ref[rows, :]
        away = (away_total[rows, :] + product_back(mate_rows, mate_weight_ref[1])).astype(BF16)
        width = away.shape[1] // chunks
        for chunk in range(chunks):
            away_refs[chunk][...] = away[:, chunk * width : (chunk + 1) * width]
        own_ref[...] = own_total[rows, :] + product_back(mate_rows, mate_weight_ref[0])


def back(table, m, here, weight, for_mate, chunks, after=()):
    nodes, width = here.shape
    step = width // chunks
    down = lambda h, i: (i * h, 0)
    return launch(
        f"back{m}", functools.partial(back_kernel, chunks), table,
        [
            (here, None, None),
            (for_mate, None, None),
            (here, (WIDE, width), lambda h, i: (i * (1 - h) + h * (nodes // WIDE - 1), 0)),
            (weight, weight.shape, lambda h, i: (0, 0, 0)),
        ],
        [((nodes, width), F32, (WIDE, width), down)]
        + [((nodes, step), BF16, (WIDE, step), down) for _ in range(chunks)],
        grid=(2, nodes // WIDE), after=after, barrier=BACK_ID + m,
        scratch=[
            pltpu.VMEM((nodes, width), BF16),
            pltpu.VMEM(for_mate.shape, BF16),
            pltpu.VMEM((nodes, width), F32),
            pltpu.VMEM((nodes, width), F32),
            pltpu.SemaphoreType.DMA((2,)),
            pltpu.SemaphoreType.DMA((2,)),
        ],
    )


def scatter_kernel(table_ref, own_ref, got_ref, scale_ref, matrix_ref, out_ref, sum_ref):
    @pl.when(pl.program_id(0) == 0)
    def _():
        grad_mixed = (own_ref[...] + got_ref[...].astype(F32)).astype(BF16)
        sum_ref[...] = scaled(grad_mixed.astype(F32), scale_ref[0]).astype(BF16)

    out_ref[0] = product(matrix_ref[0], sum_ref[...]).astype(BF16)


def scatter(table, m, chunk, own, got, scale, matrix, grads, after=()):
    nodes, width = own.shape
    step = got.shape[1]
    return launch(
        f"scatter{m}_{chunk}", scatter_kernel, table,
        [
            (own, (nodes, step), lambda i: (0, chunk)),
            (got, (nodes, step), lambda i: (0, 0)),
            (scale, (1, nodes, LANES), lambda i: (m, 0, 0)),
            (matrix, (1, WIDE, nodes), lambda i: (m, i, 0)),
        ],
        [((MB, nodes, width), BF16, (1, WIDE, step), lambda i: (m, i, chunk))],
        grid=(nodes // WIDE,), after=after, alias=None if grads is None else (grads, 0),
        scratch=[pltpu.VMEM((nodes, step), BF16)],
    )[0]


def weight_kernel(parts, table_ref, *refs):
    blocks = 4
    mixed_refs, pre_refs = refs[: MB * blocks], refs[MB * blocks : MB * blocks + MB]
    bias_refs = refs[MB * blocks + MB : MB * blocks + 2 * MB]
    keep_refs, sent_refs = refs[MB * blocks + 2 * MB :][:2], refs[MB * blocks + 2 * MB + 2 : -2]
    bias_out_ref, total_ref = refs[-2:]
    step = pl.program_id(0)

    for m in range(MB):

        @pl.when(step // parts == m)
        def _(m=m):
            for block in range(blocks):
                source = mixed_refs[m * blocks + block]
                term = product_rows(source[0] if block == 0 else source[...], pre_refs[m][...])
                if m == 0:
                    term = jnp.where(step == 0, term, total_ref[block] + term)
                else:
                    term = total_ref[block] + term
                total_ref[block] = term

    @pl.when(step == parts * MB - 1)
    def _():
        bias_out_ref[...] = sum(ref[...] for ref in bias_refs)
        width = total_ref.shape[1]
        quarter = width // 4
        upper = (table_ref[GROUP] & 1) == 1
        for block in range(blocks):
            rows = pl.ds(pl.multiple_of((table_ref[COLUMN] ^ block) * width, width), width)
            for chunk in range(2):
                low = total_ref[block, :, chunk * quarter : (chunk + 1) * quarter]
                high = total_ref[block, :, (2 + chunk) * quarter : (3 + chunk) * quarter]
                keep_refs[chunk][rows, :] = jnp.where(upper, high, low)
                sent_refs[chunk][rows, :] = jnp.where(upper, low, high).astype(BF16)


def weight_gradient(table, here, mixed, pres, biases, after=()):
    nodes, width = pres[0].shape
    parts = 2
    rows, quarter = nodes // parts, width // 4

    def turn(m):
        return lambda i: (jnp.clip(i - m * parts, 0, parts - 1), 0)

    whole = lambda i: (0, 0)
    ins = []
    for m in range(MB):
        ins.append((here, (1, rows, width), lambda i, m=m: (m, *turn(m)(i))))
        ins += [(part, (rows, width), turn(m)) for part in mixed[m]]
    return launch(
        "weight", functools.partial(weight_kernel, parts), table,
        ins
        + [(pres[m], (rows, width), turn(m)) for m in range(MB)]
        + [(bias, (1, width), whole) for bias in biases],
        [((D, quarter), F32, (D, quarter), whole)] * 2
        + [((D, quarter), BF16, (D, quarter), whole)] * 2
        + [((1, width), F32, (1, width), whole)],
        grid=(parts * MB,), after=after, scratch=[pltpu.VMEM((4, width, width), F32)],
    )


def sum_kernel(groups, capacity, table_ref, *refs):
    keep_refs, sent_refs, bias_ref = refs[0:2], refs[2:4], refs[4]
    own_refs, got_refs, bias_out_ref = refs[5:7], refs[7:9], refs[9]
    *total_refs, land_ref, bias_land_ref = refs[10:14]
    levels = refs[14:]
    depth = groups.bit_length() - 2
    held_refs, out_refs, in_refs = levels[:depth], levels[depth : 2 * depth], levels[2 * depth : 3 * depth]
    end_out_ref, end_in_ref, send, receive, bias_send, bias_receive = levels[3 * depth :]
    own = lax.axis_index("clus")
    rows = keep_refs[0].shape[0]

    def copy(source, target, level, chunk, bit):
        return pltpu.make_async_remote_copy(
            src_ref=source,
            dst_ref=target,
            send_sem=send.at[level, chunk],
            recv_sem=receive.at[level, chunk],
            device_id={"clus": partner(own, bit)},
            device_id_type=pl.DeviceIdType.MESH,
        )

    def bias_copy(level):
        return pltpu.make_async_remote_copy(
            src_ref=bias_land_ref.at[level, 0],
            dst_ref=bias_land_ref.at[level, 1],
            send_sem=bias_send.at[level],
            recv_sem=bias_receive.at[level],
            device_id={"clus": partner(own, 2**level)},
            device_id_type=pl.DeviceIdType.MESH,
        )

    def bias_step(level):
        bias_copy(level).wait()
        total = bias_land_ref[level, 0] + bias_land_ref[level, 1]
        if level <= depth - 1:
            bias_land_ref[level + 1, 0] = total
            bias_copy(level + 1).start()
        else:
            bias_out_ref[...] = total

    copies = []
    barrier = pltpu.get_barrier_semaphore()
    for level in range(depth + 1):
        pl.semaphore_signal(
            barrier, inc=1, device_id={"clus": partner(own, 2**level)}, device_id_type=pl.DeviceIdType.MESH
        )
    pl.semaphore_wait(barrier, depth + 1)
    bias_land_ref[0, 0] = bias_ref[...]
    bias_copy(0).start()
    first = [copy(sent_refs[chunk], land_ref.at[chunk], 0, chunk, 1) for chunk in range(2)]
    for item in first:
        item.start()
    copies += first

    inner = [
        [
            copy(out_refs[level - 1].at[chunk], in_refs[level - 1].at[chunk], level, chunk, 2**level)
            for chunk in range(2)
        ]
        for level in range(1, depth + 1)
    ]
    bit = (own // 2) % 2
    for chunk in range(2):
        first[chunk].wait_recv()
        total_refs[chunk][:rows, :] = keep_refs[chunk][...] + land_ref[chunk].astype(F32)
        total_refs[chunk][rows:, :] = jnp.zeros((2 * capacity + SUBLANES, LANES), F32)
        for j in range(groups // 4):
            gone = 2 * j + 1 - bit
            window = take_rows(total_refs[chunk], table_ref[STARTS + 2 * gone], 2 * capacity, rows - 1)
            out_refs[0][chunk, j] = window.astype(BF16)
        inner[0][chunk].start()
        for j in range(groups // 4):
            kept = 2 * j + bit
            held_refs[0][chunk, j] = take_rows(total_refs[chunk], table_ref[STARTS + 2 * kept], 2 * capacity, rows - 1)
    bias_step(0)
    copies += inner[0]
    for level in range(2, depth + 1):
        bit = (own // 2**level) % 2
        held_ref, in_ref = held_refs[level - 2], in_refs[level - 2]
        for chunk in range(2):
            inner[level - 2][chunk].wait_recv()
            for j in range(held_refs[level - 1].shape[1]):
                gone = 2 * j + 1 - bit
                out_refs[level - 1][chunk, j] = (held_ref[chunk, gone] + in_ref[chunk, gone].astype(F32)).astype(BF16)
            inner[level - 1][chunk].start()
            for j in range(held_refs[level - 1].shape[1]):
                kept = 2 * j + bit
                held_refs[level - 1][chunk, j] = held_ref[chunk, kept] + in_ref[chunk, kept].astype(F32)
        bias_step(level - 1)
        copies += inner[level - 1]
    lead = table_ref[STARTS + (own // 2) * 2]
    ends = [copy(end_out_ref.at[chunk], end_in_ref.at[chunk], depth + 1, chunk, 1) for chunk in range(2)]
    for chunk in range(2):
        inner[depth - 1][chunk].wait_recv()
        total_refs[chunk][: 2 * capacity, :] = held_refs[depth - 1][chunk, 0] + in_refs[depth - 1][chunk, 0].astype(F32)
        other = table_ref[STARTS + partner(own, 1)] - lead
        end_out_ref[chunk] = take_rows(total_refs[chunk], other, capacity, capacity).astype(BF16)
        ends[chunk].start()
        own_refs[chunk][...] = take_rows(total_refs[chunk], table_ref[STARTS + own] - lead, capacity, capacity)
    bias_step(depth)
    for chunk in range(2):
        ends[chunk].wait_recv()
        got_refs[chunk][...] = end_in_ref[chunk]
    for item in copies + ends:
        item.wait_send()


def sum_over_owners(table, groups, capacity, keep, sent, bias, after=()):
    rows, quarter = keep[0].shape
    width = bias.shape[1]
    depth = groups.bit_length() - 2
    flat = lambda i: (0, 0)
    sizes = [(2, groups // 2 ** (level + 1), 2 * capacity, quarter) for level in range(1, depth + 1)]
    shape = (capacity, quarter)
    return launch(
        "sum", functools.partial(sum_kernel, groups, capacity), table,
        [(array, array.shape, flat) for array in (*keep, *sent, bias)],
        [(shape, F32, shape, flat)] * 2 + [(shape, BF16, shape, flat)] * 2 + [(bias.shape, F32, bias.shape, flat)],
        after=after, barrier=SUM_ID,
        scratch=[
            pltpu.VMEM((rows + 2 * capacity + SUBLANES, quarter), F32),
            pltpu.VMEM((rows + 2 * capacity + SUBLANES, quarter), F32),
            pltpu.VMEM((2, rows, quarter), BF16),
            pltpu.VMEM((depth + 1, 2, 1, width), F32),
        ]
        + [pltpu.VMEM(size, F32) for size in sizes]
        + [pltpu.VMEM(size, BF16) for size in sizes]
        + [pltpu.VMEM(size, BF16) for size in sizes]
        + [
            pltpu.VMEM((2, *shape), BF16),
            pltpu.VMEM((2, *shape), BF16),
            pltpu.SemaphoreType.DMA((depth + 2, 2)),
            pltpu.SemaphoreType.DMA((depth + 2, 2)),
            pltpu.SemaphoreType.DMA((depth + 1,)),
            pltpu.SemaphoreType.DMA((depth + 1,)),
        ],
    )


def adamw_update(current, first_moment, second_moment, gradient, step_rate):
    first_new = BETA_ONE * first_moment + (1.0 - BETA_ONE) * gradient
    second_new = BETA_TWO * second_moment + (1.0 - BETA_TWO) * gradient * gradient
    fixed_first = first_new / (1.0 - BETA_ONE**STEP)
    fixed_second = second_new / (1.0 - BETA_TWO**STEP)
    updated = current - step_rate * (
        fixed_first / (jnp.sqrt(fixed_second) + EPSILON) + DECAY * current
    )
    return (updated, first_new, second_new)


def adamw_kernel(groups, table_ref, *refs):
    own_refs, got_refs, (bias_grad_ref, *states), outs = refs[:2], refs[2:4], refs[4:11], refs[11:]
    weights, biases = states[:3], states[3:]
    rows, width = weights[0].shape
    quarter = width // 4
    own = table_ref[GROUP]
    row_ids = pl.program_id(0) * rows + lax.broadcasted_iota(jnp.int32, (rows, quarter), 0)
    used = row_ids < table_ref[STARTS + groups + own]
    for block in range(4):
        mine = (own & 1) == block // 2
        gradient = jnp.where(mine, own_refs[block % 2][...], got_refs[block % 2][...].astype(F32))
        columns = slice(block * quarter, (block + 1) * quarter)
        results = adamw_update(*(ref[:, columns] for ref in weights), gradient, RATE_WEIGHT)
        for out_ref, result in zip(outs[:3], results):
            out_ref[:, columns] = jnp.where(used, result, 0.0)
    results = adamw_update(*(ref[...] for ref in biases), bias_grad_ref[...], RATE_BIAS)
    for out_ref, result in zip(outs[3:], results):
        out_ref[...] = result


def adamw(table, groups, own, got, bias_grad, weights, biases, after=()):
    capacity, width = weights[0].shape
    steps = 4 if capacity % 64 == 0 and capacity >= 256 else 1
    rows, quarter = capacity // steps, width // 4
    down, fixed = (lambda i: (i, 0)), (lambda i: (0, 0))
    return launch(
        "adamw", functools.partial(adamw_kernel, groups), table,
        [(array, (rows, quarter), down) for array in (*own, *got)]
        + [(bias_grad, (1, width), fixed)]
        + [(array, (rows, width), down) for array in weights]
        + [(array, (1, width), fixed) for array in biases],
        [((capacity, width), F32, (rows, width), down)] * 3 + [((1, width), F32, (1, width), fixed)] * 3,
        grid=(steps,), after=after,
    )


def shards(
    features,
    neighbours,
    node_counts,
    row_counts,
    master_weight,
    weight_first,
    weight_second,
    master_bias,
    bias_first,
    bias_second,
    out_grad,
):
    groups = lax.axis_size("clus")
    capacity, width = master_weight.shape
    owner_ids = jnp.arange(groups, dtype=jnp.int32)
    starts = jnp.sum(jnp.where(owner_ids[None, :] < owner_ids[:, None], row_counts[None, :], 0), axis=1)
    table = jnp.concatenate(
        [
            jnp.stack([lax.axis_index("clus"), lax.axis_index("col")]).astype(jnp.int32),
            node_counts[:, 0],
            starts.astype(jnp.int32),
            row_counts,
        ]
    )
    bias_row, bias_first_row, bias_second_row = (
        array.reshape(1, width) for array in (master_bias, bias_first, bias_second)
    )

    picked = []
    for m in range(MB):
        picked.append(pick(table, features, m, picked[-1:]))
    far = [flip(array, "col", 2) for array in picked]

    matrix, scale, here, slots = front(
        table, groups, master_weight, jnp.swapaxes(neighbours, 1, 2), features, [picked[-1]]
    )
    weight, for_mate = place(table, slots, [here])
    last = for_mate
    outputs, input_grads = None, None
    mixed, pres, biases, own, away = [], [], [], [], []
    for m in range(MB):
        there, here_mate, there_mate = mix(table, m, matrix, scale, far[m], here, [last])
        mixed.append([here_mate, there, there_mate])
        outputs, grad_pre, bias_sum = layer(
            table, m, here, mixed[m], weight, bias_row, out_grad, outputs, [there]
        )
        pres.append(grad_pre)
        biases.append(bias_sum)
        own_m, *away_m = back(table, m, grad_pre, weight, for_mate, 2 if m == MB - 1 else 1, [bias_sum])
        own.append(own_m)
        away.append([flip(chunk, "col", 2) for chunk in away_m])
        last = own_m

    keep_low, keep_high, sent_low, sent_high, bias_sum = weight_gradient(
        table, here, mixed, pres, biases, [last]
    )
    *rows, bias_total = sum_over_owners(
        table, groups, capacity, (keep_low, keep_high), (sent_low, sent_high), bias_sum, [last]
    )
    last = bias_total
    for m in range(MB):
        if m == MB - 1:
            updated = adamw(
                table, groups, rows[:2], rows[2:], bias_total,
                (master_weight, weight_first, weight_second), (bias_row, bias_first_row, bias_second_row), [last],
            )
            last = updated[0]
        for chunk, got in enumerate(away[m]):
            last = input_grads = scatter(table, m, chunk, own[m], got, scale, matrix, input_grads, [last])
    return (outputs, input_grads, *updated[:3], *(row.reshape(width) for row in updated[3:]))


def solution(mesh):
    in_specs = (
        P(None, "clus", "col"),
        P(None, "clus", None),
        P(None, "clus"),
        P(),
        P("clus", "col"),
        P("clus", "col"),
        P("clus", "col"),
        P("col"),
        P("col"),
        P("col"),
        P(None, "clus", "col"),
    )
    out_specs = (
        P(None, "clus", "col"),
        P(None, "clus", "col"),
        P("clus", "col"),
        P("clus", "col"),
        P("clus", "col"),
        P("col"),
        P("col"),
        P("col"),
    )
    return jax.shard_map(shards, mesh=mesh, in_specs=in_specs, out_specs=out_specs, check_vma=False)
```

```python
import functools

import jax
import jax.numpy as jnp
from jax import lax
from jax.experimental import pallas as pl
from jax.experimental.pallas import tpu as pltpu
from jax.sharding import PartitionSpec as P

D = 2048
MB = 3
STEP = 10

BETA_ONE = 0.9
BETA_TWO = 0.95
EPSILON = 1e-08
DECAY = 0.1
RATE_WEIGHT = 0.06
RATE_BIAS = 0.6

LANES = 128
DIGIT_BITS = 5
DIGITS = 6
STRIP = 32
SUBLANES = 8
TILE = 256
WIDE = 512
VMEM_BYTES = 48 * 1024 * 1024

GROUP, COLUMN, LIMITS = 0, 1, 2
STARTS = LIMITS + MB

FRONT_ID, SUM_ID, BATCH_ID = 1, 2, 3

F32, BF16 = jnp.float32, jnp.bfloat16


def launch(name, body, table, ins, outs, grid=(1,), after=(), alias=None, scratch=(), barrier=None):
    def spec(block, index):
        if block is None:
            return pl.BlockSpec(memory_space=pl.ANY)
        return pl.BlockSpec(block, lambda *a: index(*a[:-1]))

    unread = ([alias[0]] if alias else []) + [array for array in after if alias is None or array is not alias[0]]

    def kernel(table_ref, *refs):
        body(table_ref, *refs[: len(ins)], *refs[len(ins) + len(unread) :])

    return pl.pallas_call(
        kernel,
        grid_spec=pltpu.PrefetchScalarGridSpec(
            num_scalar_prefetch=1,
            grid=grid,
            in_specs=[spec(block, index) for _, block, index in ins]
            + [pl.BlockSpec(memory_space=pl.ANY)] * len(unread),
            out_specs=[spec(block, index) for _, _, block, index in outs],
            scratch_shapes=list(scratch),
        ),
        out_shape=[jax.ShapeDtypeStruct(shape, kind) for shape, kind, _, _ in outs],
        input_output_aliases={1 + len(ins): alias[1]} if alias else {},
        compiler_params=pltpu.CompilerParams(
            vmem_limit_bytes=VMEM_BYTES, collective_id=barrier, has_side_effects=barrier is not None
        ),
        cost_estimate=pl.CostEstimate(flops=1, bytes_accessed=1, transcendentals=0),
        name=name,
    )(table, *(array for array, _, _ in ins), *unread)


def flip(values, axis, bit):
    size = lax.axis_size(axis)
    return lax.ppermute(values, axis, [(i, i ^ bit) for i in range(size)])


def partner(index, bit):
    return index + bit * (1 - 2 * ((index // bit) % 2))


def product(left, right):
    return jnp.dot(left, right, preferred_element_type=F32)


def product_back(left, right):
    return lax.dot_general(left, right, (((1,), (1,)), ((), ())), preferred_element_type=F32)


def product_rows(left, right):
    return lax.dot_general(left, right, (((0,), (0,)), ((), ())), preferred_element_type=F32)


def scaled(values, scale):
    return values * jnp.concatenate([scale] * (values.shape[1] // LANES), axis=1)


def put_rows(ref, first, rows):
    base = pl.multiple_of((first // SUBLANES) * SUBLANES, SUBLANES)
    offset = first - base
    spare = jnp.zeros((SUBLANES, rows.shape[1]), rows.dtype)
    moved = pltpu.roll(jnp.concatenate([rows, spare], axis=0), offset, 0)
    head = ref[pl.ds(base, SUBLANES), :]
    row_ids = lax.broadcasted_iota(jnp.int32, head.shape, 0)
    ref[pl.ds(base, SUBLANES), :] = jnp.where(row_ids < offset, head, moved[:SUBLANES])
    ref[pl.ds(pl.multiple_of(base + SUBLANES, SUBLANES), rows.shape[0]), :] = moved[SUBLANES:]


def take_rows(ref, first, count, largest):
    bit = 1 << (largest.bit_length() - 1)
    rows = ref[: count + 2 * bit, :]
    while bit:
        length = count + max(bit, SUBLANES)
        moved = rows[bit : bit + length] if bit >= SUBLANES else pltpu.roll(rows, length - bit, 0)
        chosen = (jnp.broadcast_to(first, (length, rows.shape[1])) & bit) != 0
        rows = jnp.where(chosen, moved, rows[:length])
        bit //= 2
    return rows[:count]


def pick_kernel(m, table_ref, source_ref, out_ref, semaphore):
    copy = pltpu.make_async_copy(source_ref.at[m], out_ref, semaphore)
    copy.start()
    copy.wait()


def pick(table, stacked, m, after=()):
    return launch(
        f"pick{m}", functools.partial(pick_kernel, m), table,
        [(stacked, None, None)], [(stacked.shape[1:], stacked.dtype, None, None)],
        after=after, scratch=[pltpu.SemaphoreType.DMA],
    )[0]


def count_tile(limit, first, neighbour_ref, matrix_ref, scale_ref, lanes):
    nodes = matrix_ref.shape[1]
    words = -(-(nodes // LANES) // DIGITS)
    entries = neighbour_ref[0, :, lanes]
    node_ids = first + lax.broadcasted_iota(jnp.int32, entries.shape, 1)
    valid = (entries < limit) & (node_ids < limit)
    low = entries & (LANES - 1)
    high = entries >> 7
    digits = []
    for word in range(words):
        inside = valid & (high >= word * DIGITS) & (high < (word + 1) * DIGITS)
        shift = jnp.where(inside, (high - word * DIGITS) * DIGIT_BITS, 0)
        digits.append(jnp.where(inside, jnp.left_shift(1, shift), 0))
    for strip in range(LANES // STRIP):
        row_ids = strip * STRIP + lax.broadcasted_iota(jnp.int32, (STRIP, LANES), 0)
        sums = [jnp.zeros((STRIP, LANES), jnp.int32) for _ in range(words)]
        for entry in range(entries.shape[0]):
            hit = row_ids == low[entry : entry + 1, :]
            for word in range(words):
                sums[word] = sums[word] + jnp.where(hit, digits[word][entry : entry + 1, :], 0)
        for block in range(nodes // LANES):
            word, digit = block // DIGITS, block % DIGITS
            count = jnp.right_shift(sums[word], digit * DIGIT_BITS) & ((1 << DIGIT_BITS) - 1)
            rows = slice(block * LANES + strip * STRIP, block * LANES + (strip + 1) * STRIP)
            matrix_ref[0, rows, lanes] = count.astype(F32).astype(BF16)
    rows = pl.ds(pl.multiple_of(first, LANES), LANES)
    square = matrix_ref[0, rows, lanes].astype(F32)
    on_diagonal = lax.broadcasted_iota(jnp.int32, square.shape, 0) == lax.broadcasted_iota(jnp.int32, square.shape, 1)
    matrix_ref[0, rows, lanes] = jnp.where(on_diagonal, 2.0 * square + 2.0, square).astype(BF16)
    degree = 1.0 + jnp.sum(valid.astype(F32), axis=0, keepdims=True)
    factor = (node_ids[:1] < limit).astype(F32) / degree
    scale_ref[0, lanes, :] = jnp.transpose(jnp.broadcast_to(factor, (LANES, LANES)))


def front_kernel(
    groups, total, table_ref, master_ref, neighbour_ref, feature_ref, matrix_ref, scale_ref, mixed_ref, slots_ref,
    block_ref, local_semaphore, line_send, line_receive, pair_send, pair_receive,
):
    batch, tile_id = pl.program_id(0), pl.program_id(1)
    tiles = pl.num_programs(1)
    step = batch * tiles + tile_id
    own = lax.axis_index("clus")
    place, side = own // 2, own % 2
    pairs = groups // 2
    other = partner(own, 1)

    def line_copy(direction, hop):
        origin = place - hop if direction == 0 else place + hop
        target = place + 1 if direction == 0 else place - 1
        slot = origin * 2 + side
        return pltpu.make_async_remote_copy(
            src_ref=block_ref if hop == 0 else slots_ref.at[slot],
            dst_ref=slots_ref.at[slot],
            send_sem=line_send.at[direction, hop],
            recv_sem=line_receive.at[direction, hop],
            device_id={"clus": target * 2 + side},
            device_id_type=pl.DeviceIdType.MESH,
        )

    def sends(direction, hop):
        if direction == 0:
            return (place - hop >= 0) & (place + 1 < pairs)
        return (place + hop < pairs) & (place - 1 >= 0)

    def arrives(direction, hop):
        return place - 1 - hop >= 0 if direction == 0 else place + 1 + hop < pairs

    def arrival(direction, hop):
        origin = place - 1 - hop if direction == 0 else place + 1 + hop
        slot = slots_ref.at[origin * 2 + side]
        return pltpu.make_async_remote_copy(
            src_ref=slot,
            dst_ref=slot,
            send_sem=line_send.at[direction, hop],
            recv_sem=line_receive.at[direction, hop],
            device_id={"clus": other},
            device_id_type=pl.DeviceIdType.MESH,
        )

    def pair_copy(direction, hop):
        origin = place - 1 - hop if direction == 0 else place + 1 + hop
        number = 0 if hop < 0 else 1 + 2 * hop + direction
        slot = own if hop < 0 else origin * 2 + side
        return pltpu.make_async_remote_copy(
            src_ref=block_ref if hop < 0 else slots_ref.at[slot],
            dst_ref=slots_ref.at[slot],
            send_sem=pair_send.at[number],
            recv_sem=pair_receive.at[number],
            device_id={"clus": other},
            device_id_type=pl.DeviceIdType.MESH,
        )

    def pair_arrival(direction, hop):
        origin = place - 1 - hop if direction == 0 else place + 1 + hop
        number = 0 if hop < 0 else 1 + 2 * hop + direction
        slot = slots_ref.at[other if hop < 0 else origin * 2 + 1 - side]
        return pltpu.make_async_remote_copy(
            src_ref=slot,
            dst_ref=slot,
            send_sem=pair_send.at[number],
            recv_sem=pair_receive.at[number],
            device_id={"clus": other},
            device_id_type=pl.DeviceIdType.MESH,
        )

    local_copy = pltpu.make_async_copy(block_ref, slots_ref.at[own], local_semaphore)
    hops = pairs - 1

    @pl.when(step == 0)
    def _():
        barrier = pltpu.get_barrier_semaphore()

        def greet(index):
            pl.semaphore_signal(barrier, inc=1, device_id={"clus": index}, device_id_type=pl.DeviceIdType.MESH)

        greet(other)

        @pl.when(place + 1 < pairs)
        def _():
            greet(own + 2)

        @pl.when(place - 1 >= 0)
        def _():
            greet(own - 2)

        pl.semaphore_wait(barrier, 1 + jnp.where(place + 1 < pairs, 1, 0) + jnp.where(place - 1 >= 0, 1, 0))
        block_ref[...] = master_ref[...].astype(BF16)
        local_copy.start()
        for direction in range(2):
            pl.when(sends(direction, 0))(line_copy(direction, 0).start)
        pair_copy(0, -1).start()

    limit = table_ref[LIMITS + batch]
    tile = mixed_ref.shape[1]
    for part in range(tile // LANES):
        first = tile_id * tile + part * LANES
        count_tile(limit, first, neighbour_ref, matrix_ref, scale_ref, slice(part * LANES, (part + 1) * LANES))
    mixed_ref[0] = scaled(product_rows(matrix_ref[0], feature_ref[0]), scale_ref[0]).astype(BF16)

    for hop in range(hops):
        when = min(total - 1, ((hop + 1) * total) // hops)

        @pl.when(step == when)
        def _(hop=hop):
            for direction in range(2):

                @pl.when(arrives(direction, hop))
                def _(direction=direction):
                    arrival(direction, hop).wait_recv()
                    pair_copy(direction, hop).start()

                if hop + 1 < hops:
                    pl.when(sends(direction, hop + 1))(line_copy(direction, hop + 1).start)

    @pl.when(step == total - 1)
    def _():
        local_copy.wait()
        pair_copy(0, -1).wait_send()
        pair_arrival(0, -1).wait_recv()
        for hop in range(hops):
            for direction in range(2):
                pl.when(sends(direction, hop))(line_copy(direction, hop).wait_send)

                @pl.when(arrives(direction, hop))
                def _(direction=direction, hop=hop):
                    pair_copy(direction, hop).wait_send()
                    pair_arrival(direction, hop).wait_recv()


def front(table, groups, master, neighbours, features, after=()):
    _, entries, nodes = neighbours.shape
    capacity, width = master.shape
    hops = groups // 2 - 1
    steps = MB * (nodes // TILE)
    return launch(
        "front", functools.partial(front_kernel, groups, steps), table,
        [
            (master, (capacity, width), lambda b, i: (0, 0)),
            (neighbours, (1, entries, TILE), lambda b, i: (b, 0, i)),
            (features, (1, nodes, width), lambda b, i: (b, 0, 0)),
        ],
        [
            ((MB, nodes, nodes), BF16, (1, nodes, TILE), lambda b, i: (b, 0, i)),
            ((MB, nodes, LANES), F32, (1, TILE, LANES), lambda b, i: (b, i, 0)),
            ((MB, nodes, width), BF16, (1, TILE, width), lambda b, i: (b, i, 0)),
            ((groups, capacity, width), BF16, None, None),
        ],
        grid=(MB, nodes // TILE), after=after, barrier=FRONT_ID,
        scratch=[
            pltpu.VMEM((capacity, width), BF16),
            pltpu.SemaphoreType.DMA,
            pltpu.SemaphoreType.DMA((2, hops)),
            pltpu.SemaphoreType.DMA((2, hops)),
            pltpu.SemaphoreType.DMA((1 + 2 * hops,)),
            pltpu.SemaphoreType.DMA((1 + 2 * hops,)),
        ],
    )


def greet_mate(mate):
    barrier = pltpu.get_barrier_semaphore()
    pl.semaphore_signal(barrier, inc=1, device_id={"col": mate}, device_id_type=pl.DeviceIdType.MESH)
    pl.semaphore_wait(barrier, 1)


def place_kernel(groups, table_ref, slots_ref, weight_ref, mate_ref, rows_ref):
    owner = pl.program_id(0)

    @pl.when(owner == 0)
    def _():
        rows_ref[...] = jnp.zeros_like(rows_ref)

    put_rows(rows_ref, table_ref[STARTS + owner], slots_ref[0].astype(F32))

    @pl.when(owner == groups - 1)
    def _():
        width = weight_ref.shape[2]
        for block in range(weight_ref.shape[0]):
            source = pl.multiple_of((table_ref[COLUMN] ^ block) * width, width)
            rows = rows_ref[pl.ds(source, width), :].astype(BF16)
            weight_ref[block] = rows
            if block % 2:
                mate_ref[block // 2] = rows


def place(table, slots, after=()):
    groups, capacity, width = slots.shape
    blocks = D // width
    return launch(
        "place", functools.partial(place_kernel, groups), table,
        [(slots, (1, capacity, width), lambda i: (i, 0, 0))],
        [
            ((blocks, width, width), BF16, (blocks, width, width), lambda i: (0, 0, 0)),
            ((blocks // 2, width, width), BF16, (blocks // 2, width, width), lambda i: (0, 0, 0)),
        ],
        grid=(groups,), after=after, scratch=[pltpu.VMEM((D + capacity + SUBLANES, width), F32)],
    )


def batch_kernel(m, chunks, table_ref, *refs):
    matrix_hbm, scale_hbm, far_hbm, here_hbm, weight_hbm, for_mate_hbm, grad_hbm, bias_ref = refs[:8]
    refs = refs[8:]
    total_hbm, bias_sum_in = refs[:2] if m else (None, None)
    refs = refs[2:] if m else refs
    out_hbm, own_hbm = refs[:2]
    away_hbm, refs = refs[2 : 2 + chunks], refs[2 + chunks :]
    ended = m == MB - 1
    results, refs = (refs[:4], refs[4:]) if ended else (refs[:1], refs[1:])
    bias_sum_ref, refs = refs[0], refs[1:]
    (
        matrix_ref, scale_ref, far_ref, mixed_ref, weight_ref, mate_weight_ref, grad_ref, out_ref, pre_ref, mate_pre_ref,
        own_ref, away_ref, total_ref, load, store, send, receive,
    ) = refs
    nodes, width = far_ref.shape
    wide, narrow = nodes // WIDE, nodes // TILE
    mate = partner(lax.axis_index("col"), 1)

    def at(index, size):
        return pl.ds(pl.multiple_of(index * size, size), size)

    def matrix_load(i):
        return pltpu.make_async_copy(
            matrix_hbm.at[m, :, at(i, WIDE)], matrix_ref.at[:, at(i, WIDE)], load.at[i]
        )

    loads = [
        pltpu.make_async_copy(source, target, load.at[wide + i])
        for i, (source, target) in enumerate(
            [
                (far_hbm, far_ref),
                (scale_hbm.at[m], scale_ref),
                (weight_hbm, weight_ref),
                (here_hbm.at[m], mixed_ref.at[0]),
                (grad_hbm.at[m], grad_ref),
            ]
            + ([(total_hbm, total_ref)] if m else [])
        )
    ]

    def remote(source, target, number):
        return pltpu.make_async_remote_copy(
            src_ref=source,
            dst_ref=target,
            send_sem=send.at[number],
            recv_sem=receive.at[number],
            device_id={"col": mate},
            device_id_type=pl.DeviceIdType.MESH,
        )

    here_copy = remote(here_hbm.at[m], mixed_ref.at[1], 0)
    weight_copy = remote(for_mate_hbm, mate_weight_ref, 1)

    def there_copy(i):
        return remote(mixed_ref.at[2, at(i, WIDE)], mixed_ref.at[3, at(i, WIDE)], 2 + i)

    def pre_copy(i):
        return remote(pre_ref.at[at(i, TILE)], mate_pre_ref.at[at(i, TILE)], 2 + wide + i)

    loads[0].start()
    matrix_load(0).start()
    loads[1].start()
    for i in range(1, wide):
        matrix_load(i).start()
    for item in loads[2:]:
        item.start()
    greet_mate(mate)
    here_copy.start()
    loads[0].wait()
    loads[1].wait()

    @pl.loop(0, wide)
    def _(i):
        matrix_load(i).wait()
        rows = at(i, WIDE)
        there = product_rows(matrix_ref[:, rows], far_ref[...])
        mixed_ref[2, rows, :] = scaled(there, scale_ref[rows, :]).astype(BF16)
        there_copy(i).start()

    weight_copy.start()
    for item in loads[2:5]:
        item.wait()
    here_copy.wait_recv()
    bias_sum_ref[...] = bias_sum_in[...] if m else jnp.zeros_like(bias_sum_ref)

    @pl.loop(0, narrow)
    def _(i):
        @pl.when(i % (WIDE // TILE) == 0)
        def _():
            there_copy(i // (WIDE // TILE)).wait_recv()

        rows = at(i, TILE)
        preact = bias_ref[...]
        for block in range(4):
            preact = preact + product(mixed_ref[block, rows, :], weight_ref[block])
        row_ids = i * TILE + lax.broadcasted_iota(jnp.int32, preact.shape, 0)
        live = row_ids < table_ref[LIMITS + m]
        gate = jax.nn.sigmoid(preact)
        out_ref[rows, :] = jnp.where(live, preact * gate, 0.0).astype(BF16)
        slope = gate * (1.0 + preact * (1.0 - gate))
        grad_pre = jnp.where(live, grad_ref[rows, :].astype(F32) * slope, 0.0).astype(BF16)
        pre_ref[rows, :] = grad_pre
        pre_copy(i).start()
        bias_sum_ref[...] += jnp.sum(grad_pre.astype(F32), axis=0, keepdims=True)

    stores = [pltpu.make_async_copy(out_ref, out_hbm, store.at[0])]
    stores[0].start()
    weight_copy.wait_recv()

    @pl.loop(0, wide)
    def _(i):
        for part in range(WIDE // TILE):
            pre_copy(i * (WIDE // TILE) + part).wait_recv()
        rows = at(i, WIDE)
        here, there = pre_ref[rows, :], mate_pre_ref[rows, :]
        away = product_back(here, weight_ref[2]) + product_back(there, mate_weight_ref[1])
        away_ref[rows, :] = away.astype(BF16)
        own_ref[rows, :] = product_back(here, weight_ref[0]) + product_back(there, mate_weight_ref[0])

    step = width // chunks
    for chunk in range(chunks):
        stores.append(
            pltpu.make_async_copy(
                away_ref.at[:, chunk * step : (chunk + 1) * step], away_hbm[chunk], store.at[1 + chunk]
            )
        )
    stores.append(pltpu.make_async_copy(own_ref, own_hbm, store.at[1 + chunks]))
    for item in stores[1:]:
        item.start()

    if m:
        loads[5].wait()

    @pl.loop(0, 4)
    def _(block):
        term = product_rows(mixed_ref[block], pre_ref[...])
        total_ref[block] = total_ref[block] + term if m else term

    if ended:
        quarter = width // 4
        upper = lax.axis_index("clus") % 2 == 1
        column = lax.axis_index("col")
        for block in range(4):
            source = partner(column, 1) if block % 2 else column
            source = partner(source, 2) if block >= 2 else source
            rows = at(source, width)
            for chunk in range(2):
                low = total_ref[block, :, chunk * quarter : (chunk + 1) * quarter]
                high = total_ref[block, :, (2 + chunk) * quarter : (3 + chunk) * quarter]
                results[chunk][rows, :] = jnp.where(upper, high, low)
                results[2 + chunk][rows, :] = jnp.where(upper, low, high).astype(BF16)
    else:
        stores.append(pltpu.make_async_copy(total_ref, results[0], store.at[2 + chunks]))
        stores[-1].start()
    here_copy.wait_send()
    weight_copy.wait_send()
    for i in range(wide):
        there_copy(i).wait_send()
    for i in range(narrow):
        pre_copy(i).wait_send()
    for item in stores:
        item.wait()


def batch(table, m, matrix, scale, far, here, weight, for_mate, out_grad, bias, total, bias_sum, chunks, after=()):
    nodes, width = far.shape
    wide, narrow = nodes // WIDE, nodes // TILE
    quarter = width // 4
    flat = lambda i: (0, 0)
    ended = m == MB - 1
    if ended:
        results = [((D, quarter), F32, (D, quarter), flat)] * 2 + [((D, quarter), BF16, (D, quarter), flat)] * 2
    else:
        results = [((4, width, width), F32, None, None)]
    return launch(
        f"batch{m}", functools.partial(batch_kernel, m, chunks), table,
        [(array, None, None) for array in (matrix, scale, far, here, weight, for_mate, out_grad)]
        + [(bias, (1, width), flat)]
        + ([(total, None, None), (bias_sum, (1, width), flat)] if m else []),
        [((nodes, width), BF16, None, None), ((nodes, width), F32, None, None)]
        + [((nodes, width // chunks), BF16, None, None)] * chunks
        + results
        + [((1, width), F32, (1, width), flat)],
        after=after, barrier=BATCH_ID + m,
        scratch=[
            pltpu.VMEM((nodes, nodes), BF16),
            pltpu.VMEM((nodes, LANES), F32),
            pltpu.VMEM((nodes, width), BF16),
            pltpu.VMEM((4, nodes, width), BF16),
            pltpu.VMEM(weight.shape, BF16),
            pltpu.VMEM(for_mate.shape, BF16),
            pltpu.VMEM((nodes, width), BF16),
            pltpu.VMEM((nodes, width), BF16),
            pltpu.VMEM((nodes, width), BF16),
            pltpu.VMEM((nodes, width), BF16),
            pltpu.VMEM((nodes, width), F32),
            pltpu.VMEM((nodes, width), BF16),
            pltpu.VMEM((4, width, width), F32),
            pltpu.SemaphoreType.DMA((wide + 6,)),
            pltpu.SemaphoreType.DMA((3 + chunks,)),
            pltpu.SemaphoreType.DMA((2 + wide + narrow,)),
            pltpu.SemaphoreType.DMA((2 + wide + narrow,)),
        ],
    )


def collect_kernel(table_ref, *refs):
    sources, out_ref, semaphore = refs[:MB], refs[MB], refs[MB + 1]
    copies = [pltpu.make_async_copy(sources[m], out_ref.at[m], semaphore.at[m]) for m in range(MB)]
    for item in copies:
        item.start()
    for item in copies:
        item.wait()


def collect(table, arrays, after=()):
    return launch(
        "collect", collect_kernel, table,
        [(array, None, None) for array in arrays],
        [((MB, *arrays[0].shape), arrays[0].dtype, None, None)],
        after=after, scratch=[pltpu.SemaphoreType.DMA((MB,))],
    )[0]


def scatter_kernel(table_ref, own_ref, got_ref, scale_ref, matrix_ref, out_ref, sum_ref):
    @pl.when(pl.program_id(0) == 0)
    def _():
        grad_mixed = (own_ref[...] + got_ref[...].astype(F32)).astype(BF16)
        sum_ref[...] = scaled(grad_mixed.astype(F32), scale_ref[0]).astype(BF16)

    out_ref[0] = product(matrix_ref[0], sum_ref[...]).astype(BF16)


def scatter(table, m, chunk, own, got, scale, matrix, grads, after=()):
    nodes, width = own.shape
    step = got.shape[1]
    return launch(
        f"scatter{m}_{chunk}", scatter_kernel, table,
        [
            (own, (nodes, step), lambda i: (0, chunk)),
            (got, (nodes, step), lambda i: (0, 0)),
            (scale, (1, nodes, LANES), lambda i: (m, 0, 0)),
            (matrix, (1, WIDE, nodes), lambda i: (m, i, 0)),
        ],
        [((MB, nodes, width), BF16, (1, WIDE, step), lambda i: (m, i, chunk))],
        grid=(nodes // WIDE,), after=after, alias=None if grads is None else (grads, 0),
        scratch=[pltpu.VMEM((nodes, step), BF16)],
    )[0]


def sum_kernel(groups, capacity, table_ref, *refs):
    keep_refs, sent_refs, bias_ref = refs[0:2], refs[2:4], refs[4]
    own_refs, got_refs, bias_out_ref = refs[5:7], refs[7:9], refs[9]
    *total_refs, land_ref, bias_land_ref = refs[10:14]
    levels = refs[14:]
    depth = groups.bit_length() - 2
    held_refs, out_refs, in_refs = levels[:depth], levels[depth : 2 * depth], levels[2 * depth : 3 * depth]
    end_out_ref, end_in_ref, send, receive, bias_send, bias_receive = levels[3 * depth :]
    own = lax.axis_index("clus")
    rows = keep_refs[0].shape[0]

    def copy(source, target, level, chunk, bit):
        return pltpu.make_async_remote_copy(
            src_ref=source,
            dst_ref=target,
            send_sem=send.at[level, chunk],
            recv_sem=receive.at[level, chunk],
            device_id={"clus": partner(own, bit)},
            device_id_type=pl.DeviceIdType.MESH,
        )

    def bias_copy(level):
        return pltpu.make_async_remote_copy(
            src_ref=bias_land_ref.at[level, 0],
            dst_ref=bias_land_ref.at[level, 1],
            send_sem=bias_send.at[level],
            recv_sem=bias_receive.at[level],
            device_id={"clus": partner(own, 2**level)},
            device_id_type=pl.DeviceIdType.MESH,
        )

    def bias_step(level):
        bias_copy(level).wait()
        total = bias_land_ref[level, 0] + bias_land_ref[level, 1]
        if level <= depth - 1:
            bias_land_ref[level + 1, 0] = total
            bias_copy(level + 1).start()
        else:
            bias_out_ref[...] = total

    copies = []
    barrier = pltpu.get_barrier_semaphore()
    for level in range(depth + 1):
        pl.semaphore_signal(
            barrier, inc=1, device_id={"clus": partner(own, 2**level)}, device_id_type=pl.DeviceIdType.MESH
        )
    pl.semaphore_wait(barrier, depth + 1)
    bias_land_ref[0, 0] = bias_ref[...]
    bias_copy(0).start()
    first = [copy(sent_refs[chunk], land_ref.at[chunk], 0, chunk, 1) for chunk in range(2)]
    for item in first:
        item.start()
    copies += first

    inner = [
        [
            copy(out_refs[level - 1].at[chunk], in_refs[level - 1].at[chunk], level, chunk, 2**level)
            for chunk in range(2)
        ]
        for level in range(1, depth + 1)
    ]
    bit = (own // 2) % 2
    for chunk in range(2):
        first[chunk].wait_recv()
        total_refs[chunk][:rows, :] = keep_refs[chunk][...] + land_ref[chunk].astype(F32)
        total_refs[chunk][rows:, :] = jnp.zeros((2 * capacity + SUBLANES, LANES), F32)
        for j in range(groups // 4):
            gone = 2 * j + 1 - bit
            window = take_rows(total_refs[chunk], table_ref[STARTS + 2 * gone], 2 * capacity, rows - 1)
            out_refs[0][chunk, j] = window.astype(BF16)
        inner[0][chunk].start()
        for j in range(groups // 4):
            kept = 2 * j + bit
            held_refs[0][chunk, j] = take_rows(total_refs[chunk], table_ref[STARTS + 2 * kept], 2 * capacity, rows - 1)
    bias_step(0)
    copies += inner[0]
    for level in range(2, depth + 1):
        bit = (own // 2**level) % 2
        held_ref, in_ref = held_refs[level - 2], in_refs[level - 2]
        for chunk in range(2):
            inner[level - 2][chunk].wait_recv()
            for j in range(held_refs[level - 1].shape[1]):
                gone = 2 * j + 1 - bit
                out_refs[level - 1][chunk, j] = (held_ref[chunk, gone] + in_ref[chunk, gone].astype(F32)).astype(BF16)
            inner[level - 1][chunk].start()
            for j in range(held_refs[level - 1].shape[1]):
                kept = 2 * j + bit
                held_refs[level - 1][chunk, j] = held_ref[chunk, kept] + in_ref[chunk, kept].astype(F32)
        bias_step(level - 1)
        copies += inner[level - 1]
    lead = table_ref[STARTS + (own // 2) * 2]
    ends = [copy(end_out_ref.at[chunk], end_in_ref.at[chunk], depth + 1, chunk, 1) for chunk in range(2)]
    for chunk in range(2):
        inner[depth - 1][chunk].wait_recv()
        total_refs[chunk][: 2 * capacity, :] = held_refs[depth - 1][chunk, 0] + in_refs[depth - 1][chunk, 0].astype(F32)
        other = table_ref[STARTS + partner(own, 1)] - lead
        end_out_ref[chunk] = take_rows(total_refs[chunk], other, capacity, capacity).astype(BF16)
        ends[chunk].start()
        own_refs[chunk][...] = take_rows(total_refs[chunk], table_ref[STARTS + own] - lead, capacity, capacity)
    bias_step(depth)
    for chunk in range(2):
        ends[chunk].wait_recv()
        got_refs[chunk][...] = end_in_ref[chunk]
    for item in copies + ends:
        item.wait_send()


def sum_over_owners(table, groups, capacity, keep, sent, bias, after=()):
    rows, quarter = keep[0].shape
    width = bias.shape[1]
    depth = groups.bit_length() - 2
    flat = lambda i: (0, 0)
    sizes = [(2, groups // 2 ** (level + 1), 2 * capacity, quarter) for level in range(1, depth + 1)]
    shape = (capacity, quarter)
    return launch(
        "sum", functools.partial(sum_kernel, groups, capacity), table,
        [(array, array.shape, flat) for array in (*keep, *sent, bias)],
        [(shape, F32, shape, flat)] * 2 + [(shape, BF16, shape, flat)] * 2 + [(bias.shape, F32, bias.shape, flat)],
        after=after, barrier=SUM_ID,
        scratch=[
            pltpu.VMEM((rows + 2 * capacity + SUBLANES, quarter), F32),
            pltpu.VMEM((rows + 2 * capacity + SUBLANES, quarter), F32),
            pltpu.VMEM((2, rows, quarter), BF16),
            pltpu.VMEM((depth + 1, 2, 1, width), F32),
        ]
        + [pltpu.VMEM(size, F32) for size in sizes]
        + [pltpu.VMEM(size, BF16) for size in sizes]
        + [pltpu.VMEM(size, BF16) for size in sizes]
        + [
            pltpu.VMEM((2, *shape), BF16),
            pltpu.VMEM((2, *shape), BF16),
            pltpu.SemaphoreType.DMA((depth + 2, 2)),
            pltpu.SemaphoreType.DMA((depth + 2, 2)),
            pltpu.SemaphoreType.DMA((depth + 1,)),
            pltpu.SemaphoreType.DMA((depth + 1,)),
        ],
    )


def adamw_update(current, first_moment, second_moment, gradient, step_rate):
    first_new = BETA_ONE * first_moment + (1.0 - BETA_ONE) * gradient
    second_new = BETA_TWO * second_moment + (1.0 - BETA_TWO) * gradient * gradient
    fixed_first = first_new / (1.0 - BETA_ONE**STEP)
    fixed_second = second_new / (1.0 - BETA_TWO**STEP)
    updated = current - step_rate * (
        fixed_first / (jnp.sqrt(fixed_second) + EPSILON) + DECAY * current
    )
    return (updated, first_new, second_new)


def adamw_kernel(groups, table_ref, *refs):
    own_refs, got_refs, (bias_grad_ref, *states), outs = refs[:2], refs[2:4], refs[4:11], refs[11:]
    weights, biases = states[:3], states[3:]
    rows, width = weights[0].shape
    quarter = width // 4
    own = table_ref[GROUP]
    row_ids = pl.program_id(0) * rows + lax.broadcasted_iota(jnp.int32, (rows, quarter), 0)
    used = row_ids < table_ref[STARTS + groups + own]
    for block in range(4):
        mine = (own & 1) == block // 2
        gradient = jnp.where(mine, own_refs[block % 2][...], got_refs[block % 2][...].astype(F32))
        columns = slice(block * quarter, (block + 1) * quarter)
        results = adamw_update(*(ref[:, columns] for ref in weights), gradient, RATE_WEIGHT)
        for out_ref, result in zip(outs[:3], results):
            out_ref[:, columns] = jnp.where(used, result, 0.0)
    results = adamw_update(*(ref[...] for ref in biases), bias_grad_ref[...], RATE_BIAS)
    for out_ref, result in zip(outs[3:], results):
        out_ref[...] = result


def adamw(table, groups, own, got, bias_grad, weights, biases, after=()):
    capacity, width = weights[0].shape
    steps = 4 if capacity % 64 == 0 and capacity >= 256 else 1
    rows, quarter = capacity // steps, width // 4
    down, fixed = (lambda i: (i, 0)), (lambda i: (0, 0))
    return launch(
        "adamw", functools.partial(adamw_kernel, groups), table,
        [(array, (rows, quarter), down) for array in (*own, *got)]
        + [(bias_grad, (1, width), fixed)]
        + [(array, (rows, width), down) for array in weights]
        + [(array, (1, width), fixed) for array in biases],
        [((capacity, width), F32, (rows, width), down)] * 3 + [((1, width), F32, (1, width), fixed)] * 3,
        grid=(steps,), after=after,
    )


def shards(
    features,
    neighbours,
    node_counts,
    row_counts,
    master_weight,
    weight_first,
    weight_second,
    master_bias,
    bias_first,
    bias_second,
    out_grad,
):
    groups = lax.axis_size("clus")
    capacity, width = master_weight.shape
    owner_ids = jnp.arange(groups, dtype=jnp.int32)
    starts = jnp.sum(jnp.where(owner_ids[None, :] < owner_ids[:, None], row_counts[None, :], 0), axis=1)
    table = jnp.concatenate(
        [
            jnp.stack([lax.axis_index("clus"), lax.axis_index("col")]).astype(jnp.int32),
            node_counts[:, 0],
            starts.astype(jnp.int32),
            row_counts,
        ]
    )
    bias_row, bias_first_row, bias_second_row = (
        array.reshape(1, width) for array in (master_bias, bias_first, bias_second)
    )

    picked = []
    for m in range(MB):
        picked.append(pick(table, features, m, picked[-1:]))
    far = [flip(array, "col", 2) for array in picked]

    matrix, scale, here, slots = front(
        table, groups, master_weight, jnp.swapaxes(neighbours, 1, 2), features, [picked[-1]]
    )
    weight, for_mate = place(table, slots, [here])
    last = for_mate
    input_grads, total, bias_sum = None, None, None
    outputs, own, away = [], [], []
    for m in range(MB):
        chunks = 2 if m == MB - 1 else 1
        out_m, own_m, *rest = batch(
            table, m, matrix, scale, far[m], here, weight, for_mate, out_grad, bias_row, total, bias_sum, chunks,
            [last],
        )
        outputs.append(out_m)
        own.append(own_m)
        away.append([flip(chunk, "col", 2) for chunk in rest[:chunks]])
        total, bias_sum = rest[chunks], rest[-1]
        last = bias_sum

    keep_low, keep_high, sent_low, sent_high, bias_sum = rest[chunks:]
    *rows, bias_total = sum_over_owners(
        table, groups, capacity, (keep_low, keep_high), (sent_low, sent_high), bias_sum, [last]
    )
    last = outputs = collect(table, outputs, [bias_total])
    for m in range(MB):
        if m == MB - 1:
            updated = adamw(
                table, groups, rows[:2], rows[2:], bias_total,
                (master_weight, weight_first, weight_second), (bias_row, bias_first_row, bias_second_row), [last],
            )
            last = updated[0]
        for chunk, got in enumerate(away[m]):
            last = input_grads = scatter(table, m, chunk, own[m], got, scale, matrix, input_grads, [last])
    return (outputs, input_grads, *updated[:3], *(row.reshape(width) for row in updated[3:]))


def solution(mesh):
    in_specs = (
        P(None, "clus", "col"),
        P(None, "clus", None),
        P(None, "clus"),
        P(),
        P("clus", "col"),
        P("clus", "col"),
        P("clus", "col"),
        P("col"),
        P("col"),
        P("col"),
        P(None, "clus", "col"),
    )
    out_specs = (
        P(None, "clus", "col"),
        P(None, "clus", "col"),
        P("clus", "col"),
        P("clus", "col"),
        P("clus", "col"),
        P("col"),
        P("col"),
        P("col"),
    )
    return jax.shard_map(shards, mesh=mesh, in_specs=in_specs, out_specs=out_specs, check_vma=False)
```

```python
import functools

import jax
import jax.numpy as jnp
from jax import lax
from jax.experimental import pallas as pl
from jax.experimental.pallas import tpu as pltpu
from jax.sharding import PartitionSpec as P

D = 2048
MB = 3
STEP = 10

BETA_ONE = 0.9
BETA_TWO = 0.95
EPSILON = 1e-08
DECAY = 0.1
RATE_WEIGHT = 0.06
RATE_BIAS = 0.6

LANES = 128
DIGIT_BITS = 5
DIGITS = 6
STRIP = 32
SUBLANES = 8
TILE = 256
WIDE = 512
HALVES = 2
PIECES = 4
UNROLL = 3
CHUNKS = 8
MIB = 1024 * 1024
SMALL = 1 << 16

GROUP, COLUMN, LIMITS = 0, 1, 2
STARTS = LIMITS + MB

FRONT_ID, SUM_ID, BATCH_ID = 1, 2, 3

F32, BF16 = jnp.float32, jnp.bfloat16


class Kept:
    def __init__(self, array, space=pltpu.VMEM):
        self.array, self.space = array, space


def located(item):
    if isinstance(item, Kept):
        return pltpu.with_memory_space_constraint(item.array, item.space) if item.space else item.array
    return pltpu.with_memory_space_constraint(item, pltpu.HBM) if item.size > SMALL else item


def launch(name, body, table, ins, outs, grid=(1,), after=(), alias=None, scratch=(), barrier=None, vmem=16):
    tables = [] if table is None else [table]

    def spec(block, index):
        if block is None:
            return pl.BlockSpec(memory_space=pl.ANY)
        return pl.BlockSpec(block, lambda *a: index(*a[: len(grid)]))

    unread = ([alias[0]] if alias else []) + [array for array in after if alias is None or array is not alias[0]]

    def kernel(*refs):
        table_refs, refs = refs[: len(tables)], refs[len(tables) :]
        body(*table_refs, *refs[: len(ins)], *refs[len(ins) + len(unread) :])

    return pl.pallas_call(
        kernel,
        grid_spec=pltpu.PrefetchScalarGridSpec(
            num_scalar_prefetch=len(tables),
            grid=grid,
            in_specs=[spec(block, index) for _, block, index in ins]
            + [pl.BlockSpec(memory_space=pl.ANY)] * len(unread),
            out_specs=[spec(out[2], out[3]) for out in outs],
            scratch_shapes=list(scratch),
        ),
        out_shape=[
            pltpu.HBM(out[0], out[1]) if out[2] is None else (out[4] if len(out) > 4 else jax.ShapeDtypeStruct)(out[0], out[1])
            for out in outs
        ],
        input_output_aliases={len(tables) + len(ins): alias[1]} if alias else {},
        compiler_params=pltpu.CompilerParams(
            vmem_limit_bytes=vmem * MIB, collective_id=barrier, has_side_effects=barrier is not None
        ),
        cost_estimate=pl.CostEstimate(flops=1, bytes_accessed=1, transcendentals=0),
        name=name,
    )(*tables, *(located(item[0]) for item in ins), *(located(item) for item in unread))


def flip(values, axis, bit):
    size = lax.axis_size(axis)
    return lax.ppermute(values, axis, [(i, i ^ bit) for i in range(size)])


def partner(index, bit):
    return index + bit * (1 - 2 * ((index // bit) % 2))


def product(left, right):
    return jnp.dot(left, right, preferred_element_type=F32)


def product_back(left, right):
    return lax.dot_general(left, right, (((1,), (1,)), ((), ())), preferred_element_type=F32)


def product_rows(left, right):
    return lax.dot_general(left, right, (((0,), (0,)), ((), ())), preferred_element_type=F32)


def scaled(values, scale):
    return values * jnp.concatenate([scale] * (values.shape[1] // LANES), axis=1)


def put_rows(ref, first, rows):
    base = pl.multiple_of((first // SUBLANES) * SUBLANES, SUBLANES)
    offset = first - base
    moved = jnp.concatenate([rows, jnp.zeros((SUBLANES, rows.shape[1]), rows.dtype)], axis=0)
    wanted = jnp.broadcast_to(offset, moved.shape)
    for bit in (1, 2, 4):
        moved = jnp.where((wanted & bit) != 0, pltpu.roll(moved, bit, 0), moved)
    head = ref[pl.ds(base, SUBLANES), :]
    row_ids = lax.broadcasted_iota(jnp.int32, head.shape, 0)
    ref[pl.ds(base, SUBLANES), :] = jnp.where(row_ids < offset, head, moved[:SUBLANES])
    ref[pl.ds(pl.multiple_of(base + SUBLANES, SUBLANES), rows.shape[0]), :] = moved[SUBLANES:]


def take_rows(ref, first, count, largest):
    bit = 1 << (largest.bit_length() - 1)
    rows = ref[...]
    while bit:
        length = count + max(bit, SUBLANES)
        if bit >= SUBLANES:
            moved = rows[bit : bit + length]
            missing = length - moved.shape[0]
            if missing:
                moved = jnp.concatenate([moved, jnp.zeros((missing, rows.shape[1]), rows.dtype)], axis=0)
        else:
            moved = pltpu.roll(rows, length - bit, 0)
        chosen = (jnp.broadcast_to(first, (length, rows.shape[1])) & bit) != 0
        rows = jnp.where(chosen, moved, rows[:length])
        bit //= 2
    return rows[:count]


def relay(sources, targets, buffers, load, store):
    def piece(ref, i):
        rows = ref.shape[0] // PIECES
        return ref.at[pl.ds(i * rows, rows)]

    loads, stores = [], []
    for number, (source, target, buffer) in enumerate(zip(sources, targets, buffers)):
        for i in range(PIECES):
            place = number * PIECES + i
            loads.append(pltpu.make_async_copy(piece(source, i), piece(buffer, i), load.at[place]))
            stores.append(pltpu.make_async_copy(piece(buffer, i), piece(target, i), store.at[place]))
    return loads, stores


def pick_kernel(batches, source_ref, *refs):
    targets, (buffer_ref, load, store) = refs[:-3], refs[-3:]
    loads, stores = relay(
        [source_ref.at[m] for m in batches], targets, [buffer_ref.at[i] for i in range(len(batches))], load, store
    )
    for item in loads:
        item.start()
    for item, onward in zip(loads, stores):
        item.wait()
        onward.start()
    for item in stores:
        item.wait()


def pick(stacked, batches, after=()):
    count = len(batches)
    return launch(
        f"pick{batches[0]}", functools.partial(pick_kernel, batches), None,
        [(stacked, None, None)], [(stacked.shape[1:], stacked.dtype, None, None)] * count,
        after=after,
        scratch=[
            pltpu.VMEM((count, *stacked.shape[1:]), stacked.dtype),
            pltpu.SemaphoreType.DMA((count * PIECES,)),
            pltpu.SemaphoreType.DMA((count * PIECES,)),
        ],
    )


def count_tile(limit, first, neighbour_ref, matrix_ref, scale_ref, lanes):
    nodes = matrix_ref.shape[1]
    words = -(-(nodes // LANES) // DIGITS)
    entries = neighbour_ref[0, :, lanes]
    node_ids = first + lax.broadcasted_iota(jnp.int32, entries.shape, 1)
    valid = (entries < limit) & (node_ids < limit)
    low = entries & (LANES - 1)
    high = entries >> 7
    digits = []
    for word in range(words):
        inside = valid & (high >= word * DIGITS) & (high < (word + 1) * DIGITS)
        shift = jnp.where(inside, (high - word * DIGITS) * DIGIT_BITS, 0)
        digits.append(jnp.where(inside, jnp.left_shift(1, shift), 0))
    for strip in range(LANES // STRIP):
        row_ids = strip * STRIP + lax.broadcasted_iota(jnp.int32, (STRIP, LANES), 0)
        sums = [jnp.zeros((STRIP, LANES), jnp.int32) for _ in range(words)]
        for entry in range(entries.shape[0]):
            hit = row_ids == low[entry : entry + 1, :]
            for word in range(words):
                sums[word] = sums[word] + jnp.where(hit, digits[word][entry : entry + 1, :], 0)
        for block in range(nodes // LANES):
            word, digit = block // DIGITS, block % DIGITS
            count = jnp.right_shift(sums[word], digit * DIGIT_BITS) & ((1 << DIGIT_BITS) - 1)
            rows = slice(block * LANES + strip * STRIP, block * LANES + (strip + 1) * STRIP)
            matrix_ref[0, rows, lanes] = count.astype(F32).astype(BF16)
    rows = pl.ds(pl.multiple_of(first, LANES), LANES)
    square = matrix_ref[0, rows, lanes].astype(F32)
    on_diagonal = lax.broadcasted_iota(jnp.int32, square.shape, 0) == lax.broadcasted_iota(jnp.int32, square.shape, 1)
    matrix_ref[0, rows, lanes] = jnp.where(on_diagonal, 2.0 * square + 2.0, square).astype(BF16)
    degree = 1.0 + jnp.sum(valid.astype(F32), axis=0, keepdims=True)
    factor = (node_ids[:1] < limit).astype(F32) / degree
    scale_ref[0, lanes, :] = jnp.transpose(jnp.broadcast_to(factor, (LANES, LANES)))


def front_kernel(
    groups, total, table_ref, master_ref, neighbour_ref, feature_ref, matrix_ref, scale_ref, mixed_ref, slots_ref,
    block_ref, local_semaphore, line_send, line_receive, pair_send, pair_receive,
):
    batch, tile_id = pl.program_id(0), pl.program_id(1)
    tiles = pl.num_programs(1)
    step = batch * tiles + tile_id
    own = lax.axis_index("clus")
    place, side = own // 2, own % 2
    pairs = groups // 2
    other = partner(own, 1)

    def rows_of(half):
        size = block_ref.shape[0] // HALVES
        return pl.ds(half * size, size)

    def remote(source, target, sent, received, device):
        return pltpu.make_async_remote_copy(
            src_ref=source,
            dst_ref=target,
            send_sem=sent,
            recv_sem=received,
            device_id={"clus": device},
            device_id_type=pl.DeviceIdType.MESH,
        )

    def origin_of(direction, hop):
        return place - 1 - hop if direction == 0 else place + 1 + hop

    def line_copy(direction, hop, half):
        slot = (place - hop if direction == 0 else place + hop) * 2 + side
        target = slots_ref.at[slot, rows_of(half)]
        return remote(
            block_ref.at[rows_of(half)] if hop == 0 else target, target,
            line_send.at[direction, hop, half], line_receive.at[direction, hop, half],
            own + 2 if direction == 0 else own - 2,
        )

    def sends(direction, hop):
        if direction == 0:
            return (place - hop >= 0) & (place + 1 < pairs)
        return (place + hop < pairs) & (place - 1 >= 0)

    def arrives(direction, hop):
        return place - 1 - hop >= 0 if direction == 0 else place + 1 + hop < pairs

    def arrival(direction, hop, half):
        target = slots_ref.at[origin_of(direction, hop) * 2 + side, rows_of(half)]
        return remote(
            target, target, line_send.at[direction, hop, half], line_receive.at[direction, hop, half], other
        )

    def pair_copy(direction, hop, half):
        slot = own if hop < 0 else origin_of(direction, hop) * 2 + side
        number = 0 if hop < 0 else 1 + 2 * hop + direction
        target = slots_ref.at[slot, rows_of(half)]
        return remote(
            block_ref.at[rows_of(half)] if hop < 0 else target, target,
            pair_send.at[number, half], pair_receive.at[number, half], other,
        )

    def pair_arrival(direction, hop, half):
        slot = other if hop < 0 else origin_of(direction, hop) * 2 + 1 - side
        number = 0 if hop < 0 else 1 + 2 * hop + direction
        target = slots_ref.at[slot, rows_of(half)]
        return remote(target, target, pair_send.at[number, half], pair_receive.at[number, half], other)

    local_copy = pltpu.make_async_copy(block_ref, slots_ref.at[own], local_semaphore)
    hops = pairs - 1

    @pl.when(step == 0)
    def _():
        barrier = pltpu.get_barrier_semaphore()

        def greet(index):
            pl.semaphore_signal(barrier, inc=1, device_id={"clus": index}, device_id_type=pl.DeviceIdType.MESH)

        greet(other)

        @pl.when(place + 1 < pairs)
        def _():
            greet(own + 2)

        @pl.when(place - 1 >= 0)
        def _():
            greet(own - 2)

        pl.semaphore_wait(barrier, 1 + jnp.where(place + 1 < pairs, 1, 0) + jnp.where(place - 1 >= 0, 1, 0))
        block_ref[...] = master_ref[...].astype(BF16)
        for half in range(HALVES):
            for direction in range(2):
                pl.when(sends(direction, 0))(line_copy(direction, 0, half).start)
            pair_copy(0, -1, half).start()
        local_copy.start()

    limit = table_ref[LIMITS + batch]
    tile = mixed_ref.shape[1]
    for part in range(tile // LANES):
        first = tile_id * tile + part * LANES
        count_tile(limit, first, neighbour_ref, matrix_ref, scale_ref, slice(part * LANES, (part + 1) * LANES))
    mixed_ref[0] = scaled(product_rows(matrix_ref[0], feature_ref[0]), scale_ref[0]).astype(BF16)

    for event in range(hops * HALVES):
        hop, half = event // HALVES, event % HALVES

        @pl.when(step == min(total - 1, ((event + 1) * total) // (hops * HALVES)))
        def _(hop=hop, half=half):
            for direction in range(2):

                @pl.when(arrives(direction, hop))
                def _(direction=direction):
                    arrival(direction, hop, half).wait_recv()
                    pair_copy(direction, hop, half).start()

                if hop + 1 < hops:
                    pl.when(sends(direction, hop + 1))(line_copy(direction, hop + 1, half).start)

    @pl.when(step == total - 1)
    def _():
        local_copy.wait()
        for half in range(HALVES):
            pair_copy(0, -1, half).wait_send()
            pair_arrival(0, -1, half).wait_recv()
            for hop in range(hops):
                for direction in range(2):
                    pl.when(sends(direction, hop))(line_copy(direction, hop, half).wait_send)

                    @pl.when(arrives(direction, hop))
                    def _(direction=direction, hop=hop, half=half):
                        pair_copy(direction, hop, half).wait_send()
                        pair_arrival(direction, hop, half).wait_recv()


def front(table, groups, master, neighbours, features, after=()):
    _, entries, nodes = neighbours.shape
    capacity, width = master.shape
    hops = groups // 2 - 1
    steps = MB * (nodes // TILE)
    return launch(
        "front", functools.partial(front_kernel, groups, steps), table,
        [
            (master, (capacity, width), lambda b, i: (0, 0)),
            (neighbours, (1, entries, TILE), lambda b, i: (b, 0, i)),
            (features, (1, nodes, width), lambda b, i: (b, 0, 0)),
        ],
        [
            ((MB, nodes, nodes), BF16, (1, nodes, TILE), lambda b, i: (b, 0, i), pltpu.HBM),
            ((MB, nodes, LANES), F32, (1, TILE, LANES), lambda b, i: (b, i, 0), pltpu.VMEM),
            ((MB, nodes, width), BF16, (1, TILE, width), lambda b, i: (b, i, 0), pltpu.VMEM),
            ((groups, capacity, width), BF16, None, None),
        ],
        grid=(MB, nodes // TILE), after=after, barrier=FRONT_ID, vmem=20,
        scratch=[
            pltpu.VMEM((capacity, width), BF16),
            pltpu.SemaphoreType.DMA,
            pltpu.SemaphoreType.DMA((2, hops, HALVES)),
            pltpu.SemaphoreType.DMA((2, hops, HALVES)),
            pltpu.SemaphoreType.DMA((1 + 2 * hops, HALVES)),
            pltpu.SemaphoreType.DMA((1 + 2 * hops, HALVES)),
        ],
    )


def greet_mate(mate):
    barrier = pltpu.get_barrier_semaphore()
    pl.semaphore_signal(barrier, inc=1, device_id={"col": mate}, device_id_type=pl.DeviceIdType.MESH)
    pl.semaphore_wait(barrier, 1)


def place_kernel(groups, table_ref, slots_ref, weight_ref, mate_ref, rows_ref):
    owner = pl.program_id(0)

    @pl.when(owner == 0)
    def _():
        rows_ref[...] = jnp.zeros_like(rows_ref)

    put_rows(rows_ref, table_ref[STARTS + owner], slots_ref[0].astype(F32))

    @pl.when(owner == groups - 1)
    def _():
        width = weight_ref.shape[2]
        for block in range(weight_ref.shape[0]):
            source = pl.multiple_of((table_ref[COLUMN] ^ block) * width, width)
            rows = rows_ref[pl.ds(source, width), :].astype(BF16)
            weight_ref[block] = rows
            if block % 2:
                mate_ref[block // 2] = rows


def place(table, slots, after=()):
    groups, capacity, width = slots.shape
    blocks = D // width
    return launch(
        "place", functools.partial(place_kernel, groups), table,
        [(slots, (1, capacity, width), lambda i: (i, 0, 0))],
        [
            ((blocks, width, width), BF16, (blocks, width, width), lambda i: (0, 0, 0), pltpu.VMEM),
            ((blocks // 2, width, width), BF16, (blocks // 2, width, width), lambda i: (0, 0, 0), pltpu.VMEM),
        ],
        grid=(groups,), after=after, vmem=24, scratch=[pltpu.VMEM((D + capacity + SUBLANES, width), F32)],
    )


def batch_kernel(m, chunks, table_ref, *refs):
    matrix_hbm, scale_hbm, far_hbm, here_hbm, weight_hbm, for_mate_hbm, grad_hbm, bias_ref = refs[:8]
    refs = refs[8:]
    total_hbm, bias_sum_in = refs[:2] if m else (None, None)
    refs = refs[2:] if m else refs
    out_hbm, pre_hbm, mate_pre_hbm, mate_weight_hbm = refs[:4]
    away_hbm, refs = refs[4 : 4 + chunks], refs[4 + chunks :]
    ended = m == MB - 1
    results, refs = (refs[:2], refs[2:]) if ended else (refs[:1], refs[1:])
    bias_sum_ref, refs = refs[0], refs[1:]
    (
        matrix_ref, scale_ref, far_ref, mixed_ref, weight_ref, mate_weight_ref, grad_ref, out_ref, pre_ref, mate_pre_ref,
        away_ref, total_ref, load, store, send, receive,
    ) = refs[:16]
    parts = refs[16:]
    nodes, width = far_ref.shape
    wide, narrow = nodes // WIDE, nodes // TILE
    mate = partner(lax.axis_index("col"), 1)

    def at(index, size):
        return pl.ds(pl.multiple_of(index * size, size), size)

    def matrix_load(i):
        return pltpu.make_async_copy(
            matrix_hbm.at[m, :, at(i, WIDE)], matrix_ref.at[:, at(i, WIDE)], load.at[i]
        )

    loads = [
        pltpu.make_async_copy(source, target, load.at[wide + i])
        for i, (source, target) in enumerate(
            [
                (far_hbm, far_ref),
                (scale_hbm.at[m], scale_ref),
                (weight_hbm, weight_ref),
                (here_hbm.at[m], mixed_ref.at[0]),
                (grad_hbm.at[m], grad_ref),
            ]
            + ([(total_hbm, total_ref)] if m else [])
        )
    ]
    started = []

    def save(source, target):
        started.append(pltpu.make_async_copy(source, target, store.at[len(started)]))
        started[-1].start()

    def remote(source, target, number):
        return pltpu.make_async_remote_copy(
            src_ref=source,
            dst_ref=target,
            send_sem=send.at[number],
            recv_sem=receive.at[number],
            device_id={"col": mate},
            device_id_type=pl.DeviceIdType.MESH,
        )

    here_copy = remote(here_hbm.at[m], mixed_ref.at[1], 0)
    weight_copy = remote(for_mate_hbm, mate_weight_ref, 1)

    def there_copy(i):
        return remote(mixed_ref.at[2, at(i, WIDE)], mixed_ref.at[3, at(i, WIDE)], 2 + i)

    def pre_copy(i):
        return remote(pre_ref.at[at(i, TILE)], mate_pre_ref.at[at(i, TILE)], 2 + wide + i)

    loads[0].start()
    matrix_load(0).start()
    loads[1].start()
    for i in range(1, wide):
        matrix_load(i).start()
    for item in loads[2:]:
        item.start()
    greet_mate(mate)
    here_copy.start()
    loads[0].wait()
    loads[1].wait()

    @pl.loop(0, wide)
    def _(i):
        matrix_load(i).wait()
        rows = at(i, WIDE)
        there = product_rows(matrix_ref[:, rows], far_ref[...])
        mixed_ref[2, rows, :] = scaled(there, scale_ref[rows, :]).astype(BF16)
        there_copy(i).start()

    weight_copy.start()
    for item in loads[2:5]:
        item.wait()
    here_copy.wait_recv()
    bias_sum_ref[...] = bias_sum_in[...] if m else jnp.zeros_like(bias_sum_ref)
    for i in range(wide):
        there_copy(i).wait_recv()

    @pl.loop(0, narrow, unroll=UNROLL)
    def _(i):
        rows = at(i, TILE)
        preact = bias_ref[...]
        for block in range(4):
            preact = preact + product(mixed_ref[block, rows, :], weight_ref[block])
        row_ids = i * TILE + lax.broadcasted_iota(jnp.int32, preact.shape, 0)
        live = row_ids < table_ref[LIMITS + m]
        gate = jax.nn.sigmoid(preact)
        out_ref[rows, :] = jnp.where(live, preact * gate, 0.0).astype(BF16)
        slope = gate * (1.0 + preact * (1.0 - gate))
        grad_pre = jnp.where(live, grad_ref[rows, :].astype(F32) * slope, 0.0).astype(BF16)
        pre_ref[rows, :] = grad_pre
        pre_copy(i).start()
        bias_sum_ref[...] += jnp.sum(grad_pre.astype(F32), axis=0, keepdims=True)

    save(pre_ref, pre_hbm)
    save(out_ref, out_hbm)
    if m:
        loads[5].wait()

    @pl.loop(0, 4)
    def _(block):
        term = product_rows(mixed_ref[block], pre_ref[...])
        total_ref[block] = total_ref[block] + term if m else term

    if ended:
        half = width // 2
        upper = lax.axis_index("clus") % 2 == 1
        column = lax.axis_index("col")
        for block in range(4):
            source = partner(column, 1) if block % 2 else column
            source = partner(source, 2) if block >= 2 else source
            rows = at(source, width)
            low, high = total_ref[block, :, :half], total_ref[block, :, half:]
            parts[0][rows, :] = jnp.where(upper, high, low)
            parts[1][rows, :] = jnp.where(upper, low, high).astype(BF16)
        for part, result in zip(parts, results):
            save(part, result)
    else:
        save(total_ref, results[0])

    weight_copy.wait_recv()
    for i in range(narrow):
        pre_copy(i).wait_recv()
    step = width // chunks
    for i in range(wide):
        rows = slice(i * WIDE, (i + 1) * WIDE)
        away = product_back(pre_ref[rows, :], weight_ref[2]) + product_back(mate_pre_ref[rows, :], mate_weight_ref[1])
        away_ref[rows, :] = away.astype(BF16)
        for chunk in range(chunks):
            columns = slice(chunk * step, (chunk + 1) * step)
            save(away_ref.at[rows, columns], away_hbm[chunk].at[rows])
    save(mate_pre_ref, mate_pre_hbm)
    save(mate_weight_ref, mate_weight_hbm)
    here_copy.wait_send()
    weight_copy.wait_send()
    for i in range(wide):
        there_copy(i).wait_send()
    for i in range(narrow):
        pre_copy(i).wait_send()
    for item in started:
        item.wait()


def batch(table, m, matrix, scale, far, here, weight, for_mate, out_grad, bias, total, bias_sum, chunks, after=()):
    nodes, width = far.array.shape
    wide, narrow = nodes // WIDE, nodes // TILE
    flat = lambda i: (0, 0)
    ended = m == MB - 1
    parts = [((D, width // 2), F32), ((D, width // 2), BF16)] if ended else []
    results = [(*part, None, None) for part in parts]
    if not ended:
        results = [((4, width, width), F32, None, None)]
    return launch(
        f"batch{m}", functools.partial(batch_kernel, m, chunks), table,
        [(array, None, None) for array in (matrix, scale, far, here, weight, for_mate, out_grad)]
        + [(bias, (1, width), flat)]
        + ([(total, None, None), (bias_sum, (1, width), flat)] if m else []),
        [((nodes, width), BF16, None, None)] * 3
        + [(for_mate.array.shape, BF16, None, None)]
        + [((nodes, width // chunks), BF16, None, None)] * chunks
        + results
        + [((1, width), F32, (1, width), flat)],
        after=after, barrier=BATCH_ID + m, vmem=34,
        scratch=[
            pltpu.VMEM((nodes, nodes), BF16),
            pltpu.VMEM((nodes, LANES), F32),
            pltpu.VMEM((nodes, width), BF16),
            pltpu.VMEM((4, nodes, width), BF16),
            pltpu.VMEM(weight.array.shape, BF16),
            pltpu.VMEM(for_mate.array.shape, BF16),
            pltpu.VMEM((nodes, width), BF16),
            pltpu.VMEM((nodes, width), BF16),
            pltpu.VMEM((nodes, width), BF16),
            pltpu.VMEM((nodes, width), BF16),
            pltpu.VMEM((nodes, width), BF16),
            pltpu.VMEM((4, width, width), F32),
            pltpu.SemaphoreType.DMA((wide + 6,)),
            pltpu.SemaphoreType.DMA((6 + wide * chunks,)),
            pltpu.SemaphoreType.DMA((2 + wide + narrow,)),
            pltpu.SemaphoreType.DMA((2 + wide + narrow,)),
        ]
        + [pltpu.VMEM(*part) for part in parts],
    )


def scatter_job(m, columns, own_hbm, got_hbm, scale_hbm, matrix_hbm, grads_hbm, scratch, semaphores):
    own_ref, got_ref, scale_ref, matrix_ref, sum_ref, grad_ref = scratch
    steps = matrix_ref.shape[0] // WIDE
    loads = [
        pltpu.make_async_copy(source, target, semaphores.at[i])
        for i, (source, target) in enumerate(
            [(own_hbm.at[m, :, columns], own_ref), (got_hbm, got_ref), (scale_hbm.at[m], scale_ref)]
        )
    ]
    tiles, stores = [], []
    for i in range(steps):
        rows = pl.ds(i * WIDE, WIDE)
        tiles.append(pltpu.make_async_copy(matrix_hbm.at[m, rows], matrix_ref.at[rows], semaphores.at[3 + i]))
        stores.append(
            pltpu.make_async_copy(grad_ref.at[rows], grads_hbm.at[m, rows, columns], semaphores.at[3 + steps + i])
        )

    def work():
        for item in loads:
            item.wait()
        grad_mixed = (own_ref[...] + got_ref[...].astype(F32)).astype(BF16)
        sum_ref[...] = scaled(grad_mixed.astype(F32), scale_ref[...]).astype(BF16)
        for i in range(steps):
            tiles[i].wait()
            rows = slice(i * WIDE, (i + 1) * WIDE)
            grad_ref[rows, :] = product(matrix_ref[rows, :], sum_ref[...]).astype(BF16)
            stores[i].start()

    return loads + tiles, work, stores


def scatter_scratch(nodes, width):
    return [
        pltpu.VMEM((nodes, width), F32),
        pltpu.VMEM((nodes, width), BF16),
        pltpu.VMEM((nodes, LANES), F32),
        pltpu.VMEM((nodes, nodes), BF16),
        pltpu.VMEM((nodes, width), BF16),
        pltpu.VMEM((nodes, width), BF16),
        pltpu.SemaphoreType.DMA((3 + 2 * (nodes // WIDE),)),
    ]


def scatter_kernel(m, chunk, own_hbm, got_hbm, scale_hbm, matrix_hbm, grads_hbm, *refs):
    width = got_hbm.shape[1]
    loads, work, stores = scatter_job(
        m, pl.ds(chunk * width, width), own_hbm, got_hbm, scale_hbm, matrix_hbm, grads_hbm, refs[:6], refs[6]
    )
    for item in loads:
        item.start()
    work()
    for item in stores:
        item.wait()


def scatter(m, chunk, own, got, scale, matrix, grads, after=()):
    _, nodes, width = own.shape
    return launch(
        f"scatter{m}_{chunk}", functools.partial(scatter_kernel, m, chunk), None,
        [(array, None, None) for array in (own, got, scale, matrix)],
        [((MB, nodes, width), BF16, None, None)],
        after=after, alias=(grads, 0), scratch=scatter_scratch(nodes, got.array.shape[1]),
    )[0]


def sum_kernel(groups, capacity, table_ref, *refs):
    keep_hbm, sent_hbm, bias_ref, weight_hbm, mate_weight_hbm = refs[:5]
    pre_hbm, mate_hbm, refs = refs[5 : 5 + MB], refs[5 + MB : 5 + 2 * MB], refs[5 + 2 * MB :]
    own_ref, got_ref, bias_out_ref, back_hbm, refs = *refs[:4], refs[4:]
    pre_ref, mate_ref, weights_ref, back_ref, load, store, refs = *refs[:6], refs[6:]
    keep_ref, pair_ref, land_ref, out_ref, total_ref, end_out_ref, end_in_ref, row_ref = refs[:8]
    pair_send, pair_receive, line_send, line_receive, row_send, row_receive = refs[8:]
    own = lax.axis_index("clus")
    place, pairs = own // 2, groups // 2
    other = partner(own, 1)
    rows = keep_ref.shape[0]
    size = rows // CHUNKS
    ahead, behind = place + 1 < pairs, place >= 1

    def remote(source, target, sent, received, device):
        return pltpu.make_async_remote_copy(
            src_ref=source,
            dst_ref=target,
            send_sem=sent,
            recv_sem=received,
            device_id={"clus": device},
            device_id_type=pl.DeviceIdType.MESH,
        )

    def part(chunk):
        return pl.ds(pl.multiple_of(chunk * size, size), size)

    def pair_copy(chunk):
        return remote(
            sent_hbm.at[part(chunk)], pair_ref.at[part(chunk)], pair_send.at[chunk], pair_receive.at[chunk], other
        )

    def line_copy(direction, chunk):
        return remote(
            out_ref.at[direction, part(chunk)], land_ref.at[direction, part(chunk)],
            line_send.at[direction, chunk], line_receive.at[direction, chunk],
            own + 2 if direction == 0 else own - 2,
        )

    def row_copy(number):
        device = (other, own + 2, own - 2)[number]
        return remote(row_ref.at[number], row_ref.at[3 + number], row_send.at[number], row_receive.at[number], device)

    end_copy = remote(end_out_ref, end_in_ref, pair_send.at[CHUNKS], pair_receive.at[CHUNKS], other)

    nodes = pre_ref.shape[1]
    tiles = nodes // WIDE
    loads = [
        pltpu.make_async_copy(source, target, load.at[i])
        for i, (source, target) in enumerate(
            [(keep_hbm, keep_ref), (weight_hbm.at[0], weights_ref.at[0]), (mate_weight_hbm.at[0], weights_ref.at[1])]
            + [(source, pre_ref.at[m]) for m, source in enumerate(pre_hbm)]
            + [(source, mate_ref.at[m]) for m, source in enumerate(mate_hbm)]
        )
    ]
    stores = [pltpu.make_async_copy(back_ref.at[m], back_hbm.at[m], store.at[m]) for m in range(MB)]

    def back(number):
        m, i = number // tiles, number % tiles
        if i == 0:
            loads[3 + m].wait()
            loads[3 + MB + m].wait()
        down = slice(i * WIDE, (i + 1) * WIDE)
        back_ref[m, down, :] = product_back(pre_ref[m, down, :], weights_ref[0]) + product_back(
            mate_ref[m, down, :], weights_ref[1]
        )
        if i == tiles - 1:
            stores[m].start()

    land_ref[...] = jnp.zeros_like(land_ref)
    row_ref[...] = jnp.zeros_like(row_ref)
    row_ref[0] = bias_ref[...]
    for item in loads:
        item.start()
    barrier = pltpu.get_barrier_semaphore()

    def greet(index):
        pl.semaphore_signal(barrier, inc=1, device_id={"clus": index}, device_id_type=pl.DeviceIdType.MESH)

    greet(other)

    @pl.when(ahead)
    def _():
        greet(own + 2)

    @pl.when(behind)
    def _():
        greet(own - 2)

    pl.semaphore_wait(barrier, 1 + jnp.where(ahead, 1, 0) + jnp.where(behind, 1, 0))
    row_copy(0).start()
    for chunk in range(CHUNKS):
        pair_copy(chunk).start()
    for item in loads[:3]:
        item.wait()

    def pass_on(direction, chunk, first):
        sums = keep_ref[part(chunk), :]
        if not first:
            sums = sums + land_ref[direction, part(chunk), :].astype(F32)
        out_ref[direction, part(chunk), :] = sums.astype(BF16)
        line_copy(direction, chunk).start()

    def pass_row(direction, first):
        row_ref[1 + direction] = row_ref[0] if first else row_ref[0] + row_ref[4 + direction]
        row_copy(1 + direction).start()

    steps = CHUNKS + pairs - 1
    for step in range(steps):
        if step < CHUNKS:
            pair_copy(step).wait_recv()
            keep_ref[part(step), :] += pair_ref[part(step), :].astype(F32)
            if step == 0:
                row_copy(0).wait()
                row_ref[0] += row_ref[3]
            for direction, (here, there) in enumerate(((behind, ahead), (ahead, behind))):

                @pl.when(jnp.logical_not(here) & there)
                def _(direction=direction, step=step):
                    pass_on(direction, step, True)
                    if step == 0:
                        pass_row(direction, True)

        for direction, (here, there) in enumerate(((behind, ahead), (ahead, behind))):
            chunk = step - (place if direction == 0 else pairs - 1 - place)

            @pl.when(here & (chunk >= 0) & (chunk < CHUNKS))
            def _(direction=direction, chunk=chunk, there=there):
                line_copy(direction, chunk).wait_recv()

                @pl.when(there)
                def _():
                    pass_on(direction, chunk, False)

                @pl.when(chunk == 0)
                def _():
                    row_copy(1 + direction).wait_recv()

                    @pl.when(there)
                    def _():
                        pass_row(direction, False)

        for number in range(step * MB * tiles // steps, (step + 1) * MB * tiles // steps):
            back(number)

    total_ref[:rows, :] = keep_ref[...] + (land_ref[0].astype(F32) + land_ref[1].astype(F32))
    total_ref[rows:, :] = jnp.zeros((capacity + SUBLANES, keep_ref.shape[1]), F32)
    end_out_ref[...] = take_rows(total_ref, table_ref[STARTS + other], capacity, rows - 1).astype(BF16)
    end_copy.start()
    own_ref[...] = take_rows(total_ref, table_ref[STARTS + own], capacity, rows - 1)
    bias_out_ref[...] = row_ref[0] + (row_ref[4] + row_ref[5])
    end_copy.wait()
    got_ref[...] = end_in_ref[...]
    for chunk in range(CHUNKS):
        pair_copy(chunk).wait_send()
    for direction, there in enumerate((ahead, behind)):

        @pl.when(there)
        def _(direction=direction):
            row_copy(1 + direction).wait_send()
            for chunk in range(CHUNKS):
                line_copy(direction, chunk).wait_send()

    for item in stores:
        item.wait()


def sum_over_owners(table, groups, capacity, keep, sent, bias, weight, mate_weight, pres, mates, after=()):
    rows, half = keep.shape
    nodes, width = pres[0].shape
    flat = lambda i: (0, 0)
    shape = (capacity, half)
    return launch(
        "sum", functools.partial(sum_kernel, groups, capacity), table,
        [(array, None, None) for array in (keep, sent)]
        + [(bias, bias.shape, flat)]
        + [(array, None, None) for array in (weight, mate_weight, *pres, *mates)],
        [
            (shape, F32, shape, flat),
            (shape, BF16, shape, flat),
            (bias.shape, F32, bias.shape, flat),
            ((MB, nodes, width), F32, None, None),
        ],
        after=after, barrier=SUM_ID, vmem=38,
        scratch=[
            pltpu.VMEM((MB, nodes, width), BF16),
            pltpu.VMEM((MB, nodes, width), BF16),
            pltpu.VMEM((2, width, width), BF16),
            pltpu.VMEM((MB, nodes, width), F32),
            pltpu.SemaphoreType.DMA((3 + 2 * MB,)),
            pltpu.SemaphoreType.DMA((MB,)),
            pltpu.VMEM((rows, half), F32),
            pltpu.VMEM((rows, half), BF16),
            pltpu.VMEM((2, rows, half), BF16),
            pltpu.VMEM((2, rows, half), BF16),
            pltpu.VMEM((rows + capacity + SUBLANES, half), F32),
            pltpu.VMEM(shape, BF16),
            pltpu.VMEM(shape, BF16),
            pltpu.VMEM((6, 1, width), F32),
            pltpu.SemaphoreType.DMA((CHUNKS + 1,)),
            pltpu.SemaphoreType.DMA((CHUNKS + 1,)),
            pltpu.SemaphoreType.DMA((2, CHUNKS)),
            pltpu.SemaphoreType.DMA((2, CHUNKS)),
            pltpu.SemaphoreType.DMA((3,)),
            pltpu.SemaphoreType.DMA((3,)),
        ],
    )


def adamw_update(current, first_moment, second_moment, gradient, step_rate):
    first_new = BETA_ONE * first_moment + (1.0 - BETA_ONE) * gradient
    second_new = BETA_TWO * second_moment + (1.0 - BETA_TWO) * gradient * gradient
    fixed_first = first_new / (1.0 - BETA_ONE**STEP)
    fixed_second = second_new / (1.0 - BETA_TWO**STEP)
    updated = current - step_rate * (
        fixed_first / (jnp.sqrt(fixed_second) + EPSILON) + DECAY * current
    )
    return (updated, first_new, second_new)


def finish_kernel(groups, table_ref, *refs):
    done = MB - 1
    own_ref, got_ref, bias_grad_ref, biases = refs[0], refs[1], refs[2], refs[3:6]
    weights_hbm, out_parts, refs = refs[6:9], refs[9 : 9 + MB], refs[9 + MB :]
    back_hbm, gots, (scale_hbm, matrix_hbm), refs = refs[0], refs[1 : 1 + done], refs[1 + done : 3 + done], refs[3 + done :]
    updated_hbm, bias_outs, (out_hbm, grads_hbm), refs = refs[:3], refs[3:6], refs[6:8], refs[8:]
    weights, buffers, (weight_load, weight_store, load, store), refs = refs[:3], refs[3], refs[4:8], refs[8:]
    jobs = [
        scatter_job(
            m, pl.ds(0, back_hbm.shape[2]), back_hbm, gots[m], scale_hbm, matrix_hbm, grads_hbm,
            refs[7 * m : 7 * m + 6], refs[7 * m + 6],
        )
        for m in range(done)
    ]
    weight_loads = [
        pltpu.make_async_copy(source, target, weight_load.at[i])
        for i, (source, target) in enumerate(zip(weights_hbm, weights))
    ]
    weight_stores = [
        pltpu.make_async_copy(source, target, weight_store.at[i])
        for i, (source, target) in enumerate(zip(weights, updated_hbm))
    ]
    out_loads, out_stores = relay(
        out_parts, [out_hbm.at[m] for m in range(MB)], [buffers.at[m] for m in range(MB)], load, store
    )
    for item in jobs[0][0] + weight_loads:
        item.start()
    for later, _, _ in jobs[1:]:
        for item in later:
            item.start()
    for item in out_loads:
        item.start()
    jobs[0][1]()

    for item in weight_loads:
        item.wait()
    rows, width = weights[0].shape
    half = width // 2
    strip = min(rows, TILE // 2)
    own = table_ref[GROUP]
    for first in range(0, rows, strip):
        row_ids = first + lax.broadcasted_iota(jnp.int32, (strip, half), 0)
        used = row_ids < table_ref[STARTS + groups + own]
        down = slice(first, first + strip)
        for side in range(2):
            mine = (own & 1) == side
            here, there = own_ref[down, :], got_ref[down, :].astype(F32)
            columns = slice(side * half, (side + 1) * half)
            results = adamw_update(*(ref[down, columns] for ref in weights), jnp.where(mine, here, there), RATE_WEIGHT)
            for ref, result in zip(weights, results):
                ref[down, columns] = jnp.where(used, result, 0.0)
    for item in weight_stores:
        item.start()
    results = adamw_update(*(ref[...] for ref in biases), bias_grad_ref[...], RATE_BIAS)
    for ref, result in zip(bias_outs, results):
        ref[...] = result

    for _, work, _ in jobs[1:]:
        work()
    for item, onward in zip(out_loads, out_stores):
        item.wait()
        onward.start()
    for item in weight_stores + out_stores:
        item.wait()
    for _, _, stores in jobs:
        for item in stores:
            item.wait()


def finish(table, groups, mine, other, bias_grad, biases, weights, outputs, backs, gots, scale, matrix, after=()):
    capacity, width = weights[0].shape
    nodes = outputs[0].shape[0]
    fixed = lambda i: (0, 0)
    scratch = [pltpu.VMEM((capacity, width), F32)] * 3 + [
        pltpu.VMEM((MB, nodes, width), BF16),
        pltpu.SemaphoreType.DMA((3,)),
        pltpu.SemaphoreType.DMA((3,)),
        pltpu.SemaphoreType.DMA((MB * PIECES,)),
        pltpu.SemaphoreType.DMA((MB * PIECES,)),
    ]
    for _ in gots:
        scratch += scatter_scratch(nodes, width)
    return launch(
        "finish", functools.partial(finish_kernel, groups), table,
        [(array, array.shape, fixed) for array in (mine, other)]
        + [(array, (1, width), fixed) for array in (bias_grad, *biases)]
        + [(array, None, None) for array in (*weights, *outputs, backs, *gots, scale, matrix)],
        [((capacity, width), F32, None, None)] * 3
        + [((1, width), F32, (1, width), fixed)] * 3
        + [((MB, nodes, width), BF16, None, None)] * 2,
        after=after, scratch=scratch, vmem=35,
    )


def shards(
    features,
    neighbours,
    node_counts,
    row_counts,
    master_weight,
    weight_first,
    weight_second,
    master_bias,
    bias_first,
    bias_second,
    out_grad,
):
    groups = lax.axis_size("clus")
    capacity, width = master_weight.shape
    owner_ids = jnp.arange(groups, dtype=jnp.int32)
    starts = jnp.sum(jnp.where(owner_ids[None, :] < owner_ids[:, None], row_counts[None, :], 0), axis=1)
    table = jnp.concatenate(
        [
            jnp.stack([lax.axis_index("clus"), lax.axis_index("col")]).astype(jnp.int32),
            node_counts[:, 0],
            starts.astype(jnp.int32),
            row_counts,
        ]
    )
    bias_row, bias_first_row, bias_second_row = (
        array.reshape(1, width) for array in (master_bias, bias_first, bias_second)
    )

    picked = pick(features, (0,))
    picked = picked + pick(features, tuple(range(1, MB)), picked)
    far = [Kept(flip(array, "col", 2), None) for array in picked]

    matrix, *kept, slots = front(table, groups, master_weight, jnp.swapaxes(neighbours, 1, 2), features, [picked[-1]])
    scale, here = (Kept(array) for array in kept)
    weight, for_mate = (Kept(array) for array in place(table, slots))
    last = for_mate
    total, bias_sum = None, None
    outputs, pres, mates, away = [], [], [], []
    for m in range(MB):
        chunks = 2 if m == MB - 1 else 1
        out_m, pre_m, mate_m, mate_weight, *rest = batch(
            table, m, matrix, scale, far[m], here, weight, for_mate, out_grad, bias_row, total, bias_sum, chunks,
            [last],
        )
        outputs.append(out_m)
        pres.append(pre_m)
        mates.append(mate_m)
        away.append([Kept(flip(chunk, "col", 2), None) for chunk in rest[:chunks]])
        total, bias_sum = rest[chunks], rest[-1]
        last = bias_sum

    keep, sent, bias_sum = rest[chunks:]
    mine, other, bias_total, backs = sum_over_owners(
        table, groups, capacity, keep, sent, bias_sum, weight, mate_weight, pres, mates, [last]
    )
    *updated, outputs, input_grads = finish(
        table, groups, mine, other, bias_total, (bias_row, bias_first_row, bias_second_row),
        (master_weight, weight_first, weight_second), outputs, backs, [part[0] for part in away[:-1]],
        scale, matrix, [bias_total],
    )
    for chunk, got in enumerate(away[-1]):
        input_grads = scatter(MB - 1, chunk, backs, got, scale, matrix, input_grads)
    return (outputs, input_grads, *updated[:3], *(row.reshape(width) for row in updated[3:]))


def solution(mesh):
    in_specs = (
        P(None, "clus", "col"),
        P(None, "clus", None),
        P(None, "clus"),
        P(),
        P("clus", "col"),
        P("clus", "col"),
        P("clus", "col"),
        P("col"),
        P("col"),
        P("col"),
        P(None, "clus", "col"),
    )
    out_specs = (
        P(None, "clus", "col"),
        P(None, "clus", "col"),
        P("clus", "col"),
        P("clus", "col"),
        P("clus", "col"),
        P("col"),
        P("col"),
        P("col"),
    )
    return jax.shard_map(shards, mesh=mesh, in_specs=in_specs, out_specs=out_specs, check_vma=False)
```

```python
import functools

import jax
import jax.numpy as jnp
from jax import lax
from jax.experimental import pallas as pl
from jax.experimental.pallas import tpu as pltpu
from jax.sharding import PartitionSpec as P

D = 2048
MB = 3
STEP = 10

BETA_ONE = 0.9
BETA_TWO = 0.95
EPSILON = 1e-08
DECAY = 0.1
RATE_WEIGHT = 0.06
RATE_BIAS = 0.6

LANES = 128
DIGIT_BITS = 5
DIGITS = 6
STRIP = 32
SUBLANES = 8
TILE = 256
WIDE = 512
HALVES = 2
PIECES = 4
UNROLL = 3
CHUNKS = 8
MIB = 1024 * 1024
SMALL = 1 << 16

GROUP, COLUMN, LIMITS = 0, 1, 2
STARTS = LIMITS + MB

FRONT_ID, SUM_ID, BATCH_ID = 1, 2, 3

F32, BF16 = jnp.float32, jnp.bfloat16


class Kept:
    def __init__(self, array, space=pltpu.VMEM):
        self.array, self.space = array, space


def located(item):
    if isinstance(item, Kept):
        return pltpu.with_memory_space_constraint(item.array, item.space) if item.space else item.array
    return pltpu.with_memory_space_constraint(item, pltpu.HBM) if item.size > SMALL else item


def launch(name, body, table, ins, outs, grid=(1,), after=(), alias=None, scratch=(), barrier=None, vmem=16):
    tables = [] if table is None else [table]

    def spec(block, index):
        if block is None:
            return pl.BlockSpec(memory_space=pl.ANY)
        return pl.BlockSpec(block, lambda *a: index(*a[: len(grid)]))

    unread = ([alias[0]] if alias else []) + [array for array in after if alias is None or array is not alias[0]]

    def kernel(*refs):
        table_refs, refs = refs[: len(tables)], refs[len(tables) :]
        body(*table_refs, *refs[: len(ins)], *refs[len(ins) + len(unread) :])

    return pl.pallas_call(
        kernel,
        grid_spec=pltpu.PrefetchScalarGridSpec(
            num_scalar_prefetch=len(tables),
            grid=grid,
            in_specs=[spec(block, index) for _, block, index in ins]
            + [pl.BlockSpec(memory_space=pl.ANY)] * len(unread),
            out_specs=[spec(out[2], out[3]) for out in outs],
            scratch_shapes=list(scratch),
        ),
        out_shape=[
            (out[4] if len(out) > 4 else pltpu.HBM if out[2] is None else jax.ShapeDtypeStruct)(out[0], out[1])
            for out in outs
        ],
        input_output_aliases={len(tables) + len(ins): alias[1]} if alias else {},
        compiler_params=pltpu.CompilerParams(
            vmem_limit_bytes=vmem * MIB, collective_id=barrier, has_side_effects=barrier is not None
        ),
        cost_estimate=pl.CostEstimate(flops=1, bytes_accessed=1, transcendentals=0),
        name=name,
    )(*tables, *(located(item[0]) for item in ins), *(located(item) for item in unread))


def flip(values, axis, bit):
    size = lax.axis_size(axis)
    return lax.ppermute(values, axis, [(i, i ^ bit) for i in range(size)])


def partner(index, bit):
    return index + bit * (1 - 2 * ((index // bit) % 2))


def product(left, right):
    return jnp.dot(left, right, preferred_element_type=F32)


def product_back(left, right):
    return lax.dot_general(left, right, (((1,), (1,)), ((), ())), preferred_element_type=F32)


def product_rows(left, right):
    return lax.dot_general(left, right, (((0,), (0,)), ((), ())), preferred_element_type=F32)


def scaled(values, scale):
    return values * jnp.concatenate([scale] * (values.shape[1] // LANES), axis=1)


def put_rows(ref, first, rows):
    base = pl.multiple_of((first // SUBLANES) * SUBLANES, SUBLANES)
    offset = first - base
    moved = jnp.concatenate([rows, jnp.zeros((SUBLANES, rows.shape[1]), rows.dtype)], axis=0)
    wanted = jnp.broadcast_to(offset, moved.shape)
    for bit in (1, 2, 4):
        moved = jnp.where((wanted & bit) != 0, pltpu.roll(moved, bit, 0), moved)
    head = ref[pl.ds(base, SUBLANES), :]
    row_ids = lax.broadcasted_iota(jnp.int32, head.shape, 0)
    ref[pl.ds(base, SUBLANES), :] = jnp.where(row_ids < offset, head, moved[:SUBLANES])
    ref[pl.ds(pl.multiple_of(base + SUBLANES, SUBLANES), rows.shape[0]), :] = moved[SUBLANES:]


def take_rows(ref, first, count, largest):
    bit = 1 << (largest.bit_length() - 1)
    rows = ref[...]
    while bit:
        length = count + max(bit, SUBLANES)
        if bit >= SUBLANES:
            moved = rows[bit : bit + length]
            missing = length - moved.shape[0]
            if missing:
                moved = jnp.concatenate([moved, jnp.zeros((missing, rows.shape[1]), rows.dtype)], axis=0)
        else:
            moved = pltpu.roll(rows, length - bit, 0)
        chosen = (jnp.broadcast_to(first, (length, rows.shape[1])) & bit) != 0
        rows = jnp.where(chosen, moved, rows[:length])
        bit //= 2
    return rows[:count]


def relay(sources, targets, buffers, load, store):
    def piece(ref, i):
        rows = ref.shape[0] // PIECES
        return ref.at[pl.ds(i * rows, rows)]

    loads, stores = [], []
    for number, (source, target, buffer) in enumerate(zip(sources, targets, buffers)):
        for i in range(PIECES):
            place = number * PIECES + i
            loads.append(pltpu.make_async_copy(piece(source, i), piece(buffer, i), load.at[place]))
            stores.append(pltpu.make_async_copy(piece(buffer, i), piece(target, i), store.at[place]))
    return loads, stores


def pick_kernel(batches, source_ref, *refs):
    targets, (buffer_ref, load, store) = refs[:-3], refs[-3:]
    loads, stores = relay(
        [source_ref.at[m] for m in batches], targets, [buffer_ref.at[i] for i in range(len(batches))], load, store
    )
    for item in loads:
        item.start()
    for item, onward in zip(loads, stores):
        item.wait()
        onward.start()
    for item in stores:
        item.wait()


def pick(stacked, batches, after=()):
    count = len(batches)
    return launch(
        f"pick{batches[0]}", functools.partial(pick_kernel, batches), None,
        [(stacked, None, None)], [(stacked.shape[1:], stacked.dtype, None, None)] * count,
        after=after,
        scratch=[
            pltpu.VMEM((count, *stacked.shape[1:]), stacked.dtype),
            pltpu.SemaphoreType.DMA((count * PIECES,)),
            pltpu.SemaphoreType.DMA((count * PIECES,)),
        ],
    )


def count_tile(limit, first, neighbour_ref, matrix_ref, scale_ref, lanes):
    nodes = matrix_ref.shape[1]
    words = -(-(nodes // LANES) // DIGITS)
    entries = neighbour_ref[0, :, lanes]
    node_ids = first + lax.broadcasted_iota(jnp.int32, entries.shape, 1)
    valid = (entries < limit) & (node_ids < limit)
    low = entries & (LANES - 1)
    high = entries >> 7
    digits = []
    for word in range(words):
        inside = valid & (high >= word * DIGITS) & (high < (word + 1) * DIGITS)
        shift = jnp.where(inside, (high - word * DIGITS) * DIGIT_BITS, 0)
        digits.append(jnp.where(inside, jnp.left_shift(1, shift), 0))
    for strip in range(LANES // STRIP):
        row_ids = strip * STRIP + lax.broadcasted_iota(jnp.int32, (STRIP, LANES), 0)
        sums = [jnp.zeros((STRIP, LANES), jnp.int32) for _ in range(words)]
        for entry in range(entries.shape[0]):
            hit = row_ids == low[entry : entry + 1, :]
            for word in range(words):
                sums[word] = sums[word] + jnp.where(hit, digits[word][entry : entry + 1, :], 0)
        for block in range(nodes // LANES):
            word, digit = block // DIGITS, block % DIGITS
            count = jnp.right_shift(sums[word], digit * DIGIT_BITS) & ((1 << DIGIT_BITS) - 1)
            rows = slice(block * LANES + strip * STRIP, block * LANES + (strip + 1) * STRIP)
            matrix_ref[0, rows, lanes] = count.astype(F32).astype(BF16)
    rows = pl.ds(pl.multiple_of(first, LANES), LANES)
    square = matrix_ref[0, rows, lanes].astype(F32)
    on_diagonal = lax.broadcasted_iota(jnp.int32, square.shape, 0) == lax.broadcasted_iota(jnp.int32, square.shape, 1)
    matrix_ref[0, rows, lanes] = jnp.where(on_diagonal, 2.0 * square + 2.0, square).astype(BF16)
    degree = 1.0 + jnp.sum(valid.astype(F32), axis=0, keepdims=True)
    factor = (node_ids[:1] < limit).astype(F32) / degree
    scale_ref[0, lanes, :] = jnp.transpose(jnp.broadcast_to(factor, (LANES, LANES)))


def front_kernel(
    groups, total, table_ref, master_ref, neighbour_ref, feature_ref, matrix_ref, scale_ref, mixed_ref, slots_ref,
    block_ref, local_semaphore, line_send, line_receive, pair_send, pair_receive,
):
    batch, tile_id = pl.program_id(0), pl.program_id(1)
    tiles = pl.num_programs(1)
    step = batch * tiles + tile_id
    own = lax.axis_index("clus")
    place, side = own // 2, own % 2
    pairs = groups // 2
    other = partner(own, 1)

    def rows_of(half):
        size = block_ref.shape[0] // HALVES
        return pl.ds(half * size, size)

    def remote(source, target, sent, received, device):
        return pltpu.make_async_remote_copy(
            src_ref=source,
            dst_ref=target,
            send_sem=sent,
            recv_sem=received,
            device_id={"clus": device},
            device_id_type=pl.DeviceIdType.MESH,
        )

    def origin_of(direction, hop):
        return place - 1 - hop if direction == 0 else place + 1 + hop

    def line_copy(direction, hop, half):
        slot = (place - hop if direction == 0 else place + hop) * 2 + side
        target = slots_ref.at[slot, rows_of(half)]
        return remote(
            block_ref.at[rows_of(half)] if hop == 0 else target, target,
            line_send.at[direction, hop, half], line_receive.at[direction, hop, half],
            own + 2 if direction == 0 else own - 2,
        )

    def sends(direction, hop):
        if direction == 0:
            return (place - hop >= 0) & (place + 1 < pairs)
        return (place + hop < pairs) & (place - 1 >= 0)

    def arrives(direction, hop):
        return place - 1 - hop >= 0 if direction == 0 else place + 1 + hop < pairs

    def arrival(direction, hop, half):
        target = slots_ref.at[origin_of(direction, hop) * 2 + side, rows_of(half)]
        return remote(
            target, target, line_send.at[direction, hop, half], line_receive.at[direction, hop, half], other
        )

    def pair_copy(direction, hop, half):
        slot = own if hop < 0 else origin_of(direction, hop) * 2 + side
        number = 0 if hop < 0 else 1 + 2 * hop + direction
        target = slots_ref.at[slot, rows_of(half)]
        return remote(
            block_ref.at[rows_of(half)] if hop < 0 else target, target,
            pair_send.at[number, half], pair_receive.at[number, half], other,
        )

    def pair_arrival(direction, hop, half):
        slot = other if hop < 0 else origin_of(direction, hop) * 2 + 1 - side
        number = 0 if hop < 0 else 1 + 2 * hop + direction
        target = slots_ref.at[slot, rows_of(half)]
        return remote(target, target, pair_send.at[number, half], pair_receive.at[number, half], other)

    local_copy = pltpu.make_async_copy(block_ref, slots_ref.at[own], local_semaphore)
    hops = pairs - 1

    @pl.when(step == 0)
    def _():
        barrier = pltpu.get_barrier_semaphore()

        def greet(index):
            pl.semaphore_signal(barrier, inc=1, device_id={"clus": index}, device_id_type=pl.DeviceIdType.MESH)

        greet(other)

        @pl.when(place + 1 < pairs)
        def _():
            greet(own + 2)

        @pl.when(place - 1 >= 0)
        def _():
            greet(own - 2)

        pl.semaphore_wait(barrier, 1 + jnp.where(place + 1 < pairs, 1, 0) + jnp.where(place - 1 >= 0, 1, 0))
        block_ref[...] = master_ref[...].astype(BF16)
        for half in range(HALVES):
            for direction in range(2):
                pl.when(sends(direction, 0))(line_copy(direction, 0, half).start)
            pair_copy(0, -1, half).start()
        local_copy.start()

    limit = table_ref[LIMITS + batch]
    tile = mixed_ref.shape[1]
    for part in range(tile // LANES):
        first = tile_id * tile + part * LANES
        count_tile(limit, first, neighbour_ref, matrix_ref, scale_ref, slice(part * LANES, (part + 1) * LANES))
    mixed_ref[0] = scaled(product_rows(matrix_ref[0], feature_ref[0]), scale_ref[0]).astype(BF16)

    for event in range(hops * HALVES):
        hop, half = event // HALVES, event % HALVES

        @pl.when(step == min(total - 1, ((event + 1) * total) // (hops * HALVES)))
        def _(hop=hop, half=half):
            for direction in range(2):

                @pl.when(arrives(direction, hop))
                def _(direction=direction):
                    arrival(direction, hop, half).wait_recv()
                    pair_copy(direction, hop, half).start()

                if hop + 1 < hops:
                    pl.when(sends(direction, hop + 1))(line_copy(direction, hop + 1, half).start)

    @pl.when(step == total - 1)
    def _():
        local_copy.wait()
        for half in range(HALVES):
            pair_copy(0, -1, half).wait_send()
            pair_arrival(0, -1, half).wait_recv()
            for hop in range(hops):
                for direction in range(2):
                    pl.when(sends(direction, hop))(line_copy(direction, hop, half).wait_send)

                    @pl.when(arrives(direction, hop))
                    def _(direction=direction, hop=hop, half=half):
                        pair_copy(direction, hop, half).wait_send()
                        pair_arrival(direction, hop, half).wait_recv()


def front(table, groups, master, neighbours, features, after=()):
    _, entries, nodes = neighbours.shape
    capacity, width = master.shape
    hops = groups // 2 - 1
    steps = MB * (nodes // TILE)
    return launch(
        "front", functools.partial(front_kernel, groups, steps), table,
        [
            (master, (capacity, width), lambda b, i: (0, 0)),
            (neighbours, (1, entries, TILE), lambda b, i: (b, 0, i)),
            (features, (1, nodes, width), lambda b, i: (b, 0, 0)),
        ],
        [
            ((MB, nodes, nodes), BF16, (1, nodes, TILE), lambda b, i: (b, 0, i), pltpu.HBM),
            ((MB, nodes, LANES), F32, (1, TILE, LANES), lambda b, i: (b, i, 0), pltpu.VMEM),
            ((MB, nodes, width), BF16, (1, TILE, width), lambda b, i: (b, i, 0), pltpu.VMEM),
            ((groups, capacity, width), BF16, None, None),
        ],
        grid=(MB, nodes // TILE), after=after, barrier=FRONT_ID, vmem=20,
        scratch=[
            pltpu.VMEM((capacity, width), BF16),
            pltpu.SemaphoreType.DMA,
            pltpu.SemaphoreType.DMA((2, hops, HALVES)),
            pltpu.SemaphoreType.DMA((2, hops, HALVES)),
            pltpu.SemaphoreType.DMA((1 + 2 * hops, HALVES)),
            pltpu.SemaphoreType.DMA((1 + 2 * hops, HALVES)),
        ],
    )


def greet_mate(mate):
    barrier = pltpu.get_barrier_semaphore()
    pl.semaphore_signal(barrier, inc=1, device_id={"col": mate}, device_id_type=pl.DeviceIdType.MESH)
    pl.semaphore_wait(barrier, 1)


def place_kernel(groups, table_ref, slots_ref, weight_ref, mate_ref, rows_ref):
    owner = pl.program_id(0)

    @pl.when(owner == 0)
    def _():
        rows_ref[...] = jnp.zeros_like(rows_ref)

    put_rows(rows_ref, table_ref[STARTS + owner], slots_ref[0].astype(F32))

    @pl.when(owner == groups - 1)
    def _():
        width = weight_ref.shape[2]
        for block in range(weight_ref.shape[0]):
            source = pl.multiple_of((table_ref[COLUMN] ^ block) * width, width)
            rows = rows_ref[pl.ds(source, width), :].astype(BF16)
            weight_ref[block] = rows
            if block % 2:
                mate_ref[block // 2] = rows


def place(table, slots, after=()):
    groups, capacity, width = slots.shape
    blocks = D // width
    return launch(
        "place", functools.partial(place_kernel, groups), table,
        [(slots, (1, capacity, width), lambda i: (i, 0, 0))],
        [
            ((blocks, width, width), BF16, (blocks, width, width), lambda i: (0, 0, 0), pltpu.VMEM),
            ((blocks // 2, width, width), BF16, (blocks // 2, width, width), lambda i: (0, 0, 0), pltpu.VMEM),
        ],
        grid=(groups,), after=after, vmem=24, scratch=[pltpu.VMEM((D + capacity + SUBLANES, width), F32)],
    )


def batch_kernel(m, chunks, table_ref, *refs):
    matrix_hbm, scale_hbm, far_hbm, here_hbm, weight_hbm, for_mate_hbm, grad_hbm, bias_ref = refs[:8]
    refs = refs[8:]
    total_hbm, bias_sum_in = refs[:2] if m else (None, None)
    refs = refs[2:] if m else refs
    ended = m == MB - 1
    out_hbm, pre_hbm, mate_pre_hbm = refs[:3]
    away_hbm, refs = refs[3 : 3 + chunks], refs[3 + chunks :]
    mate_weight_hbm, refs = (refs[0], refs[1:]) if ended else (None, refs)
    results, refs = (refs[:2], refs[2:]) if ended else (refs[:1], refs[1:])
    bias_sum_ref, refs = refs[0], refs[1:]
    (
        matrix_ref, scale_ref, far_ref, mixed_ref, weight_ref, mate_weight_ref, grad_ref, out_ref, pre_ref, mate_pre_ref,
        away_ref, total_ref, load, store, send, receive,
    ) = refs[:16]
    parts = refs[16:]
    nodes, width = far_ref.shape
    wide, narrow = nodes // WIDE, nodes // TILE
    mate = partner(lax.axis_index("col"), 1)

    def at(index, size):
        return pl.ds(pl.multiple_of(index * size, size), size)

    def matrix_load(i):
        return pltpu.make_async_copy(
            matrix_hbm.at[m, :, at(i, WIDE)], matrix_ref.at[:, at(i, WIDE)], load.at[i]
        )

    loads = [
        pltpu.make_async_copy(source, target, load.at[wide + i])
        for i, (source, target) in enumerate(
            [
                (far_hbm, far_ref),
                (scale_hbm.at[m], scale_ref),
                (weight_hbm, weight_ref),
                (here_hbm.at[m], mixed_ref.at[0]),
                (grad_hbm.at[m], grad_ref),
            ]
            + ([(total_hbm, total_ref)] if m else [])
        )
    ]
    started = []

    def save(source, target):
        started.append(pltpu.make_async_copy(source, target, store.at[len(started)]))
        started[-1].start()

    def remote(source, target, number):
        return pltpu.make_async_remote_copy(
            src_ref=source,
            dst_ref=target,
            send_sem=send.at[number],
            recv_sem=receive.at[number],
            device_id={"col": mate},
            device_id_type=pl.DeviceIdType.MESH,
        )

    here_copy = remote(here_hbm.at[m], mixed_ref.at[1], 0)
    weight_copy = remote(for_mate_hbm, mate_weight_ref, 1)

    def there_copy(i):
        return remote(mixed_ref.at[2, at(i, WIDE)], mixed_ref.at[3, at(i, WIDE)], 2 + i)

    def pre_copy(i):
        return remote(pre_ref.at[at(i, TILE)], mate_pre_ref.at[at(i, TILE)], 2 + wide + i)

    loads[0].start()
    matrix_load(0).start()
    loads[1].start()
    for i in range(1, wide):
        matrix_load(i).start()
    for item in loads[2:]:
        item.start()
    greet_mate(mate)
    here_copy.start()
    loads[0].wait()
    loads[1].wait()

    @pl.loop(0, wide)
    def _(i):
        matrix_load(i).wait()
        rows = at(i, WIDE)
        there = product_rows(matrix_ref[:, rows], far_ref[...])
        mixed_ref[2, rows, :] = scaled(there, scale_ref[rows, :]).astype(BF16)
        there_copy(i).start()

    weight_copy.start()
    for item in loads[2:5]:
        item.wait()
    here_copy.wait_recv()
    bias_sum_ref[...] = bias_sum_in[...] if m else jnp.zeros_like(bias_sum_ref)
    for i in range(wide):
        there_copy(i).wait_recv()

    @pl.loop(0, narrow, unroll=UNROLL)
    def _(i):
        rows = at(i, TILE)
        preact = bias_ref[...]
        for block in range(4):
            preact = preact + product(mixed_ref[block, rows, :], weight_ref[block])
        row_ids = i * TILE + lax.broadcasted_iota(jnp.int32, preact.shape, 0)
        live = row_ids < table_ref[LIMITS + m]
        gate = jax.nn.sigmoid(preact)
        out_ref[rows, :] = jnp.where(live, preact * gate, 0.0).astype(BF16)
        slope = gate * (1.0 + preact * (1.0 - gate))
        grad_pre = jnp.where(live, grad_ref[rows, :].astype(F32) * slope, 0.0).astype(BF16)
        pre_ref[rows, :] = grad_pre
        pre_copy(i).start()
        bias_sum_ref[...] += jnp.sum(grad_pre.astype(F32), axis=0, keepdims=True)

    save(pre_ref, pre_hbm)
    save(out_ref, out_hbm)
    if m:
        loads[5].wait()

    @pl.loop(0, 4)
    def _(block):
        term = product_rows(mixed_ref[block], pre_ref[...])
        total_ref[block] = total_ref[block] + term if m else term

    if ended:
        half = width // 2
        upper = lax.axis_index("clus") % 2 == 1
        column = lax.axis_index("col")
        for block in range(4):
            source = partner(column, 1) if block % 2 else column
            source = partner(source, 2) if block >= 2 else source
            rows = at(source, width)
            low, high = total_ref[block, :, :half], total_ref[block, :, half:]
            parts[0][rows, :] = jnp.where(upper, high, low)
            parts[1][rows, :] = jnp.where(upper, low, high).astype(BF16)
        for part, result in zip(parts, results):
            save(part, result)
    else:
        save(total_ref, results[0])

    weight_copy.wait_recv()
    for i in range(narrow):
        pre_copy(i).wait_recv()
    save(mate_pre_ref, mate_pre_hbm)
    if ended:
        save(mate_weight_ref, mate_weight_hbm)
    step = width // chunks
    for i in range(wide):
        rows = slice(i * WIDE, (i + 1) * WIDE)
        away = product_back(pre_ref[rows, :], weight_ref[2]) + product_back(mate_pre_ref[rows, :], mate_weight_ref[1])
        away_ref[rows, :] = away.astype(BF16)
        for chunk in range(chunks):
            columns = slice(chunk * step, (chunk + 1) * step)
            save(away_ref.at[rows, columns], away_hbm[chunk].at[rows])
    here_copy.wait_send()
    weight_copy.wait_send()
    for i in range(wide):
        there_copy(i).wait_send()
    for i in range(narrow):
        pre_copy(i).wait_send()
    for item in started:
        item.wait()


def batch(table, m, matrix, scale, far, here, weight, for_mate, out_grad, bias, total, bias_sum, chunks, after=()):
    nodes, width = far.array.shape
    wide, narrow = nodes // WIDE, nodes // TILE
    flat = lambda i: (0, 0)
    ended = m == MB - 1
    parts = [((D, width // 2), F32), ((D, width // 2), BF16)] if ended else []
    results = [(*part, None, None) for part in parts]
    if not ended:
        results = [((4, width, width), F32, None, None, pltpu.VMEM)]
    return launch(
        f"batch{m}", functools.partial(batch_kernel, m, chunks), table,
        [(array, None, None) for array in (matrix, scale, far, here, weight, for_mate, out_grad)]
        + [(bias, (1, width), flat)]
        + ([(total, None, None), (bias_sum, (1, width), flat)] if m else []),
        [((nodes, width), BF16, None, None, pltpu.VMEM)]
        + [((nodes, width), BF16, None, None)] * 2
        + [((nodes, width // chunks), BF16, None, None)] * chunks
        + ([(for_mate.array.shape, BF16, None, None)] if ended else [])
        + results
        + [((1, width), F32, (1, width), flat)],
        after=after, barrier=BATCH_ID + m, vmem=34 if m == MB - 1 else 32,
        scratch=[
            pltpu.VMEM((nodes, nodes), BF16),
            pltpu.VMEM((nodes, LANES), F32),
            pltpu.VMEM((nodes, width), BF16),
            pltpu.VMEM((4, nodes, width), BF16),
            pltpu.VMEM(weight.array.shape, BF16),
            pltpu.VMEM(for_mate.array.shape, BF16),
            pltpu.VMEM((nodes, width), BF16),
            pltpu.VMEM((nodes, width), BF16),
            pltpu.VMEM((nodes, width), BF16),
            pltpu.VMEM((nodes, width), BF16),
            pltpu.VMEM((nodes, width), BF16),
            pltpu.VMEM((4, width, width), F32),
            pltpu.SemaphoreType.DMA((wide + 6,)),
            pltpu.SemaphoreType.DMA((6 + wide * chunks,)),
            pltpu.SemaphoreType.DMA((2 + wide + narrow,)),
            pltpu.SemaphoreType.DMA((2 + wide + narrow,)),
        ]
        + [pltpu.VMEM(*part) for part in parts],
    )


def scatter_job(m, columns, own_source, got_source, scale_source, matrix_source, grads_hbm, scratch, semaphores):
    own_ref, got_ref, scale_ref, matrix_ref, sum_ref, grad_ref = scratch
    steps = matrix_ref.shape[0] // WIDE
    loads = [
        pltpu.make_async_copy(source, target, semaphores.at[i])
        for i, (source, target) in enumerate(
            [(own_source.at[:, columns], own_ref), (got_source, got_ref), (scale_source.at[m], scale_ref)]
        )
    ]
    tiles, stores = [], []
    for i in range(steps):
        rows = pl.ds(i * WIDE, WIDE)
        tiles.append(pltpu.make_async_copy(matrix_source.at[rows], matrix_ref.at[rows], semaphores.at[3 + i]))
        stores.append(
            pltpu.make_async_copy(grad_ref.at[rows], grads_hbm.at[m, rows, columns], semaphores.at[3 + steps + i])
        )

    def work():
        for item in loads:
            item.wait()
        grad_mixed = (own_ref[...].astype(F32) + got_ref[...].astype(F32)).astype(BF16)
        sum_ref[...] = scaled(grad_mixed.astype(F32), scale_ref[...]).astype(BF16)
        for i in range(steps):
            tiles[i].wait()
            rows = slice(i * WIDE, (i + 1) * WIDE)
            grad_ref[rows, :] = product(matrix_ref[rows, :], sum_ref[...]).astype(BF16)
            stores[i].start()

    return loads + tiles, work, stores


def scatter_scratch(nodes, width):
    return [
        pltpu.VMEM((nodes, width), BF16),
        pltpu.VMEM((nodes, width), BF16),
        pltpu.VMEM((nodes, LANES), F32),
        pltpu.VMEM((nodes, nodes), BF16),
        pltpu.VMEM((nodes, width), BF16),
        pltpu.VMEM((nodes, width), BF16),
        pltpu.SemaphoreType.DMA((3 + 2 * (nodes // WIDE),)),
    ]


def scatter_kernel(m, chunk, own_hbm, got_hbm, scale_hbm, matrix_hbm, grads_hbm, *refs):
    width = got_hbm.shape[1]
    loads, work, stores = scatter_job(
        m, pl.ds(chunk * width, width), own_hbm, got_hbm, scale_hbm, matrix_hbm, grads_hbm, refs[:6], refs[6]
    )
    for item in loads:
        item.start()
    work()
    for item in stores:
        item.wait()


def scatter(m, chunk, own, got, scale, matrix, grads, after=()):
    nodes, width = own.array.shape
    return launch(
        f"scatter{m}_{chunk}", functools.partial(scatter_kernel, m, chunk), None,
        [(array, None, None) for array in (own, got, scale, matrix)],
        [((MB, nodes, width), BF16, None, None)],
        after=after, alias=(grads, 0), scratch=scatter_scratch(nodes, got.array.shape[1]),
    )[0]


def sum_kernel(groups, capacity, table_ref, *refs):
    keep_hbm, sent_hbm, bias_ref, weight_hbm, mate_weight_hbm = refs[:5]
    pre_hbm, mate_hbm, refs = refs[5 : 5 + MB], refs[5 + MB : 5 + 2 * MB], refs[5 + 2 * MB :]
    own_ref, got_ref, bias_out_ref, back_hbm, refs = *refs[:4], refs[4:]
    pre_ref, mate_ref, weights_ref, back_ref, load, store, refs = *refs[:6], refs[6:]
    keep_ref, pair_ref, land_ref, out_ref, total_ref, end_out_ref, end_in_ref, row_ref = refs[:8]
    pair_send, pair_receive, line_send, line_receive, row_send, row_receive = refs[8:]
    own = lax.axis_index("clus")
    place, pairs = own // 2, groups // 2
    other = partner(own, 1)
    rows = keep_ref.shape[0]
    size = rows // CHUNKS
    ahead, behind = place + 1 < pairs, place >= 1

    def remote(source, target, sent, received, device):
        return pltpu.make_async_remote_copy(
            src_ref=source,
            dst_ref=target,
            send_sem=sent,
            recv_sem=received,
            device_id={"clus": device},
            device_id_type=pl.DeviceIdType.MESH,
        )

    def part(chunk):
        return pl.ds(pl.multiple_of(chunk * size, size), size)

    def pair_copy(chunk):
        return remote(
            sent_hbm.at[part(chunk)], pair_ref.at[part(chunk)], pair_send.at[chunk], pair_receive.at[chunk], other
        )

    def line_copy(direction, chunk):
        return remote(
            out_ref.at[direction, part(chunk)], land_ref.at[direction, part(chunk)],
            line_send.at[direction, chunk], line_receive.at[direction, chunk],
            own + 2 if direction == 0 else own - 2,
        )

    def row_copy(number):
        device = (other, own + 2, own - 2)[number]
        return remote(row_ref.at[number], row_ref.at[3 + number], row_send.at[number], row_receive.at[number], device)

    end_copy = remote(end_out_ref, end_in_ref, pair_send.at[CHUNKS], pair_receive.at[CHUNKS], other)

    nodes = pre_ref.shape[1]
    tiles = nodes // WIDE
    loads = [
        pltpu.make_async_copy(source, target, load.at[i])
        for i, (source, target) in enumerate(
            [(keep_hbm, keep_ref), (weight_hbm.at[0], weights_ref.at[0]), (mate_weight_hbm.at[0], weights_ref.at[1])]
            + [(source, pre_ref.at[m]) for m, source in enumerate(pre_hbm)]
            + [(source, mate_ref.at[m]) for m, source in enumerate(mate_hbm)]
        )
    ]
    stores = [pltpu.make_async_copy(back_ref.at[m], back_hbm.at[m], store.at[m]) for m in range(MB)]

    def back(number):
        m, i = number // tiles, number % tiles
        if i == 0:
            loads[3 + m].wait()
            loads[3 + MB + m].wait()
        down = slice(i * WIDE, (i + 1) * WIDE)
        term = product_back(pre_ref[m, down, :], weights_ref[0]) + product_back(mate_ref[m, down, :], weights_ref[1])
        back_ref[m, down, :] = term.astype(BF16)
        if i == tiles - 1:
            stores[m].start()

    land_ref[...] = jnp.zeros_like(land_ref)
    row_ref[...] = jnp.zeros_like(row_ref)
    row_ref[0] = bias_ref[...]
    for item in loads:
        item.start()
    barrier = pltpu.get_barrier_semaphore()

    def greet(index):
        pl.semaphore_signal(barrier, inc=1, device_id={"clus": index}, device_id_type=pl.DeviceIdType.MESH)

    greet(other)

    @pl.when(ahead)
    def _():
        greet(own + 2)

    @pl.when(behind)
    def _():
        greet(own - 2)

    pl.semaphore_wait(barrier, 1 + jnp.where(ahead, 1, 0) + jnp.where(behind, 1, 0))
    row_copy(0).start()
    for chunk in range(CHUNKS):
        pair_copy(chunk).start()
    for item in loads[:3]:
        item.wait()

    def pass_on(direction, chunk, first):
        sums = keep_ref[part(chunk), :]
        if not first:
            sums = sums + land_ref[direction, part(chunk), :].astype(F32)
        out_ref[direction, part(chunk), :] = sums.astype(BF16)
        line_copy(direction, chunk).start()

    def pass_row(direction, first):
        row_ref[1 + direction] = row_ref[0] if first else row_ref[0] + row_ref[4 + direction]
        row_copy(1 + direction).start()

    steps = CHUNKS + pairs - 1
    for step in range(steps):
        if step < CHUNKS:
            pair_copy(step).wait_recv()
            keep_ref[part(step), :] += pair_ref[part(step), :].astype(F32)
            if step == 0:
                row_copy(0).wait()
                row_ref[0] += row_ref[3]
            for direction, (here, there) in enumerate(((behind, ahead), (ahead, behind))):

                @pl.when(jnp.logical_not(here) & there)
                def _(direction=direction, step=step):
                    pass_on(direction, step, True)
                    if step == 0:
                        pass_row(direction, True)

        for direction, (here, there) in enumerate(((behind, ahead), (ahead, behind))):
            chunk = step - (place if direction == 0 else pairs - 1 - place)

            @pl.when(here & (chunk >= 0) & (chunk < CHUNKS))
            def _(direction=direction, chunk=chunk, there=there):
                line_copy(direction, chunk).wait_recv()

                @pl.when(there)
                def _():
                    pass_on(direction, chunk, False)

                @pl.when(chunk == 0)
                def _():
                    row_copy(1 + direction).wait_recv()

                    @pl.when(there)
                    def _():
                        pass_row(direction, False)

        for number in range(step * MB * tiles // steps, (step + 1) * MB * tiles // steps):
            back(number)

    total_ref[:rows, :] = keep_ref[...] + (land_ref[0].astype(F32) + land_ref[1].astype(F32))
    total_ref[rows:, :] = jnp.zeros((capacity + SUBLANES, keep_ref.shape[1]), F32)
    end_out_ref[...] = take_rows(total_ref, table_ref[STARTS + other], capacity, rows - 1).astype(BF16)
    end_copy.start()
    own_ref[...] = take_rows(total_ref, table_ref[STARTS + own], capacity, rows - 1)
    bias_out_ref[...] = row_ref[0] + (row_ref[4] + row_ref[5])
    end_copy.wait()
    got_ref[...] = end_in_ref[...]
    for chunk in range(CHUNKS):
        pair_copy(chunk).wait_send()
    for direction, there in enumerate((ahead, behind)):

        @pl.when(there)
        def _(direction=direction):
            row_copy(1 + direction).wait_send()
            for chunk in range(CHUNKS):
                line_copy(direction, chunk).wait_send()

    for item in stores:
        item.wait()


def sum_over_owners(table, groups, capacity, keep, sent, bias, weight, mate_weight, pres, mates, after=()):
    rows, half = keep.shape
    nodes, width = pres[0].shape
    flat = lambda i: (0, 0)
    shape = (capacity, half)
    return launch(
        "sum", functools.partial(sum_kernel, groups, capacity), table,
        [(array, None, None) for array in (keep, sent)]
        + [(bias, bias.shape, flat)]
        + [(array, None, None) for array in (weight, mate_weight, *pres, *mates)],
        [
            (shape, F32, shape, flat),
            (shape, BF16, shape, flat),
            (bias.shape, F32, bias.shape, flat),
            ((MB, nodes, width), BF16, None, None),
        ],
        after=after, barrier=SUM_ID, vmem=34,
        scratch=[
            pltpu.VMEM((MB, nodes, width), BF16),
            pltpu.VMEM((MB, nodes, width), BF16),
            pltpu.VMEM((2, width, width), BF16),
            pltpu.VMEM((MB, nodes, width), BF16),
            pltpu.SemaphoreType.DMA((3 + 2 * MB,)),
            pltpu.SemaphoreType.DMA((MB,)),
            pltpu.VMEM((rows, half), F32),
            pltpu.VMEM((rows, half), BF16),
            pltpu.VMEM((2, rows, half), BF16),
            pltpu.VMEM((2, rows, half), BF16),
            pltpu.VMEM((rows + capacity + SUBLANES, half), F32),
            pltpu.VMEM(shape, BF16),
            pltpu.VMEM(shape, BF16),
            pltpu.VMEM((6, 1, width), F32),
            pltpu.SemaphoreType.DMA((CHUNKS + 1,)),
            pltpu.SemaphoreType.DMA((CHUNKS + 1,)),
            pltpu.SemaphoreType.DMA((2, CHUNKS)),
            pltpu.SemaphoreType.DMA((2, CHUNKS)),
            pltpu.SemaphoreType.DMA((3,)),
            pltpu.SemaphoreType.DMA((3,)),
        ],
    )


def adamw_update(current, first_moment, second_moment, gradient, step_rate):
    first_new = BETA_ONE * first_moment + (1.0 - BETA_ONE) * gradient
    second_new = BETA_TWO * second_moment + (1.0 - BETA_TWO) * gradient * gradient
    fixed_first = first_new / (1.0 - BETA_ONE**STEP)
    fixed_second = second_new / (1.0 - BETA_TWO**STEP)
    updated = current - step_rate * (
        fixed_first / (jnp.sqrt(fixed_second) + EPSILON) + DECAY * current
    )
    return (updated, first_new, second_new)


def finish_kernel(groups, table_ref, *refs):
    done = MB - 1
    own_ref, got_ref, bias_grad_ref, biases = refs[0], refs[1], refs[2], refs[3:6]
    weights_hbm, out_parts, refs = refs[6:9], refs[9 : 9 + MB], refs[9 + MB :]
    back_hbm, gots, (scale_hbm, matrix_hbm), refs = refs[0], refs[1 : 1 + done], refs[1 + done : 3 + done], refs[3 + done :]
    updated_hbm, bias_outs, (out_hbm, grads_hbm, last_back_ref, last_matrix_ref), refs = refs[:3], refs[3:6], refs[6:10], refs[10:]
    weights, (weight_load, weight_store, store), refs = refs[:3], refs[3:6], refs[6:]
    jobs = [
        scatter_job(
            m, pl.ds(0, back_hbm.shape[2]), back_hbm.at[m], gots[m], scale_hbm, matrix_hbm.at[m], grads_hbm,
            refs[7 * m : 7 * m + 6], refs[7 * m + 6],
        )
        for m in range(done)
    ]
    weight_loads = [
        pltpu.make_async_copy(source, target, weight_load.at[i])
        for i, (source, target) in enumerate(zip(weights_hbm, weights))
    ]
    weight_stores = [
        pltpu.make_async_copy(source, target, weight_store.at[i])
        for i, (source, target) in enumerate(zip(weights, updated_hbm))
    ]
    moves = [
        pltpu.make_async_copy(source, target, store.at[i])
        for i, (source, target) in enumerate(
            [(part, out_hbm.at[m]) for m, part in enumerate(out_parts)]
            + [(back_hbm.at[done], last_back_ref), (matrix_hbm.at[done], last_matrix_ref)]
        )
    ]
    for item in jobs[0][0] + weight_loads:
        item.start()
    for later, _, _ in jobs[1:]:
        for item in later:
            item.start()
    for item in moves:
        item.start()
    jobs[0][1]()

    for item in weight_loads:
        item.wait()
    rows, width = weights[0].shape
    half = width // 2
    strip = min(rows, TILE // 2)
    own = table_ref[GROUP]
    for first in range(0, rows, strip):
        row_ids = first + lax.broadcasted_iota(jnp.int32, (strip, half), 0)
        used = row_ids < table_ref[STARTS + groups + own]
        down = slice(first, first + strip)
        for side in range(2):
            mine = (own & 1) == side
            here, there = own_ref[down, :], got_ref[down, :].astype(F32)
            columns = slice(side * half, (side + 1) * half)
            results = adamw_update(*(ref[down, columns] for ref in weights), jnp.where(mine, here, there), RATE_WEIGHT)
            for ref, result in zip(weights, results):
                ref[down, columns] = jnp.where(used, result, 0.0)
    for item in weight_stores:
        item.start()
    results = adamw_update(*(ref[...] for ref in biases), bias_grad_ref[...], RATE_BIAS)
    for ref, result in zip(bias_outs, results):
        ref[...] = result

    for _, work, _ in jobs[1:]:
        work()
    for item in weight_stores + moves:
        item.wait()
    for _, _, stores in jobs:
        for item in stores:
            item.wait()


def finish(table, groups, mine, other, bias_grad, biases, weights, outputs, backs, gots, scale, matrix, after=()):
    capacity, width = weights[0].shape
    nodes = outputs[0].array.shape[0]
    fixed = lambda i: (0, 0)
    scratch = [pltpu.VMEM((capacity, width), F32)] * 3 + [
        pltpu.SemaphoreType.DMA((3,)),
        pltpu.SemaphoreType.DMA((3,)),
        pltpu.SemaphoreType.DMA((MB + 2,)),
    ]
    for _ in gots:
        scratch += scatter_scratch(nodes, width)
    return launch(
        "finish", functools.partial(finish_kernel, groups), table,
        [(array, array.array.shape, fixed) for array in (mine, other)]
        + [(array, (1, width), fixed) for array in (bias_grad, *biases)]
        + [(array, None, None) for array in (*weights, *outputs, backs, *gots, scale, matrix)],
        [((capacity, width), F32, None, None)] * 3
        + [((1, width), F32, (1, width), fixed)] * 3
        + [((MB, nodes, width), BF16, None, None)] * 2
        + [((nodes, width), BF16, None, None, pltpu.VMEM), ((nodes, nodes), BF16, None, None, pltpu.VMEM)],
        after=after, scratch=scratch, vmem=32,
    )


def shards(
    features,
    neighbours,
    node_counts,
    row_counts,
    master_weight,
    weight_first,
    weight_second,
    master_bias,
    bias_first,
    bias_second,
    out_grad,
):
    groups = lax.axis_size("clus")
    capacity, width = master_weight.shape
    owner_ids = jnp.arange(groups, dtype=jnp.int32)
    starts = jnp.sum(jnp.where(owner_ids[None, :] < owner_ids[:, None], row_counts[None, :], 0), axis=1)
    table = jnp.concatenate(
        [
            jnp.stack([lax.axis_index("clus"), lax.axis_index("col")]).astype(jnp.int32),
            node_counts[:, 0],
            starts.astype(jnp.int32),
            row_counts,
        ]
    )
    bias_row, bias_first_row, bias_second_row = (
        array.reshape(1, width) for array in (master_bias, bias_first, bias_second)
    )

    picked = pick(features, (0,))
    picked = picked + pick(features, tuple(range(1, MB)), picked)
    far = [Kept(flip(array, "col", 2), None) for array in picked]

    matrix, *kept, slots = front(table, groups, master_weight, jnp.swapaxes(neighbours, 1, 2), features, [picked[-1]])
    scale, here = (Kept(array) for array in kept)
    weight, for_mate = (Kept(array) for array in place(table, slots))
    last = for_mate
    total, bias_sum = None, None
    outputs, pres, mates, away = [], [], [], []
    for m in range(MB):
        chunks = 2 if m == MB - 1 else 1
        out_m, pre_m, mate_m, *rest = batch(
            table, m, matrix, scale, far[m], here, weight, for_mate, out_grad, bias_row, total, bias_sum, chunks,
            [last],
        )
        outputs.append(Kept(out_m))
        pres.append(pre_m)
        mates.append(mate_m)
        away.append([Kept(flip(chunk, "col", 2), None) for chunk in rest[:chunks]])
        total, bias_sum = Kept(rest[chunks]), rest[-1]
        last = bias_sum

    mate_weight, keep, sent, bias_sum = rest[chunks:]
    mine, other, bias_total, backs = sum_over_owners(
        table, groups, capacity, keep, sent, bias_sum, weight, mate_weight, pres, mates, [last]
    )
    *updated, outputs, input_grads, last_back, last_matrix = finish(
        table, groups, Kept(mine, None), Kept(other, None), bias_total, (bias_row, bias_first_row, bias_second_row),
        (master_weight, weight_first, weight_second), outputs, backs, [part[0] for part in away[:-1]],
        scale, matrix, [bias_total],
    )
    for chunk, got in enumerate(away[-1]):
        input_grads = scatter(MB - 1, chunk, Kept(last_back), got, scale, Kept(last_matrix), input_grads)
    return (outputs, input_grads, *updated[:3], *(row.reshape(width) for row in updated[3:]))


def solution(mesh):
    in_specs = (
        P(None, "clus", "col"),
        P(None, "clus", None),
        P(None, "clus"),
        P(),
        P("clus", "col"),
        P("clus", "col"),
        P("clus", "col"),
        P("col"),
        P("col"),
        P("col"),
        P(None, "clus", "col"),
    )
    out_specs = (
        P(None, "clus", "col"),
        P(None, "clus", "col"),
        P("clus", "col"),
        P("clus", "col"),
        P("clus", "col"),
        P("col"),
        P("col"),
        P("col"),
    )
    return jax.shard_map(shards, mesh=mesh, in_specs=in_specs, out_specs=out_specs, check_vma=False)
```

```python
import functools

import jax
import jax.numpy as jnp
from jax import lax
from jax.experimental import pallas as pl
from jax.experimental.pallas import tpu as pltpu
from jax.sharding import PartitionSpec as P

D = 2048
MB = 3
STEP = 10

BETA_ONE = 0.9
BETA_TWO = 0.95
EPSILON = 1e-08
DECAY = 0.1
RATE_WEIGHT = 0.06
RATE_BIAS = 0.6

LANES = 128
DIGIT_BITS = 5
DIGITS = 6
STRIP = 32
SUBLANES = 8
TILE = 256
WIDE = 512
HALVES = 2
PIECES = 4
UNROLL = 3
CHUNKS = 8
MIB = 1024 * 1024
SMALL = 1 << 16

GROUP, COLUMN, LIMITS = 0, 1, 2
STARTS = LIMITS + MB

FRONT_ID, SUM_ID, BATCH_ID = 1, 2, 3

F32, BF16 = jnp.float32, jnp.bfloat16


class Kept:
    def __init__(self, array, space=pltpu.VMEM):
        self.array, self.space = array, space


def located(item):
    if isinstance(item, Kept):
        return pltpu.with_memory_space_constraint(item.array, item.space) if item.space else item.array
    return pltpu.with_memory_space_constraint(item, pltpu.HBM) if item.size > SMALL else item


def launch(name, body, table, ins, outs, grid=(1,), after=(), alias=None, scratch=(), barrier=None, vmem=16):
    tables = [] if table is None else [table]

    def spec(block, index):
        if block is None:
            return pl.BlockSpec(memory_space=pl.ANY)
        return pl.BlockSpec(block, lambda *a: index(*a[: len(grid)]))

    unread = ([alias[0]] if alias else []) + [array for array in after if alias is None or array is not alias[0]]

    def kernel(*refs):
        table_refs, refs = refs[: len(tables)], refs[len(tables) :]
        body(*table_refs, *refs[: len(ins)], *refs[len(ins) + len(unread) :])

    return pl.pallas_call(
        kernel,
        grid_spec=pltpu.PrefetchScalarGridSpec(
            num_scalar_prefetch=len(tables),
            grid=grid,
            in_specs=[spec(block, index) for _, block, index in ins]
            + [pl.BlockSpec(memory_space=pl.ANY)] * len(unread),
            out_specs=[spec(out[2], out[3]) for out in outs],
            scratch_shapes=list(scratch),
        ),
        out_shape=[
            (out[4] if len(out) > 4 else pltpu.HBM if out[2] is None else jax.ShapeDtypeStruct)(out[0], out[1])
            for out in outs
        ],
        input_output_aliases={len(tables) + len(ins): alias[1]} if alias else {},
        compiler_params=pltpu.CompilerParams(
            vmem_limit_bytes=vmem * MIB, collective_id=barrier, has_side_effects=barrier is not None
        ),
        cost_estimate=pl.CostEstimate(flops=1, bytes_accessed=1, transcendentals=0),
        name=name,
    )(*tables, *(located(item[0]) for item in ins), *(located(item) for item in unread))


def flip(values, axis, bit):
    size = lax.axis_size(axis)
    return lax.ppermute(values, axis, [(i, i ^ bit) for i in range(size)])


def partner(index, bit):
    return index + bit * (1 - 2 * ((index // bit) % 2))


def product(left, right):
    return jnp.dot(left, right, preferred_element_type=F32)


def product_back(left, right):
    return lax.dot_general(left, right, (((1,), (1,)), ((), ())), preferred_element_type=F32)


def product_rows(left, right):
    return lax.dot_general(left, right, (((0,), (0,)), ((), ())), preferred_element_type=F32)


def scaled(values, scale):
    return values * jnp.concatenate([scale] * (values.shape[1] // LANES), axis=1)


def put_rows(ref, first, rows):
    base = pl.multiple_of((first // SUBLANES) * SUBLANES, SUBLANES)
    offset = first - base
    moved = jnp.concatenate([rows, jnp.zeros((SUBLANES, rows.shape[1]), rows.dtype)], axis=0)
    wanted = jnp.broadcast_to(offset, moved.shape)
    for bit in (1, 2, 4):
        moved = jnp.where((wanted & bit) != 0, pltpu.roll(moved, bit, 0), moved)
    head = ref[pl.ds(base, SUBLANES), :]
    row_ids = lax.broadcasted_iota(jnp.int32, head.shape, 0)
    ref[pl.ds(base, SUBLANES), :] = jnp.where(row_ids < offset, head, moved[:SUBLANES])
    ref[pl.ds(pl.multiple_of(base + SUBLANES, SUBLANES), rows.shape[0]), :] = moved[SUBLANES:]


def take_rows(ref, first, count, largest):
    bit = 1 << (largest.bit_length() - 1)
    rows = ref[...]
    while bit:
        length = count + max(bit, SUBLANES)
        if bit >= SUBLANES:
            moved = rows[bit : bit + length]
            missing = length - moved.shape[0]
            if missing:
                moved = jnp.concatenate([moved, jnp.zeros((missing, rows.shape[1]), rows.dtype)], axis=0)
        else:
            moved = pltpu.roll(rows, length - bit, 0)
        chosen = (jnp.broadcast_to(first, (length, rows.shape[1])) & bit) != 0
        rows = jnp.where(chosen, moved, rows[:length])
        bit //= 2
    return rows[:count]


def relay(sources, targets, buffers, load, store):
    def piece(ref, i):
        rows = ref.shape[0] // PIECES
        return ref.at[pl.ds(i * rows, rows)]

    loads, stores = [], []
    for number, (source, target, buffer) in enumerate(zip(sources, targets, buffers)):
        for i in range(PIECES):
            place = number * PIECES + i
            loads.append(pltpu.make_async_copy(piece(source, i), piece(buffer, i), load.at[place]))
            stores.append(pltpu.make_async_copy(piece(buffer, i), piece(target, i), store.at[place]))
    return loads, stores


def first_kernel(source_hbm, target_ref, semaphore):
    copy = pltpu.make_async_copy(source_hbm.at[0], target_ref, semaphore)
    copy.start()
    copy.wait()


def pick_first(stacked):
    return launch(
        "first", first_kernel, None,
        [(stacked, None, None)], [(stacked.shape[1:], stacked.dtype, None, None, pltpu.VMEM)],
        scratch=[pltpu.SemaphoreType.DMA],
    )


def pick_kernel(batches, source_ref, *refs):
    targets, (buffer_ref, load, store) = refs[:-3], refs[-3:]
    loads, stores = relay(
        [source_ref.at[m] for m in batches], targets, [buffer_ref.at[i] for i in range(len(batches))], load, store
    )
    for item in loads:
        item.start()
    for item, onward in zip(loads, stores):
        item.wait()
        onward.start()
    for item in stores:
        item.wait()


def pick(stacked, batches, after=()):
    count = len(batches)
    return launch(
        f"pick{batches[0]}", functools.partial(pick_kernel, batches), None,
        [(stacked, None, None)], [(stacked.shape[1:], stacked.dtype, None, None)] * count,
        after=after,
        scratch=[
            pltpu.VMEM((count, *stacked.shape[1:]), stacked.dtype),
            pltpu.SemaphoreType.DMA((count * PIECES,)),
            pltpu.SemaphoreType.DMA((count * PIECES,)),
        ],
    )


def count_tile(limit, first, neighbour_ref, matrix_ref, scale_ref, lanes):
    nodes = matrix_ref.shape[1]
    words = -(-(nodes // LANES) // DIGITS)
    entries = neighbour_ref[0, :, lanes]
    node_ids = first + lax.broadcasted_iota(jnp.int32, entries.shape, 1)
    valid = (entries < limit) & (node_ids < limit)
    low = entries & (LANES - 1)
    high = entries >> 7
    digits = []
    for word in range(words):
        inside = valid & (high >= word * DIGITS) & (high < (word + 1) * DIGITS)
        shift = jnp.where(inside, (high - word * DIGITS) * DIGIT_BITS, 0)
        digits.append(jnp.where(inside, jnp.left_shift(1, shift), 0))
    for strip in range(LANES // STRIP):
        row_ids = strip * STRIP + lax.broadcasted_iota(jnp.int32, (STRIP, LANES), 0)
        sums = [jnp.zeros((STRIP, LANES), jnp.int32) for _ in range(words)]
        for entry in range(entries.shape[0]):
            hit = row_ids == low[entry : entry + 1, :]
            for word in range(words):
                sums[word] = sums[word] + jnp.where(hit, digits[word][entry : entry + 1, :], 0)
        for block in range(nodes // LANES):
            word, digit = block // DIGITS, block % DIGITS
            count = jnp.right_shift(sums[word], digit * DIGIT_BITS) & ((1 << DIGIT_BITS) - 1)
            rows = slice(block * LANES + strip * STRIP, block * LANES + (strip + 1) * STRIP)
            matrix_ref[0, rows, lanes] = count.astype(F32).astype(BF16)
    rows = pl.ds(pl.multiple_of(first, LANES), LANES)
    square = matrix_ref[0, rows, lanes].astype(F32)
    on_diagonal = lax.broadcasted_iota(jnp.int32, square.shape, 0) == lax.broadcasted_iota(jnp.int32, square.shape, 1)
    matrix_ref[0, rows, lanes] = jnp.where(on_diagonal, 2.0 * square + 2.0, square).astype(BF16)
    degree = 1.0 + jnp.sum(valid.astype(F32), axis=0, keepdims=True)
    factor = (node_ids[:1] < limit).astype(F32) / degree
    scale_ref[0, lanes, :] = jnp.transpose(jnp.broadcast_to(factor, (LANES, LANES)))


def front_kernel(
    groups, total, table_ref, master_ref, neighbour_ref, feature_ref, matrix_ref, scale_ref, mixed_ref, slots_ref,
    block_ref, local_semaphore, line_send, line_receive, pair_send, pair_receive,
):
    batch, tile_id = pl.program_id(0), pl.program_id(1)
    tiles = pl.num_programs(1)
    step = batch * tiles + tile_id
    own = lax.axis_index("clus")
    place, side = own // 2, own % 2
    pairs = groups // 2
    other = partner(own, 1)

    def rows_of(half):
        size = block_ref.shape[0] // HALVES
        return pl.ds(half * size, size)

    def remote(source, target, sent, received, device):
        return pltpu.make_async_remote_copy(
            src_ref=source,
            dst_ref=target,
            send_sem=sent,
            recv_sem=received,
            device_id={"clus": device},
            device_id_type=pl.DeviceIdType.MESH,
        )

    def origin_of(direction, hop):
        return place - 1 - hop if direction == 0 else place + 1 + hop

    def line_copy(direction, hop, half):
        slot = (place - hop if direction == 0 else place + hop) * 2 + side
        target = slots_ref.at[slot, rows_of(half)]
        return remote(
            block_ref.at[rows_of(half)] if hop == 0 else target, target,
            line_send.at[direction, hop, half], line_receive.at[direction, hop, half],
            own + 2 if direction == 0 else own - 2,
        )

    def sends(direction, hop):
        if direction == 0:
            return (place - hop >= 0) & (place + 1 < pairs)
        return (place + hop < pairs) & (place - 1 >= 0)

    def arrives(direction, hop):
        return place - 1 - hop >= 0 if direction == 0 else place + 1 + hop < pairs

    def arrival(direction, hop, half):
        target = slots_ref.at[origin_of(direction, hop) * 2 + side, rows_of(half)]
        return remote(
            target, target, line_send.at[direction, hop, half], line_receive.at[direction, hop, half], other
        )

    def pair_copy(direction, hop, half):
        slot = own if hop < 0 else origin_of(direction, hop) * 2 + side
        number = 0 if hop < 0 else 1 + 2 * hop + direction
        target = slots_ref.at[slot, rows_of(half)]
        return remote(
            block_ref.at[rows_of(half)] if hop < 0 else target, target,
            pair_send.at[number, half], pair_receive.at[number, half], other,
        )

    def pair_arrival(direction, hop, half):
        slot = other if hop < 0 else origin_of(direction, hop) * 2 + 1 - side
        number = 0 if hop < 0 else 1 + 2 * hop + direction
        target = slots_ref.at[slot, rows_of(half)]
        return remote(target, target, pair_send.at[number, half], pair_receive.at[number, half], other)

    local_copy = pltpu.make_async_copy(block_ref, slots_ref.at[own], local_semaphore)
    hops = pairs - 1

    @pl.when(step == 0)
    def _():
        barrier = pltpu.get_barrier_semaphore()

        def greet(index):
            pl.semaphore_signal(barrier, inc=1, device_id={"clus": index}, device_id_type=pl.DeviceIdType.MESH)

        greet(other)

        @pl.when(place + 1 < pairs)
        def _():
            greet(own + 2)

        @pl.when(place - 1 >= 0)
        def _():
            greet(own - 2)

        pl.semaphore_wait(barrier, 1 + jnp.where(place + 1 < pairs, 1, 0) + jnp.where(place - 1 >= 0, 1, 0))
        block_ref[...] = master_ref[...].astype(BF16)
        for half in range(HALVES):
            for direction in range(2):
                pl.when(sends(direction, 0))(line_copy(direction, 0, half).start)
            pair_copy(0, -1, half).start()
        local_copy.start()

    limit = table_ref[LIMITS + batch]
    tile = mixed_ref.shape[1]
    for part in range(tile // LANES):
        first = tile_id * tile + part * LANES
        count_tile(limit, first, neighbour_ref, matrix_ref, scale_ref, slice(part * LANES, (part + 1) * LANES))
    mixed_ref[0] = scaled(product_rows(matrix_ref[0], feature_ref[0]), scale_ref[0]).astype(BF16)

    for event in range(hops * HALVES):
        hop, half = event // HALVES, event % HALVES

        @pl.when(step == min(total - 1, ((event + 1) * total) // (hops * HALVES)))
        def _(hop=hop, half=half):
            for direction in range(2):

                @pl.when(arrives(direction, hop))
                def _(direction=direction):
                    arrival(direction, hop, half).wait_recv()
                    pair_copy(direction, hop, half).start()

                if hop + 1 < hops:
                    pl.when(sends(direction, hop + 1))(line_copy(direction, hop + 1, half).start)

    @pl.when(step == total - 1)
    def _():
        local_copy.wait()
        for half in range(HALVES):
            pair_copy(0, -1, half).wait_send()
            pair_arrival(0, -1, half).wait_recv()
            for hop in range(hops):
                for direction in range(2):
                    pl.when(sends(direction, hop))(line_copy(direction, hop, half).wait_send)

                    @pl.when(arrives(direction, hop))
                    def _(direction=direction, hop=hop, half=half):
                        pair_copy(direction, hop, half).wait_send()
                        pair_arrival(direction, hop, half).wait_recv()


def front(table, groups, master, neighbours, features, after=()):
    _, entries, nodes = neighbours.shape
    capacity, width = master.shape
    hops = groups // 2 - 1
    steps = MB * (nodes // TILE)
    return launch(
        "front", functools.partial(front_kernel, groups, steps), table,
        [
            (master, (capacity, width), lambda b, i: (0, 0)),
            (neighbours, (1, entries, TILE), lambda b, i: (b, 0, i)),
            (features, (1, nodes, width), lambda b, i: (b, 0, 0)),
        ],
        [
            ((MB, nodes, nodes), BF16, (1, nodes, TILE), lambda b, i: (b, 0, i), pltpu.HBM),
            ((MB, nodes, LANES), F32, (1, TILE, LANES), lambda b, i: (b, i, 0), pltpu.VMEM),
            ((MB, nodes, width), BF16, (1, TILE, width), lambda b, i: (b, i, 0), pltpu.HBM),
            ((groups, capacity, width), BF16, None, None),
        ],
        grid=(MB, nodes // TILE), after=after, barrier=FRONT_ID, vmem=20,
        scratch=[
            pltpu.VMEM((capacity, width), BF16),
            pltpu.SemaphoreType.DMA,
            pltpu.SemaphoreType.DMA((2, hops, HALVES)),
            pltpu.SemaphoreType.DMA((2, hops, HALVES)),
            pltpu.SemaphoreType.DMA((1 + 2 * hops, HALVES)),
            pltpu.SemaphoreType.DMA((1 + 2 * hops, HALVES)),
        ],
    )


def greet_mate(mate):
    barrier = pltpu.get_barrier_semaphore()
    pl.semaphore_signal(barrier, inc=1, device_id={"col": mate}, device_id_type=pl.DeviceIdType.MESH)
    pl.semaphore_wait(barrier, 1)


def place_kernel(groups, table_ref, slots_ref, weight_ref, mate_ref, rows_ref):
    owner = pl.program_id(0)

    @pl.when(owner == 0)
    def _():
        rows_ref[...] = jnp.zeros_like(rows_ref)

    put_rows(rows_ref, table_ref[STARTS + owner], slots_ref[0].astype(F32))

    @pl.when(owner == groups - 1)
    def _():
        width = weight_ref.shape[2]
        for block in range(weight_ref.shape[0]):
            source = pl.multiple_of((table_ref[COLUMN] ^ block) * width, width)
            rows = rows_ref[pl.ds(source, width), :].astype(BF16)
            weight_ref[block] = rows
            if block % 2:
                mate_ref[block // 2] = rows


def place(table, slots, after=()):
    groups, capacity, width = slots.shape
    blocks = D // width
    return launch(
        "place", functools.partial(place_kernel, groups), table,
        [(slots, (1, capacity, width), lambda i: (i, 0, 0))],
        [
            ((blocks, width, width), BF16, (blocks, width, width), lambda i: (0, 0, 0), pltpu.VMEM),
            ((blocks // 2, width, width), BF16, (blocks // 2, width, width), lambda i: (0, 0, 0), pltpu.VMEM),
        ],
        grid=(groups,), after=after, vmem=24, scratch=[pltpu.VMEM((D + capacity + SUBLANES, width), F32)],
    )


def batch_kernel(m, chunks, table_ref, *refs):
    matrix_hbm, scale_hbm, far_hbm, here_hbm, weight_hbm, for_mate_hbm, grad_hbm, bias_ref = refs[:8]
    refs = refs[8:]
    total_hbm, bias_sum_in = refs[:2] if m else (None, None)
    refs = refs[2:] if m else refs
    ended = m == MB - 1
    out_hbm, pre_hbm, mate_pre_hbm = refs[:3]
    away_hbm, refs = refs[3 : 3 + chunks], refs[3 + chunks :]
    mate_weight_hbm, refs = (refs[0], refs[1:]) if ended else (None, refs)
    results, refs = (refs[:2], refs[2:]) if ended else (refs[:1], refs[1:])
    bias_sum_ref, refs = refs[0], refs[1:]
    (
        matrix_ref, scale_ref, far_ref, mixed_ref, weight_ref, mate_weight_ref, grad_ref, out_ref, pre_ref, mate_pre_ref,
        away_ref, total_ref, load, store, send, receive,
    ) = refs[:16]
    parts = refs[16:]
    nodes, width = far_ref.shape
    wide, narrow = nodes // WIDE, nodes // TILE
    mate = partner(lax.axis_index("col"), 1)

    def at(index, size):
        return pl.ds(pl.multiple_of(index * size, size), size)

    def matrix_load(i):
        return pltpu.make_async_copy(
            matrix_hbm.at[m, :, at(i, WIDE)], matrix_ref.at[:, at(i, WIDE)], load.at[i]
        )

    loads = [
        pltpu.make_async_copy(source, target, load.at[wide + i])
        for i, (source, target) in enumerate(
            [
                (far_hbm, far_ref),
                (scale_hbm.at[m], scale_ref),
                (weight_hbm, weight_ref),
                (here_hbm.at[m], mixed_ref.at[0]),
                (grad_hbm.at[m], grad_ref),
            ]
            + ([(total_hbm, total_ref)] if m else [])
        )
    ]
    started = []

    def save(source, target):
        started.append(pltpu.make_async_copy(source, target, store.at[len(started)]))
        started[-1].start()

    def remote(source, target, number):
        return pltpu.make_async_remote_copy(
            src_ref=source,
            dst_ref=target,
            send_sem=send.at[number],
            recv_sem=receive.at[number],
            device_id={"col": mate},
            device_id_type=pl.DeviceIdType.MESH,
        )

    here_copy = remote(here_hbm.at[m], mixed_ref.at[1], 0)
    weight_copy = remote(for_mate_hbm, mate_weight_ref, 1)

    def there_copy(i):
        return remote(mixed_ref.at[2, at(i, WIDE)], mixed_ref.at[3, at(i, WIDE)], 2 + i)

    def pre_copy(i):
        return remote(pre_ref.at[at(i, TILE)], mate_pre_ref.at[at(i, TILE)], 2 + wide + i)

    loads[0].start()
    matrix_load(0).start()
    loads[1].start()
    for i in range(1, wide):
        matrix_load(i).start()
    for item in loads[2:]:
        item.start()
    greet_mate(mate)
    here_copy.start()
    loads[0].wait()
    loads[1].wait()

    @pl.loop(0, wide)
    def _(i):
        matrix_load(i).wait()
        rows = at(i, WIDE)
        there = product_rows(matrix_ref[:, rows], far_ref[...])
        mixed_ref[2, rows, :] = scaled(there, scale_ref[rows, :]).astype(BF16)
        there_copy(i).start()

    weight_copy.start()
    for item in loads[2:5]:
        item.wait()
    here_copy.wait_recv()
    bias_sum_ref[...] = bias_sum_in[...] if m else jnp.zeros_like(bias_sum_ref)
    for i in range(wide):
        there_copy(i).wait_recv()

    @pl.loop(0, narrow, unroll=UNROLL)
    def _(i):
        rows = at(i, TILE)
        preact = bias_ref[...]
        for block in range(4):
            preact = preact + product(mixed_ref[block, rows, :], weight_ref[block])
        row_ids = i * TILE + lax.broadcasted_iota(jnp.int32, preact.shape, 0)
        live = row_ids < table_ref[LIMITS + m]
        gate = jax.nn.sigmoid(preact)
        out_ref[rows, :] = jnp.where(live, preact * gate, 0.0).astype(BF16)
        slope = gate * (1.0 + preact * (1.0 - gate))
        grad_pre = jnp.where(live, grad_ref[rows, :].astype(F32) * slope, 0.0).astype(BF16)
        pre_ref[rows, :] = grad_pre
        pre_copy(i).start()
        bias_sum_ref[...] += jnp.sum(grad_pre.astype(F32), axis=0, keepdims=True)

    save(pre_ref, pre_hbm)
    save(out_ref, out_hbm)
    if m:
        loads[5].wait()

    @pl.loop(0, 4)
    def _(block):
        term = product_rows(mixed_ref[block], pre_ref[...])
        total_ref[block] = total_ref[block] + term if m else term

    if ended:
        half = width // 2
        upper = lax.axis_index("clus") % 2 == 1
        column = lax.axis_index("col")
        for block in range(4):
            source = partner(column, 1) if block % 2 else column
            source = partner(source, 2) if block >= 2 else source
            rows = at(source, width)
            low, high = total_ref[block, :, :half], total_ref[block, :, half:]
            parts[0][rows, :] = jnp.where(upper, high, low)
            parts[1][rows, :] = jnp.where(upper, low, high).astype(BF16)
        for part, result in zip(parts, results):
            save(part, result)
    else:
        save(total_ref, results[0])

    weight_copy.wait_recv()
    for i in range(narrow):
        pre_copy(i).wait_recv()
    save(mate_pre_ref, mate_pre_hbm)
    if ended:
        save(mate_weight_ref, mate_weight_hbm)
    step = width // chunks
    for i in range(wide):
        rows = slice(i * WIDE, (i + 1) * WIDE)
        away = product_back(pre_ref[rows, :], weight_ref[2]) + product_back(mate_pre_ref[rows, :], mate_weight_ref[1])
        away_ref[rows, :] = away.astype(BF16)
        for chunk in range(chunks):
            columns = slice(chunk * step, (chunk + 1) * step)
            save(away_ref.at[rows, columns], away_hbm[chunk].at[rows])
    here_copy.wait_send()
    weight_copy.wait_send()
    for i in range(wide):
        there_copy(i).wait_send()
    for i in range(narrow):
        pre_copy(i).wait_send()
    for item in started:
        item.wait()


def batch(table, m, matrix, scale, far, here, weight, for_mate, out_grad, bias, total, bias_sum, chunks, after=()):
    nodes, width = far.array.shape
    wide, narrow = nodes // WIDE, nodes // TILE
    flat = lambda i: (0, 0)
    ended = m == MB - 1
    parts = [((D, width // 2), F32), ((D, width // 2), BF16)] if ended else []
    results = [(*part, None, None) for part in parts]
    if not ended:
        results = [((4, width, width), F32, None, None, pltpu.VMEM)]
    return launch(
        f"batch{m}", functools.partial(batch_kernel, m, chunks), table,
        [(array, None, None) for array in (matrix, scale, far, here, weight, for_mate, out_grad)]
        + [(bias, (1, width), flat)]
        + ([(total, None, None), (bias_sum, (1, width), flat)] if m else []),
        [((nodes, width), BF16, None, None, pltpu.VMEM)]
        + [((nodes, width), BF16, None, None)] * 2
        + [((nodes, width // chunks), BF16, None, None)] * chunks
        + ([(for_mate.array.shape, BF16, None, None)] if ended else [])
        + results
        + [((1, width), F32, (1, width), flat)],
        after=after, barrier=BATCH_ID + m, vmem=34 if m == MB - 1 else 32,
        scratch=[
            pltpu.VMEM((nodes, nodes), BF16),
            pltpu.VMEM((nodes, LANES), F32),
            pltpu.VMEM((nodes, width), BF16),
            pltpu.VMEM((4, nodes, width), BF16),
            pltpu.VMEM(weight.array.shape, BF16),
            pltpu.VMEM(for_mate.array.shape, BF16),
            pltpu.VMEM((nodes, width), BF16),
            pltpu.VMEM((nodes, width), BF16),
            pltpu.VMEM((nodes, width), BF16),
            pltpu.VMEM((nodes, width), BF16),
            pltpu.VMEM((nodes, width), BF16),
            pltpu.VMEM((4, width, width), F32),
            pltpu.SemaphoreType.DMA((wide + 6,)),
            pltpu.SemaphoreType.DMA((6 + wide * chunks,)),
            pltpu.SemaphoreType.DMA((2 + wide + narrow,)),
            pltpu.SemaphoreType.DMA((2 + wide + narrow,)),
        ]
        + [pltpu.VMEM(*part) for part in parts],
    )


def scatter_job(m, columns, own_source, got_source, scale_source, matrix_source, grads_hbm, scratch, semaphores):
    own_ref, got_ref, scale_ref, matrix_ref, sum_ref, grad_ref = scratch
    steps = matrix_ref.shape[0] // WIDE
    loads = [
        pltpu.make_async_copy(source, target, semaphores.at[i])
        for i, (source, target) in enumerate(
            [(own_source.at[:, columns], own_ref), (got_source, got_ref), (scale_source.at[m], scale_ref)]
        )
    ]
    tiles, stores = [], []
    for i in range(steps):
        rows = pl.ds(i * WIDE, WIDE)
        tiles.append(pltpu.make_async_copy(matrix_source.at[rows], matrix_ref.at[rows], semaphores.at[3 + i]))
        stores.append(
            pltpu.make_async_copy(grad_ref.at[rows], grads_hbm.at[m, rows, columns], semaphores.at[3 + steps + i])
        )

    def work():
        for item in loads:
            item.wait()
        grad_mixed = (own_ref[...].astype(F32) + got_ref[...].astype(F32)).astype(BF16)
        sum_ref[...] = scaled(grad_mixed.astype(F32), scale_ref[...]).astype(BF16)
        for i in range(steps):
            tiles[i].wait()
            rows = slice(i * WIDE, (i + 1) * WIDE)
            grad_ref[rows, :] = product(matrix_ref[rows, :], sum_ref[...]).astype(BF16)
            stores[i].start()

    return loads + tiles, work, stores


def scatter_scratch(nodes, width):
    return [
        pltpu.VMEM((nodes, width), BF16),
        pltpu.VMEM((nodes, width), BF16),
        pltpu.VMEM((nodes, LANES), F32),
        pltpu.VMEM((nodes, nodes), BF16),
        pltpu.VMEM((nodes, width), BF16),
        pltpu.VMEM((nodes, width), BF16),
        pltpu.SemaphoreType.DMA((3 + 2 * (nodes // WIDE),)),
    ]


def scatter_kernel(m, chunk, own_hbm, got_hbm, scale_hbm, matrix_hbm, grads_hbm, *refs):
    width = got_hbm.shape[1]
    loads, work, stores = scatter_job(
        m, pl.ds(chunk * width, width), own_hbm, got_hbm, scale_hbm, matrix_hbm, grads_hbm, refs[:6], refs[6]
    )
    for item in loads:
        item.start()
    work()
    for item in stores:
        item.wait()


def scatter(m, chunk, own, got, scale, matrix, grads, after=()):
    nodes, width = own.array.shape
    return launch(
        f"scatter{m}_{chunk}", functools.partial(scatter_kernel, m, chunk), None,
        [(array, None, None) for array in (own, got, scale, matrix)],
        [((MB, nodes, width), BF16, None, None)],
        after=after, alias=(grads, 0), scratch=scatter_scratch(nodes, got.array.shape[1]),
    )[0]


def sum_kernel(groups, capacity, table_ref, *refs):
    keep_hbm, sent_hbm, bias_ref, weight_hbm, mate_weight_hbm = refs[:5]
    pre_hbm, mate_hbm, refs = refs[5 : 5 + MB], refs[5 + MB : 5 + 2 * MB], refs[5 + 2 * MB :]
    own_ref, got_ref, bias_out_ref, back_hbm, refs = *refs[:4], refs[4:]
    pre_ref, mate_ref, weights_ref, back_ref, load, store, refs = *refs[:6], refs[6:]
    keep_ref, pair_ref, land_ref, out_ref, total_ref, end_out_ref, end_in_ref, row_ref = refs[:8]
    pair_send, pair_receive, line_send, line_receive, row_send, row_receive = refs[8:]
    own = lax.axis_index("clus")
    place, pairs = own // 2, groups // 2
    other = partner(own, 1)
    rows = keep_ref.shape[0]
    size = rows // CHUNKS
    ahead, behind = place + 1 < pairs, place >= 1

    def remote(source, target, sent, received, device):
        return pltpu.make_async_remote_copy(
            src_ref=source,
            dst_ref=target,
            send_sem=sent,
            recv_sem=received,
            device_id={"clus": device},
            device_id_type=pl.DeviceIdType.MESH,
        )

    def part(chunk):
        return pl.ds(pl.multiple_of(chunk * size, size), size)

    def pair_copy(chunk):
        return remote(
            sent_hbm.at[part(chunk)], pair_ref.at[part(chunk)], pair_send.at[chunk], pair_receive.at[chunk], other
        )

    def line_copy(direction, chunk):
        return remote(
            out_ref.at[direction, part(chunk)], land_ref.at[direction, part(chunk)],
            line_send.at[direction, chunk], line_receive.at[direction, chunk],
            own + 2 if direction == 0 else own - 2,
        )

    def row_copy(number):
        device = (other, own + 2, own - 2)[number]
        return remote(row_ref.at[number], row_ref.at[3 + number], row_send.at[number], row_receive.at[number], device)

    end_copy = remote(end_out_ref, end_in_ref, pair_send.at[CHUNKS], pair_receive.at[CHUNKS], other)

    nodes = pre_ref.shape[1]
    tiles = nodes // WIDE
    loads = [
        pltpu.make_async_copy(source, target, load.at[i])
        for i, (source, target) in enumerate(
            [(keep_hbm, keep_ref), (weight_hbm.at[0], weights_ref.at[0]), (mate_weight_hbm.at[0], weights_ref.at[1])]
            + [(source, pre_ref.at[m]) for m, source in enumerate(pre_hbm)]
            + [(source, mate_ref.at[m]) for m, source in enumerate(mate_hbm)]
        )
    ]
    stores = [pltpu.make_async_copy(back_ref.at[m], back_hbm.at[m], store.at[m]) for m in range(MB)]

    def back(number):
        m, i = number // tiles, number % tiles
        if i == 0:
            loads[3 + m].wait()
            loads[3 + MB + m].wait()
        down = slice(i * WIDE, (i + 1) * WIDE)
        term = product_back(pre_ref[m, down, :], weights_ref[0]) + product_back(mate_ref[m, down, :], weights_ref[1])
        back_ref[m, down, :] = term.astype(BF16)
        if i == tiles - 1:
            stores[m].start()

    land_ref[...] = jnp.zeros_like(land_ref)
    row_ref[...] = jnp.zeros_like(row_ref)
    row_ref[0] = bias_ref[...]
    for item in loads:
        item.start()
    barrier = pltpu.get_barrier_semaphore()

    def greet(index):
        pl.semaphore_signal(barrier, inc=1, device_id={"clus": index}, device_id_type=pl.DeviceIdType.MESH)

    greet(other)

    @pl.when(ahead)
    def _():
        greet(own + 2)

    @pl.when(behind)
    def _():
        greet(own - 2)

    pl.semaphore_wait(barrier, 1 + jnp.where(ahead, 1, 0) + jnp.where(behind, 1, 0))
    row_copy(0).start()
    for chunk in range(CHUNKS):
        pair_copy(chunk).start()
    for item in loads[:3]:
        item.wait()

    def pass_on(direction, chunk, first):
        sums = keep_ref[part(chunk), :]
        if not first:
            sums = sums + land_ref[direction, part(chunk), :].astype(F32)
        out_ref[direction, part(chunk), :] = sums.astype(BF16)
        line_copy(direction, chunk).start()

    def pass_row(direction, first):
        row_ref[1 + direction] = row_ref[0] if first else row_ref[0] + row_ref[4 + direction]
        row_copy(1 + direction).start()

    steps = CHUNKS + pairs - 1
    for step in range(steps):
        if step < CHUNKS:
            pair_copy(step).wait_recv()
            keep_ref[part(step), :] += pair_ref[part(step), :].astype(F32)
            if step == 0:
                row_copy(0).wait()
                row_ref[0] += row_ref[3]
            for direction, (here, there) in enumerate(((behind, ahead), (ahead, behind))):

                @pl.when(jnp.logical_not(here) & there)
                def _(direction=direction, step=step):
                    pass_on(direction, step, True)
                    if step == 0:
                        pass_row(direction, True)

        for direction, (here, there) in enumerate(((behind, ahead), (ahead, behind))):
            chunk = step - (place if direction == 0 else pairs - 1 - place)

            @pl.when(here & (chunk >= 0) & (chunk < CHUNKS))
            def _(direction=direction, chunk=chunk, there=there):
                line_copy(direction, chunk).wait_recv()

                @pl.when(there)
                def _():
                    pass_on(direction, chunk, False)

                @pl.when(chunk == 0)
                def _():
                    row_copy(1 + direction).wait_recv()

                    @pl.when(there)
                    def _():
                        pass_row(direction, False)

        for number in range(step * MB * tiles // steps, (step + 1) * MB * tiles // steps):
            back(number)

    total_ref[:rows, :] = keep_ref[...] + (land_ref[0].astype(F32) + land_ref[1].astype(F32))
    total_ref[rows:, :] = jnp.zeros((capacity + SUBLANES, keep_ref.shape[1]), F32)
    end_out_ref[...] = take_rows(total_ref, table_ref[STARTS + other], capacity, rows - 1).astype(BF16)
    end_copy.start()
    own_ref[...] = take_rows(total_ref, table_ref[STARTS + own], capacity, rows - 1)
    bias_out_ref[...] = row_ref[0] + (row_ref[4] + row_ref[5])
    end_copy.wait()
    got_ref[...] = end_in_ref[...]
    for chunk in range(CHUNKS):
        pair_copy(chunk).wait_send()
    for direction, there in enumerate((ahead, behind)):

        @pl.when(there)
        def _(direction=direction):
            row_copy(1 + direction).wait_send()
            for chunk in range(CHUNKS):
                line_copy(direction, chunk).wait_send()

    for item in stores:
        item.wait()


def sum_over_owners(table, groups, capacity, keep, sent, bias, weight, mate_weight, pres, mates, after=()):
    rows, half = keep.shape
    nodes, width = pres[0].shape
    flat = lambda i: (0, 0)
    shape = (capacity, half)
    return launch(
        "sum", functools.partial(sum_kernel, groups, capacity), table,
        [(array, None, None) for array in (keep, sent)]
        + [(bias, bias.shape, flat)]
        + [(array, None, None) for array in (weight, mate_weight, *pres, *mates)],
        [
            (shape, F32, shape, flat),
            (shape, BF16, shape, flat),
            (bias.shape, F32, bias.shape, flat),
            ((MB, nodes, width), BF16, None, None),
        ],
        after=after, barrier=SUM_ID, vmem=34,
        scratch=[
            pltpu.VMEM((MB, nodes, width), BF16),
            pltpu.VMEM((MB, nodes, width), BF16),
            pltpu.VMEM((2, width, width), BF16),
            pltpu.VMEM((MB, nodes, width), BF16),
            pltpu.SemaphoreType.DMA((3 + 2 * MB,)),
            pltpu.SemaphoreType.DMA((MB,)),
            pltpu.VMEM((rows, half), F32),
            pltpu.VMEM((rows, half), BF16),
            pltpu.VMEM((2, rows, half), BF16),
            pltpu.VMEM((2, rows, half), BF16),
            pltpu.VMEM((rows + capacity + SUBLANES, half), F32),
            pltpu.VMEM(shape, BF16),
            pltpu.VMEM(shape, BF16),
            pltpu.VMEM((6, 1, width), F32),
            pltpu.SemaphoreType.DMA((CHUNKS + 1,)),
            pltpu.SemaphoreType.DMA((CHUNKS + 1,)),
            pltpu.SemaphoreType.DMA((2, CHUNKS)),
            pltpu.SemaphoreType.DMA((2, CHUNKS)),
            pltpu.SemaphoreType.DMA((3,)),
            pltpu.SemaphoreType.DMA((3,)),
        ],
    )


def adamw_update(current, first_moment, second_moment, gradient, step_rate):
    first_new = BETA_ONE * first_moment + (1.0 - BETA_ONE) * gradient
    second_new = BETA_TWO * second_moment + (1.0 - BETA_TWO) * gradient * gradient
    fixed_first = first_new / (1.0 - BETA_ONE**STEP)
    fixed_second = second_new / (1.0 - BETA_TWO**STEP)
    updated = current - step_rate * (
        fixed_first / (jnp.sqrt(fixed_second) + EPSILON) + DECAY * current
    )
    return (updated, first_new, second_new)


def finish_kernel(groups, table_ref, *refs):
    done = MB - 1
    own_ref, got_ref, bias_grad_ref, biases = refs[0], refs[1], refs[2], refs[3:6]
    weights_hbm, out_parts, refs = refs[6:9], refs[9 : 9 + MB], refs[9 + MB :]
    back_hbm, gots, (scale_hbm, matrix_hbm), refs = refs[0], refs[1 : 1 + done], refs[1 + done : 3 + done], refs[3 + done :]
    updated_hbm, bias_outs, (out_hbm, grads_hbm, last_back_ref, last_matrix_ref), refs = refs[:3], refs[3:6], refs[6:10], refs[10:]
    weights, (weight_load, weight_store, store), refs = refs[:3], refs[3:6], refs[6:]
    jobs = [
        scatter_job(
            m, pl.ds(0, back_hbm.shape[2]), back_hbm.at[m], gots[m], scale_hbm, matrix_hbm.at[m], grads_hbm,
            refs[7 * m : 7 * m + 6], refs[7 * m + 6],
        )
        for m in range(done)
    ]
    weight_loads = [
        pltpu.make_async_copy(source, target, weight_load.at[i])
        for i, (source, target) in enumerate(zip(weights_hbm, weights))
    ]
    weight_stores = [
        pltpu.make_async_copy(source, target, weight_store.at[i])
        for i, (source, target) in enumerate(zip(weights, updated_hbm))
    ]
    moves = [
        pltpu.make_async_copy(source, target, store.at[i])
        for i, (source, target) in enumerate(
            [(part, out_hbm.at[m]) for m, part in enumerate(out_parts)]
            + [(back_hbm.at[done], last_back_ref), (matrix_hbm.at[done], last_matrix_ref)]
        )
    ]
    for item in jobs[0][0] + weight_loads:
        item.start()
    for later, _, _ in jobs[1:]:
        for item in later:
            item.start()
    for item in moves:
        item.start()
    jobs[0][1]()

    for item in weight_loads:
        item.wait()
    rows, width = weights[0].shape
    half = width // 2
    strip = min(rows, TILE // 2)
    own = table_ref[GROUP]
    for first in range(0, rows, strip):
        row_ids = first + lax.broadcasted_iota(jnp.int32, (strip, half), 0)
        used = row_ids < table_ref[STARTS + groups + own]
        down = slice(first, first + strip)
        for side in range(2):
            mine = (own & 1) == side
            here, there = own_ref[down, :], got_ref[down, :].astype(F32)
            columns = slice(side * half, (side + 1) * half)
            results = adamw_update(*(ref[down, columns] for ref in weights), jnp.where(mine, here, there), RATE_WEIGHT)
            for ref, result in zip(weights, results):
                ref[down, columns] = jnp.where(used, result, 0.0)
    for item in weight_stores:
        item.start()
    results = adamw_update(*(ref[...] for ref in biases), bias_grad_ref[...], RATE_BIAS)
    for ref, result in zip(bias_outs, results):
        ref[...] = result

    for _, work, _ in jobs[1:]:
        work()
    for item in weight_stores + moves:
        item.wait()
    for _, _, stores in jobs:
        for item in stores:
            item.wait()


def finish(table, groups, mine, other, bias_grad, biases, weights, outputs, backs, gots, scale, matrix, after=()):
    capacity, width = weights[0].shape
    nodes = outputs[0].array.shape[0]
    fixed = lambda i: (0, 0)
    scratch = [pltpu.VMEM((capacity, width), F32)] * 3 + [
        pltpu.SemaphoreType.DMA((3,)),
        pltpu.SemaphoreType.DMA((3,)),
        pltpu.SemaphoreType.DMA((MB + 2,)),
    ]
    for _ in gots:
        scratch += scatter_scratch(nodes, width)
    return launch(
        "finish", functools.partial(finish_kernel, groups), table,
        [(array, array.array.shape, fixed) for array in (mine, other)]
        + [(array, (1, width), fixed) for array in (bias_grad, *biases)]
        + [(array, None, None) for array in (*weights, *outputs, backs, *gots, scale, matrix)],
        [((capacity, width), F32, None, None)] * 3
        + [((1, width), F32, (1, width), fixed)] * 3
        + [((MB, nodes, width), BF16, None, None)] * 2
        + [((nodes, width), BF16, None, None, pltpu.VMEM), ((nodes, nodes), BF16, None, None, pltpu.VMEM)],
        after=after, scratch=scratch, vmem=32,
    )


def shards(
    features,
    neighbours,
    node_counts,
    row_counts,
    master_weight,
    weight_first,
    weight_second,
    master_bias,
    bias_first,
    bias_second,
    out_grad,
):
    groups = lax.axis_size("clus")
    capacity, width = master_weight.shape
    owner_ids = jnp.arange(groups, dtype=jnp.int32)
    starts = jnp.sum(jnp.where(owner_ids[None, :] < owner_ids[:, None], row_counts[None, :], 0), axis=1)
    table = jnp.concatenate(
        [
            jnp.stack([lax.axis_index("clus"), lax.axis_index("col")]).astype(jnp.int32),
            node_counts[:, 0],
            starts.astype(jnp.int32),
            row_counts,
        ]
    )
    bias_row, bias_first_row, bias_second_row = (
        array.reshape(1, width) for array in (master_bias, bias_first, bias_second)
    )

    picked = pick_first(features)
    picked = picked + pick(features, tuple(range(1, MB)), [Kept(picked[0])])
    far = [Kept(flip(array, "col", 2), None) for array in picked]

    matrix, scale, here, slots = front(
        table, groups, master_weight, jnp.swapaxes(neighbours, 1, 2), features, [picked[-1]]
    )
    scale = Kept(scale)
    weight, for_mate = (Kept(array) for array in place(table, slots))
    last = for_mate
    total, bias_sum = None, None
    outputs, pres, mates, away = [], [], [], []
    for m in range(MB):
        chunks = 2 if m == MB - 1 else 1
        out_m, pre_m, mate_m, *rest = batch(
            table, m, matrix, scale, far[m], here, weight, for_mate, out_grad, bias_row, total, bias_sum, chunks,
            [last],
        )
        outputs.append(Kept(out_m))
        pres.append(pre_m)
        mates.append(mate_m)
        away.append([Kept(flip(chunk, "col", 2), None) for chunk in rest[:chunks]])
        total, bias_sum = Kept(rest[chunks]), rest[-1]
        last = bias_sum

    mate_weight, keep, sent, bias_sum = rest[chunks:]
    mine, other, bias_total, backs = sum_over_owners(
        table, groups, capacity, keep, sent, bias_sum, weight, mate_weight, pres, mates, [last]
    )
    *updated, outputs, input_grads, last_back, last_matrix = finish(
        table, groups, Kept(mine, None), Kept(other, None), bias_total, (bias_row, bias_first_row, bias_second_row),
        (master_weight, weight_first, weight_second), outputs, backs, [part[0] for part in away[:-1]],
        scale, matrix, [bias_total],
    )
    for chunk, got in enumerate(away[-1]):
        input_grads = scatter(MB - 1, chunk, Kept(last_back), got, scale, Kept(last_matrix), input_grads)
    return (outputs, input_grads, *updated[:3], *(row.reshape(width) for row in updated[3:]))


def solution(mesh):
    in_specs = (
        P(None, "clus", "col"),
        P(None, "clus", None),
        P(None, "clus"),
        P(),
        P("clus", "col"),
        P("clus", "col"),
        P("clus", "col"),
        P("col"),
        P("col"),
        P("col"),
        P(None, "clus", "col"),
    )
    out_specs = (
        P(None, "clus", "col"),
        P(None, "clus", "col"),
        P("clus", "col"),
        P("clus", "col"),
        P("clus", "col"),
        P("col"),
        P("col"),
        P("col"),
    )
    return jax.shard_map(shards, mesh=mesh, in_specs=in_specs, out_specs=out_specs, check_vma=False)
```

```python
import functools

import jax
import jax.numpy as jnp
from jax import lax
from jax.experimental import pallas as pl
from jax.experimental.pallas import tpu as pltpu
from jax.sharding import PartitionSpec as P

D = 2048
MB = 3
STEP = 10

BETA_ONE = 0.9
BETA_TWO = 0.95
EPSILON = 1e-08
DECAY = 0.1
RATE_WEIGHT = 0.06
RATE_BIAS = 0.6

LANES = 128
DIGIT_BITS = 5
DIGITS = 6
STRIP = 32
SUBLANES = 8
TILE = 256
WIDE = 512
HALVES = 2
PIECES = 4
UNROLL = 3
CHUNKS = 8
MIB = 1024 * 1024
SMALL = 1 << 16

GROUP, COLUMN, LIMITS = 0, 1, 2
STARTS = LIMITS + MB

FRONT_ID, SUM_ID, BATCH_ID = 1, 2, 3

F32, BF16 = jnp.float32, jnp.bfloat16


class Kept:
    def __init__(self, array, space=pltpu.VMEM):
        self.array, self.space = array, space


def located(item):
    if isinstance(item, Kept):
        return pltpu.with_memory_space_constraint(item.array, item.space) if item.space else item.array
    return pltpu.with_memory_space_constraint(item, pltpu.HBM) if item.size > SMALL else item


def launch(name, body, table, ins, outs, grid=(1,), after=(), alias=None, scratch=(), barrier=None, vmem=16):
    tables = [] if table is None else [table]

    def spec(block, index):
        if block is None:
            return pl.BlockSpec(memory_space=pl.ANY)
        return pl.BlockSpec(block, lambda *a: index(*a[: len(grid)]))

    unread = ([alias[0]] if alias else []) + [array for array in after if alias is None or array is not alias[0]]

    def kernel(*refs):
        table_refs, refs = refs[: len(tables)], refs[len(tables) :]
        body(*table_refs, *refs[: len(ins)], *refs[len(ins) + len(unread) :])

    return pl.pallas_call(
        kernel,
        grid_spec=pltpu.PrefetchScalarGridSpec(
            num_scalar_prefetch=len(tables),
            grid=grid,
            in_specs=[spec(block, index) for _, block, index in ins]
            + [pl.BlockSpec(memory_space=pl.ANY)] * len(unread),
            out_specs=[spec(out[2], out[3]) for out in outs],
            scratch_shapes=list(scratch),
        ),
        out_shape=[
            (out[4] if len(out) > 4 else pltpu.HBM if out[2] is None else jax.ShapeDtypeStruct)(out[0], out[1])
            for out in outs
        ],
        input_output_aliases={len(tables) + len(ins): alias[1]} if alias else {},
        compiler_params=pltpu.CompilerParams(
            vmem_limit_bytes=vmem * MIB, collective_id=barrier, has_side_effects=barrier is not None
        ),
        cost_estimate=pl.CostEstimate(flops=1, bytes_accessed=1, transcendentals=0),
        name=name,
    )(*tables, *(located(item[0]) for item in ins), *(located(item) for item in unread))


def flip(values, axis, bit):
    size = lax.axis_size(axis)
    return lax.ppermute(values, axis, [(i, i ^ bit) for i in range(size)])


def partner(index, bit):
    return index + bit * (1 - 2 * ((index // bit) % 2))


def product(left, right):
    return jnp.dot(left, right, preferred_element_type=F32)


def product_back(left, right):
    return lax.dot_general(left, right, (((1,), (1,)), ((), ())), preferred_element_type=F32)


def product_rows(left, right):
    return lax.dot_general(left, right, (((0,), (0,)), ((), ())), preferred_element_type=F32)


def scaled(values, scale):
    return values * jnp.concatenate([scale] * (values.shape[1] // LANES), axis=1)


def put_rows(ref, first, rows):
    base = pl.multiple_of((first // SUBLANES) * SUBLANES, SUBLANES)
    offset = first - base
    moved = jnp.concatenate([rows, jnp.zeros((SUBLANES, rows.shape[1]), rows.dtype)], axis=0)
    wanted = jnp.broadcast_to(offset, moved.shape)
    for bit in (1, 2, 4):
        moved = jnp.where((wanted & bit) != 0, pltpu.roll(moved, bit, 0), moved)
    head = ref[pl.ds(base, SUBLANES), :]
    row_ids = lax.broadcasted_iota(jnp.int32, head.shape, 0)
    ref[pl.ds(base, SUBLANES), :] = jnp.where(row_ids < offset, head, moved[:SUBLANES])
    ref[pl.ds(pl.multiple_of(base + SUBLANES, SUBLANES), rows.shape[0]), :] = moved[SUBLANES:]


def take_rows(ref, first, count, largest):
    bit = 1 << (largest.bit_length() - 1)
    rows = ref[...]
    while bit:
        length = count + max(bit, SUBLANES)
        if bit >= SUBLANES:
            moved = rows[bit : bit + length]
            missing = length - moved.shape[0]
            if missing:
                moved = jnp.concatenate([moved, jnp.zeros((missing, rows.shape[1]), rows.dtype)], axis=0)
        else:
            moved = pltpu.roll(rows, length - bit, 0)
        chosen = (jnp.broadcast_to(first, (length, rows.shape[1])) & bit) != 0
        rows = jnp.where(chosen, moved, rows[:length])
        bit //= 2
    return rows[:count]


def relay(sources, targets, buffers, load, store):
    def piece(ref, i):
        rows = ref.shape[0] // PIECES
        return ref.at[pl.ds(i * rows, rows)]

    loads, stores = [], []
    for number, (source, target, buffer) in enumerate(zip(sources, targets, buffers)):
        for i in range(PIECES):
            place = number * PIECES + i
            loads.append(pltpu.make_async_copy(piece(source, i), piece(buffer, i), load.at[place]))
            stores.append(pltpu.make_async_copy(piece(buffer, i), piece(target, i), store.at[place]))
    return loads, stores


def first_kernel(source_hbm, target_ref, semaphore):
    copy = pltpu.make_async_copy(source_hbm.at[0], target_ref, semaphore)
    copy.start()
    copy.wait()


def pick_first(stacked):
    return launch(
        "first", first_kernel, None,
        [(stacked, None, None)], [(stacked.shape[1:], stacked.dtype, None, None, pltpu.VMEM)],
        scratch=[pltpu.SemaphoreType.DMA],
    )


def pick_kernel(batches, source_ref, *refs):
    targets, (buffer_ref, load, store) = refs[:-3], refs[-3:]
    loads, stores = relay(
        [source_ref.at[m] for m in batches], targets, [buffer_ref.at[i] for i in range(len(batches))], load, store
    )
    for item in loads:
        item.start()
    for item, onward in zip(loads, stores):
        item.wait()
        onward.start()
    for item in stores:
        item.wait()


def pick(stacked, batches, after=()):
    count = len(batches)
    return launch(
        f"pick{batches[0]}", functools.partial(pick_kernel, batches), None,
        [(stacked, None, None)], [(stacked.shape[1:], stacked.dtype, None, None)] * count,
        after=after,
        scratch=[
            pltpu.VMEM((count, *stacked.shape[1:]), stacked.dtype),
            pltpu.SemaphoreType.DMA((count * PIECES,)),
            pltpu.SemaphoreType.DMA((count * PIECES,)),
        ],
    )


def count_tile(limit, first, neighbour_ref, matrix_ref, scale_ref, lanes):
    nodes = matrix_ref.shape[1]
    words = -(-(nodes // LANES) // DIGITS)
    entries = neighbour_ref[0, :, lanes]
    node_ids = first + lax.broadcasted_iota(jnp.int32, entries.shape, 1)
    valid = (entries < limit) & (node_ids < limit)
    low = entries & (LANES - 1)
    high = entries >> 7
    digits = []
    for word in range(words):
        inside = valid & (high >= word * DIGITS) & (high < (word + 1) * DIGITS)
        shift = jnp.where(inside, (high - word * DIGITS) * DIGIT_BITS, 0)
        digits.append(jnp.where(inside, jnp.left_shift(1, shift), 0))
    for strip in range(LANES // STRIP):
        row_ids = strip * STRIP + lax.broadcasted_iota(jnp.int32, (STRIP, LANES), 0)
        sums = [jnp.zeros((STRIP, LANES), jnp.int32) for _ in range(words)]
        for entry in range(entries.shape[0]):
            hit = row_ids == low[entry : entry + 1, :]
            for word in range(words):
                sums[word] = sums[word] + jnp.where(hit, digits[word][entry : entry + 1, :], 0)
        for block in range(nodes // LANES):
            word, digit = block // DIGITS, block % DIGITS
            count = jnp.right_shift(sums[word], digit * DIGIT_BITS) & ((1 << DIGIT_BITS) - 1)
            rows = slice(block * LANES + strip * STRIP, block * LANES + (strip + 1) * STRIP)
            matrix_ref[0, rows, lanes] = count.astype(F32).astype(BF16)
    rows = pl.ds(pl.multiple_of(first, LANES), LANES)
    square = matrix_ref[0, rows, lanes].astype(F32)
    on_diagonal = lax.broadcasted_iota(jnp.int32, square.shape, 0) == lax.broadcasted_iota(jnp.int32, square.shape, 1)
    matrix_ref[0, rows, lanes] = jnp.where(on_diagonal, 2.0 * square + 2.0, square).astype(BF16)
    degree = 1.0 + jnp.sum(valid.astype(F32), axis=0, keepdims=True)
    factor = (node_ids[:1] < limit).astype(F32) / degree
    scale_ref[0, lanes, :] = jnp.transpose(jnp.broadcast_to(factor, (LANES, LANES)))


def front_kernel(
    groups, total, table_ref, master_ref, neighbour_ref, feature_ref, matrix_ref, scale_ref, mixed_ref, slots_ref,
    block_ref, local_semaphore, line_send, line_receive, pair_send, pair_receive,
):
    batch, tile_id = pl.program_id(0), pl.program_id(1)
    tiles = pl.num_programs(1)
    step = batch * tiles + tile_id
    own = lax.axis_index("clus")
    place, side = own // 2, own % 2
    pairs = groups // 2
    other = partner(own, 1)

    def rows_of(half):
        size = block_ref.shape[0] // HALVES
        return pl.ds(half * size, size)

    def remote(source, target, sent, received, device):
        return pltpu.make_async_remote_copy(
            src_ref=source,
            dst_ref=target,
            send_sem=sent,
            recv_sem=received,
            device_id={"clus": device},
            device_id_type=pl.DeviceIdType.MESH,
        )

    def origin_of(direction, hop):
        return place - 1 - hop if direction == 0 else place + 1 + hop

    def line_copy(direction, hop, half):
        slot = (place - hop if direction == 0 else place + hop) * 2 + side
        target = slots_ref.at[slot, rows_of(half)]
        return remote(
            block_ref.at[rows_of(half)] if hop == 0 else target, target,
            line_send.at[direction, hop, half], line_receive.at[direction, hop, half],
            own + 2 if direction == 0 else own - 2,
        )

    def sends(direction, hop):
        if direction == 0:
            return (place - hop >= 0) & (place + 1 < pairs)
        return (place + hop < pairs) & (place - 1 >= 0)

    def arrives(direction, hop):
        return place - 1 - hop >= 0 if direction == 0 else place + 1 + hop < pairs

    def arrival(direction, hop, half):
        target = slots_ref.at[origin_of(direction, hop) * 2 + side, rows_of(half)]
        return remote(
            target, target, line_send.at[direction, hop, half], line_receive.at[direction, hop, half], other
        )

    def pair_copy(direction, hop, half):
        slot = own if hop < 0 else origin_of(direction, hop) * 2 + side
        number = 0 if hop < 0 else 1 + 2 * hop + direction
        target = slots_ref.at[slot, rows_of(half)]
        return remote(
            block_ref.at[rows_of(half)] if hop < 0 else target, target,
            pair_send.at[number, half], pair_receive.at[number, half], other,
        )

    def pair_arrival(direction, hop, half):
        slot = other if hop < 0 else origin_of(direction, hop) * 2 + 1 - side
        number = 0 if hop < 0 else 1 + 2 * hop + direction
        target = slots_ref.at[slot, rows_of(half)]
        return remote(target, target, pair_send.at[number, half], pair_receive.at[number, half], other)

    local_copy = pltpu.make_async_copy(block_ref, slots_ref.at[own], local_semaphore)
    hops = pairs - 1

    @pl.when(step == 0)
    def _():
        barrier = pltpu.get_barrier_semaphore()

        def greet(index):
            pl.semaphore_signal(barrier, inc=1, device_id={"clus": index}, device_id_type=pl.DeviceIdType.MESH)

        greet(other)

        @pl.when(place + 1 < pairs)
        def _():
            greet(own + 2)

        @pl.when(place - 1 >= 0)
        def _():
            greet(own - 2)

        pl.semaphore_wait(barrier, 1 + jnp.where(place + 1 < pairs, 1, 0) + jnp.where(place - 1 >= 0, 1, 0))
        block_ref[...] = master_ref[...].astype(BF16)
        for half in range(HALVES):
            for direction in range(2):
                pl.when(sends(direction, 0))(line_copy(direction, 0, half).start)
            pair_copy(0, -1, half).start()
        local_copy.start()

    limit = table_ref[LIMITS + batch]
    tile = mixed_ref.shape[1]
    for part in range(tile // LANES):
        first = tile_id * tile + part * LANES
        count_tile(limit, first, neighbour_ref, matrix_ref, scale_ref, slice(part * LANES, (part + 1) * LANES))
    mixed_ref[0] = scaled(product_rows(matrix_ref[0], feature_ref[0]), scale_ref[0]).astype(BF16)

    for event in range(hops * HALVES):
        hop, half = event // HALVES, event % HALVES

        @pl.when(step == min(total - 1, ((event + 1) * total) // (hops * HALVES)))
        def _(hop=hop, half=half):
            for direction in range(2):

                @pl.when(arrives(direction, hop))
                def _(direction=direction):
                    arrival(direction, hop, half).wait_recv()
                    pair_copy(direction, hop, half).start()

                if hop + 1 < hops:
                    pl.when(sends(direction, hop + 1))(line_copy(direction, hop + 1, half).start)

    @pl.when(step == total - 1)
    def _():
        local_copy.wait()
        for half in range(HALVES):
            pair_copy(0, -1, half).wait_send()
            pair_arrival(0, -1, half).wait_recv()
            for hop in range(hops):
                for direction in range(2):
                    pl.when(sends(direction, hop))(line_copy(direction, hop, half).wait_send)

                    @pl.when(arrives(direction, hop))
                    def _(direction=direction, hop=hop, half=half):
                        pair_copy(direction, hop, half).wait_send()
                        pair_arrival(direction, hop, half).wait_recv()


def front(table, groups, master, neighbours, features, after=()):
    _, entries, nodes = neighbours.shape
    capacity, width = master.shape
    hops = groups // 2 - 1
    steps = MB * (nodes // TILE)
    return launch(
        "front", functools.partial(front_kernel, groups, steps), table,
        [
            (master, (capacity, width), lambda b, i: (0, 0)),
            (neighbours, (1, entries, TILE), lambda b, i: (b, 0, i)),
            (features, (1, nodes, width), lambda b, i: (b, 0, 0)),
        ],
        [
            ((MB, nodes, nodes), BF16, (1, nodes, TILE), lambda b, i: (b, 0, i), pltpu.HBM),
            ((MB, nodes, LANES), F32, (1, TILE, LANES), lambda b, i: (b, i, 0), pltpu.VMEM),
            ((MB, nodes, width), BF16, (1, TILE, width), lambda b, i: (b, i, 0), pltpu.HBM),
            ((groups, capacity, width), BF16, None, None),
        ],
        grid=(MB, nodes // TILE), after=after, barrier=FRONT_ID, vmem=20,
        scratch=[
            pltpu.VMEM((capacity, width), BF16),
            pltpu.SemaphoreType.DMA,
            pltpu.SemaphoreType.DMA((2, hops, HALVES)),
            pltpu.SemaphoreType.DMA((2, hops, HALVES)),
            pltpu.SemaphoreType.DMA((1 + 2 * hops, HALVES)),
            pltpu.SemaphoreType.DMA((1 + 2 * hops, HALVES)),
        ],
    )


def greet_mate(mate):
    barrier = pltpu.get_barrier_semaphore()
    pl.semaphore_signal(barrier, inc=1, device_id={"col": mate}, device_id_type=pl.DeviceIdType.MESH)
    pl.semaphore_wait(barrier, 1)


def place_kernel(groups, table_ref, slots_ref, weight_ref, mate_ref, rows_ref):
    owner = pl.program_id(0)

    @pl.when(owner == 0)
    def _():
        rows_ref[...] = jnp.zeros_like(rows_ref)

    put_rows(rows_ref, table_ref[STARTS + owner], slots_ref[0].astype(F32))

    @pl.when(owner == groups - 1)
    def _():
        width = weight_ref.shape[2]
        for block in range(weight_ref.shape[0]):
            source = pl.multiple_of((table_ref[COLUMN] ^ block) * width, width)
            rows = rows_ref[pl.ds(source, width), :].astype(BF16)
            weight_ref[block] = rows
            if block % 2:
                mate_ref[block // 2] = rows


def place(table, slots, after=()):
    groups, capacity, width = slots.shape
    blocks = D // width
    return launch(
        "place", functools.partial(place_kernel, groups), table,
        [(slots, (1, capacity, width), lambda i: (i, 0, 0))],
        [
            ((blocks, width, width), BF16, (blocks, width, width), lambda i: (0, 0, 0), pltpu.VMEM),
            ((blocks // 2, width, width), BF16, (blocks // 2, width, width), lambda i: (0, 0, 0), pltpu.VMEM),
        ],
        grid=(groups,), after=after, vmem=24, scratch=[pltpu.VMEM((D + capacity + SUBLANES, width), F32)],
    )


def batch_kernel(m, chunks, table_ref, *refs):
    matrix_hbm, scale_hbm, far_hbm, here_hbm, weight_hbm, for_mate_hbm, grad_hbm, bias_ref = refs[:8]
    refs = refs[8:]
    total_hbm, bias_sum_in = refs[:2] if m else (None, None)
    refs = refs[2:] if m else refs
    ended = m == MB - 1
    out_hbm, pre_hbm, mate_pre_hbm = refs[:3]
    away_hbm, refs = refs[3 : 3 + chunks], refs[3 + chunks :]
    mate_weight_hbm, refs = (refs[0], refs[1:]) if ended else (None, refs)
    results, refs = (refs[:2], refs[2:]) if ended else (refs[:1], refs[1:])
    bias_sum_ref, refs = refs[0], refs[1:]
    (
        matrix_ref, scale_ref, far_ref, mixed_ref, weight_ref, mate_weight_ref, grad_ref, out_ref, pre_ref, mate_pre_ref,
        away_ref, total_ref, load, store, send, receive,
    ) = refs[:16]
    parts = refs[16:]
    nodes, width = far_ref.shape
    wide, narrow = nodes // WIDE, nodes // TILE
    mate = partner(lax.axis_index("col"), 1)

    def at(index, size):
        return pl.ds(pl.multiple_of(index * size, size), size)

    def matrix_load(i):
        return pltpu.make_async_copy(
            matrix_hbm.at[m, :, at(i, WIDE)], matrix_ref.at[:, at(i, WIDE)], load.at[i]
        )

    loads = [
        pltpu.make_async_copy(source, target, load.at[wide + i])
        for i, (source, target) in enumerate(
            [
                (far_hbm, far_ref),
                (scale_hbm.at[m], scale_ref),
                (weight_hbm, weight_ref),
                (here_hbm.at[m], mixed_ref.at[0]),
                (grad_hbm.at[m], grad_ref),
            ]
            + ([(total_hbm, total_ref)] if m else [])
        )
    ]
    started = []

    def save(source, target):
        started.append(pltpu.make_async_copy(source, target, store.at[len(started)]))
        started[-1].start()

    def remote(source, target, number):
        return pltpu.make_async_remote_copy(
            src_ref=source,
            dst_ref=target,
            send_sem=send.at[number],
            recv_sem=receive.at[number],
            device_id={"col": mate},
            device_id_type=pl.DeviceIdType.MESH,
        )

    here_copy = remote(here_hbm.at[m], mixed_ref.at[1], 0)
    weight_copy = remote(for_mate_hbm, mate_weight_ref, 1)

    def there_copy(i):
        return remote(mixed_ref.at[2, at(i, WIDE)], mixed_ref.at[3, at(i, WIDE)], 2 + i)

    def pre_copy(i):
        return remote(pre_ref.at[at(i, TILE)], mate_pre_ref.at[at(i, TILE)], 2 + wide + i)

    loads[0].start()
    matrix_load(0).start()
    loads[1].start()
    for i in range(1, wide):
        matrix_load(i).start()
    for item in loads[2:]:
        item.start()
    greet_mate(mate)
    here_copy.start()
    loads[0].wait()
    loads[1].wait()

    @pl.loop(0, wide)
    def _(i):
        matrix_load(i).wait()
        rows = at(i, WIDE)
        there = product_rows(matrix_ref[:, rows], far_ref[...])
        mixed_ref[2, rows, :] = scaled(there, scale_ref[rows, :]).astype(BF16)
        there_copy(i).start()

    weight_copy.start()
    for item in loads[2:5]:
        item.wait()
    here_copy.wait_recv()
    bias_sum_ref[...] = bias_sum_in[...] if m else jnp.zeros_like(bias_sum_ref)
    for i in range(wide):
        there_copy(i).wait_recv()

    @pl.loop(0, narrow, unroll=UNROLL)
    def _(i):
        rows = at(i, TILE)
        preact = bias_ref[...]
        for block in range(4):
            preact = preact + product(mixed_ref[block, rows, :], weight_ref[block])
        row_ids = i * TILE + lax.broadcasted_iota(jnp.int32, preact.shape, 0)
        live = row_ids < table_ref[LIMITS + m]
        gate = jax.nn.sigmoid(preact)
        out_ref[rows, :] = jnp.where(live, preact * gate, 0.0).astype(BF16)
        slope = gate * (1.0 + preact * (1.0 - gate))
        grad_pre = jnp.where(live, grad_ref[rows, :].astype(F32) * slope, 0.0).astype(BF16)
        pre_ref[rows, :] = grad_pre
        pre_copy(i).start()
        bias_sum_ref[...] += jnp.sum(grad_pre.astype(F32), axis=0, keepdims=True)

    save(pre_ref, pre_hbm)
    save(out_ref, out_hbm)
    if m:
        loads[5].wait()

    @pl.loop(0, 4)
    def _(block):
        term = product_rows(mixed_ref[block], pre_ref[...])
        total_ref[block] = total_ref[block] + term if m else term

    if ended:
        half = width // 2
        upper = lax.axis_index("clus") % 2 == 1
        column = lax.axis_index("col")
        for block in range(4):
            source = partner(column, 1) if block % 2 else column
            source = partner(source, 2) if block >= 2 else source
            rows = at(source, width)
            low, high = total_ref[block, :, :half], total_ref[block, :, half:]
            parts[0][rows, :] = jnp.where(upper, high, low)
            parts[1][rows, :] = jnp.where(upper, low, high).astype(BF16)
        for part, result in zip(parts, results):
            save(part, result)
    else:
        save(total_ref, results[0])

    weight_copy.wait_recv()
    for i in range(narrow):
        pre_copy(i).wait_recv()
    save(mate_pre_ref, mate_pre_hbm)
    if ended:
        save(mate_weight_ref, mate_weight_hbm)
    step = width // chunks
    for i in range(wide):
        rows = slice(i * WIDE, (i + 1) * WIDE)
        away = product_back(pre_ref[rows, :], weight_ref[2]) + product_back(mate_pre_ref[rows, :], mate_weight_ref[1])
        away_ref[rows, :] = away.astype(BF16)
        for chunk in range(chunks):
            columns = slice(chunk * step, (chunk + 1) * step)
            save(away_ref.at[rows, columns], away_hbm[chunk].at[rows])
    here_copy.wait_send()
    weight_copy.wait_send()
    for i in range(wide):
        there_copy(i).wait_send()
    for i in range(narrow):
        pre_copy(i).wait_send()
    for item in started:
        item.wait()


def batch(table, m, matrix, scale, far, here, weight, for_mate, out_grad, bias, total, bias_sum, chunks, after=()):
    nodes, width = far.array.shape
    wide, narrow = nodes // WIDE, nodes // TILE
    flat = lambda i: (0, 0)
    ended = m == MB - 1
    parts = [((D, width // 2), F32), ((D, width // 2), BF16)] if ended else []
    results = [(*part, None, None) for part in parts]
    if not ended:
        results = [((4, width, width), F32, None, None, pltpu.VMEM)]
    return launch(
        f"batch{m}", functools.partial(batch_kernel, m, chunks), table,
        [(array, None, None) for array in (matrix, scale, far, here, weight, for_mate, out_grad)]
        + [(bias, (1, width), flat)]
        + ([(total, None, None), (bias_sum, (1, width), flat)] if m else []),
        [((nodes, width), BF16, None, None, pltpu.VMEM)]
        + [((nodes, width), BF16, None, None)] * 2
        + [((nodes, width // chunks), BF16, None, None)] * chunks
        + ([(for_mate.array.shape, BF16, None, None)] if ended else [])
        + results
        + [((1, width), F32, (1, width), flat)],
        after=after, barrier=BATCH_ID + m, vmem=34 if m == MB - 1 else 32,
        scratch=[
            pltpu.VMEM((nodes, nodes), BF16),
            pltpu.VMEM((nodes, LANES), F32),
            pltpu.VMEM((nodes, width), BF16),
            pltpu.VMEM((4, nodes, width), BF16),
            pltpu.VMEM(weight.array.shape, BF16),
            pltpu.VMEM(for_mate.array.shape, BF16),
            pltpu.VMEM((nodes, width), BF16),
            pltpu.VMEM((nodes, width), BF16),
            pltpu.VMEM((nodes, width), BF16),
            pltpu.VMEM((nodes, width), BF16),
            pltpu.VMEM((nodes, width), BF16),
            pltpu.VMEM((4, width, width), F32),
            pltpu.SemaphoreType.DMA((wide + 6,)),
            pltpu.SemaphoreType.DMA((6 + wide * chunks,)),
            pltpu.SemaphoreType.DMA((2 + wide + narrow,)),
            pltpu.SemaphoreType.DMA((2 + wide + narrow,)),
        ]
        + [pltpu.VMEM(*part) for part in parts],
    )


def scatter_job(m, tile, columns, own_source, got_source, scale_source, matrix_source, grads_hbm, scratch, semaphores):
    own_ref, got_ref, scale_ref, matrix_ref, sum_ref, grad_ref = scratch
    steps = matrix_ref.shape[0] // tile
    loads = [
        pltpu.make_async_copy(source, target, semaphores.at[i])
        for i, (source, target) in enumerate(
            [(own_source.at[:, columns], own_ref), (got_source, got_ref), (scale_source.at[m], scale_ref)]
        )
    ]
    tiles, stores = [], []
    for i in range(steps):
        rows = pl.ds(i * tile, tile)
        tiles.append(pltpu.make_async_copy(matrix_source.at[rows], matrix_ref.at[rows], semaphores.at[3 + i]))
        stores.append(
            pltpu.make_async_copy(grad_ref.at[rows], grads_hbm.at[m, rows, columns], semaphores.at[3 + steps + i])
        )

    def work():
        for item in loads:
            item.wait()
        grad_mixed = (own_ref[...].astype(F32) + got_ref[...].astype(F32)).astype(BF16)
        sum_ref[...] = scaled(grad_mixed.astype(F32), scale_ref[...]).astype(BF16)
        for i in range(steps):
            tiles[i].wait()
            rows = slice(i * tile, (i + 1) * tile)
            grad_ref[rows, :] = product(matrix_ref[rows, :], sum_ref[...]).astype(BF16)
            stores[i].start()

    return loads + tiles, work, stores


def scatter_scratch(nodes, width):
    return [
        pltpu.VMEM((nodes, width), BF16),
        pltpu.VMEM((nodes, width), BF16),
        pltpu.VMEM((nodes, LANES), F32),
        pltpu.VMEM((nodes, nodes), BF16),
        pltpu.VMEM((nodes, width), BF16),
        pltpu.VMEM((nodes, width), BF16),
        pltpu.SemaphoreType.DMA((3 + 2 * (nodes // WIDE),)),
    ]


def scatter_kernel(m, chunk, own_hbm, got_hbm, scale_hbm, matrix_hbm, grads_hbm, *refs):
    width = got_hbm.shape[1]
    loads, work, stores = scatter_job(
        m, own_hbm.shape[0], pl.ds(chunk * width, width), own_hbm, got_hbm, scale_hbm, matrix_hbm, grads_hbm, refs[:6], refs[6]
    )
    for item in loads:
        item.start()
    work()
    for item in stores:
        item.wait()


def scatter(m, chunk, own, got, scale, matrix, grads, after=()):
    nodes, width = own.array.shape
    return launch(
        f"scatter{m}_{chunk}", functools.partial(scatter_kernel, m, chunk), None,
        [(array, None, None) for array in (own, got, scale, matrix)],
        [((MB, nodes, width), BF16, None, None)],
        after=after, alias=(grads, 0), scratch=scatter_scratch(nodes, got.array.shape[1]),
    )[0]


def sum_kernel(groups, capacity, table_ref, *refs):
    keep_hbm, sent_hbm, bias_ref, weight_hbm, mate_weight_hbm = refs[:5]
    pre_hbm, mate_hbm, refs = refs[5 : 5 + MB], refs[5 + MB : 5 + 2 * MB], refs[5 + 2 * MB :]
    own_ref, got_ref, bias_out_ref, back_hbm, refs = *refs[:4], refs[4:]
    pre_ref, mate_ref, weights_ref, back_ref, load, store, refs = *refs[:6], refs[6:]
    keep_ref, pair_ref, land_ref, out_ref, total_ref, end_out_ref, end_in_ref, row_ref = refs[:8]
    pair_send, pair_receive, line_send, line_receive, row_send, row_receive = refs[8:]
    own = lax.axis_index("clus")
    place, pairs = own // 2, groups // 2
    other = partner(own, 1)
    rows = keep_ref.shape[0]
    size = rows // CHUNKS
    ahead, behind = place + 1 < pairs, place >= 1

    def remote(source, target, sent, received, device):
        return pltpu.make_async_remote_copy(
            src_ref=source,
            dst_ref=target,
            send_sem=sent,
            recv_sem=received,
            device_id={"clus": device},
            device_id_type=pl.DeviceIdType.MESH,
        )

    def part(chunk):
        return pl.ds(pl.multiple_of(chunk * size, size), size)

    def pair_copy(chunk):
        return remote(
            sent_hbm.at[part(chunk)], pair_ref.at[part(chunk)], pair_send.at[chunk], pair_receive.at[chunk], other
        )

    def line_copy(direction, chunk):
        return remote(
            out_ref.at[direction, part(chunk)], land_ref.at[direction, part(chunk)],
            line_send.at[direction, chunk], line_receive.at[direction, chunk],
            own + 2 if direction == 0 else own - 2,
        )

    def row_copy(number):
        device = (other, own + 2, own - 2)[number]
        return remote(row_ref.at[number], row_ref.at[3 + number], row_send.at[number], row_receive.at[number], device)

    end_copy = remote(end_out_ref, end_in_ref, pair_send.at[CHUNKS], pair_receive.at[CHUNKS], other)

    nodes = pre_ref.shape[1]
    tiles = nodes // WIDE
    loads = [
        pltpu.make_async_copy(source, target, load.at[i])
        for i, (source, target) in enumerate(
            [(keep_hbm, keep_ref), (weight_hbm.at[0], weights_ref.at[0]), (mate_weight_hbm.at[0], weights_ref.at[1])]
            + [(source, pre_ref.at[m]) for m, source in enumerate(pre_hbm)]
            + [(source, mate_ref.at[m]) for m, source in enumerate(mate_hbm)]
        )
    ]
    stores = [pltpu.make_async_copy(back_ref.at[m], back_hbm.at[m], store.at[m]) for m in range(MB)]

    def back(number):
        m, i = number // tiles, number % tiles
        if i == 0:
            loads[3 + m].wait()
            loads[3 + MB + m].wait()
        down = slice(i * WIDE, (i + 1) * WIDE)
        term = product_back(pre_ref[m, down, :], weights_ref[0]) + product_back(mate_ref[m, down, :], weights_ref[1])
        back_ref[m, down, :] = term.astype(BF16)
        if i == tiles - 1:
            stores[m].start()

    land_ref[...] = jnp.zeros_like(land_ref)
    row_ref[...] = jnp.zeros_like(row_ref)
    row_ref[0] = bias_ref[...]
    for item in loads:
        item.start()
    barrier = pltpu.get_barrier_semaphore()

    def greet(index):
        pl.semaphore_signal(barrier, inc=1, device_id={"clus": index}, device_id_type=pl.DeviceIdType.MESH)

    greet(other)

    @pl.when(ahead)
    def _():
        greet(own + 2)

    @pl.when(behind)
    def _():
        greet(own - 2)

    pl.semaphore_wait(barrier, 1 + jnp.where(ahead, 1, 0) + jnp.where(behind, 1, 0))
    row_copy(0).start()
    for chunk in range(CHUNKS):
        pair_copy(chunk).start()
    for item in loads[:3]:
        item.wait()

    def pass_on(direction, chunk, first):
        sums = keep_ref[part(chunk), :]
        if not first:
            sums = sums + land_ref[direction, part(chunk), :].astype(F32)
        out_ref[direction, part(chunk), :] = sums.astype(BF16)
        line_copy(direction, chunk).start()

    def pass_row(direction, first):
        row_ref[1 + direction] = row_ref[0] if first else row_ref[0] + row_ref[4 + direction]
        row_copy(1 + direction).start()

    steps = CHUNKS + pairs - 1
    for step in range(steps):
        if step < CHUNKS:
            pair_copy(step).wait_recv()
            keep_ref[part(step), :] += pair_ref[part(step), :].astype(F32)
            if step == 0:
                row_copy(0).wait()
                row_ref[0] += row_ref[3]
            for direction, (here, there) in enumerate(((behind, ahead), (ahead, behind))):

                @pl.when(jnp.logical_not(here) & there)
                def _(direction=direction, step=step):
                    pass_on(direction, step, True)
                    if step == 0:
                        pass_row(direction, True)

        for direction, (here, there) in enumerate(((behind, ahead), (ahead, behind))):
            chunk = step - (place if direction == 0 else pairs - 1 - place)

            @pl.when(here & (chunk >= 0) & (chunk < CHUNKS))
            def _(direction=direction, chunk=chunk, there=there):
                line_copy(direction, chunk).wait_recv()

                @pl.when(there)
                def _():
                    pass_on(direction, chunk, False)

                @pl.when(chunk == 0)
                def _():
                    row_copy(1 + direction).wait_recv()

                    @pl.when(there)
                    def _():
                        pass_row(direction, False)

        for number in range(step * MB * tiles // steps, (step + 1) * MB * tiles // steps):
            back(number)

    total_ref[:rows, :] = keep_ref[...] + (land_ref[0].astype(F32) + land_ref[1].astype(F32))
    total_ref[rows:, :] = jnp.zeros((capacity + SUBLANES, keep_ref.shape[1]), F32)
    end_out_ref[...] = take_rows(total_ref, table_ref[STARTS + other], capacity, rows - 1).astype(BF16)
    end_copy.start()
    own_ref[...] = take_rows(total_ref, table_ref[STARTS + own], capacity, rows - 1)
    bias_out_ref[...] = row_ref[0] + (row_ref[4] + row_ref[5])
    end_copy.wait()
    got_ref[...] = end_in_ref[...]
    for chunk in range(CHUNKS):
        pair_copy(chunk).wait_send()
    for direction, there in enumerate((ahead, behind)):

        @pl.when(there)
        def _(direction=direction):
            row_copy(1 + direction).wait_send()
            for chunk in range(CHUNKS):
                line_copy(direction, chunk).wait_send()

    for item in stores:
        item.wait()


def sum_over_owners(table, groups, capacity, keep, sent, bias, weight, mate_weight, pres, mates, after=()):
    rows, half = keep.shape
    nodes, width = pres[0].shape
    flat = lambda i: (0, 0)
    shape = (capacity, half)
    return launch(
        "sum", functools.partial(sum_kernel, groups, capacity), table,
        [(array, None, None) for array in (keep, sent)]
        + [(bias, bias.shape, flat)]
        + [(array, None, None) for array in (weight, mate_weight, *pres, *mates)],
        [
            (shape, F32, shape, flat),
            (shape, BF16, shape, flat),
            (bias.shape, F32, bias.shape, flat),
            ((MB, nodes, width), BF16, None, None),
        ],
        after=after, barrier=SUM_ID, vmem=34,
        scratch=[
            pltpu.VMEM((MB, nodes, width), BF16),
            pltpu.VMEM((MB, nodes, width), BF16),
            pltpu.VMEM((2, width, width), BF16),
            pltpu.VMEM((MB, nodes, width), BF16),
            pltpu.SemaphoreType.DMA((3 + 2 * MB,)),
            pltpu.SemaphoreType.DMA((MB,)),
            pltpu.VMEM((rows, half), F32),
            pltpu.VMEM((rows, half), BF16),
            pltpu.VMEM((2, rows, half), BF16),
            pltpu.VMEM((2, rows, half), BF16),
            pltpu.VMEM((rows + capacity + SUBLANES, half), F32),
            pltpu.VMEM(shape, BF16),
            pltpu.VMEM(shape, BF16),
            pltpu.VMEM((6, 1, width), F32),
            pltpu.SemaphoreType.DMA((CHUNKS + 1,)),
            pltpu.SemaphoreType.DMA((CHUNKS + 1,)),
            pltpu.SemaphoreType.DMA((2, CHUNKS)),
            pltpu.SemaphoreType.DMA((2, CHUNKS)),
            pltpu.SemaphoreType.DMA((3,)),
            pltpu.SemaphoreType.DMA((3,)),
        ],
    )


def adamw_update(current, first_moment, second_moment, gradient, step_rate):
    first_new = BETA_ONE * first_moment + (1.0 - BETA_ONE) * gradient
    second_new = BETA_TWO * second_moment + (1.0 - BETA_TWO) * gradient * gradient
    fixed_first = first_new / (1.0 - BETA_ONE**STEP)
    fixed_second = second_new / (1.0 - BETA_TWO**STEP)
    updated = current - step_rate * (
        fixed_first / (jnp.sqrt(fixed_second) + EPSILON) + DECAY * current
    )
    return (updated, first_new, second_new)


def finish_kernel(groups, table_ref, *refs):
    done = MB - 1
    own_ref, got_ref, bias_grad_ref, biases = refs[0], refs[1], refs[2], refs[3:6]
    weights_hbm, out_parts, refs = refs[6:9], refs[9 : 9 + MB], refs[9 + MB :]
    back_hbm, gots, (scale_hbm, matrix_hbm), refs = refs[0], refs[1 : 1 + done], refs[1 + done : 3 + done], refs[3 + done :]
    updated_hbm, bias_outs, (out_hbm, grads_hbm, last_back_ref, last_matrix_ref), refs = refs[:3], refs[3:6], refs[6:10], refs[10:]
    weights, (weight_load, weight_store, store), refs = refs[:3], refs[3:6], refs[6:]
    jobs = [
        scatter_job(
            m, WIDE, pl.ds(0, back_hbm.shape[2]), back_hbm.at[m], gots[m], scale_hbm, matrix_hbm.at[m], grads_hbm,
            refs[7 * m : 7 * m + 6], refs[7 * m + 6],
        )
        for m in range(done)
    ]
    weight_loads = [
        pltpu.make_async_copy(source, target, weight_load.at[i])
        for i, (source, target) in enumerate(zip(weights_hbm, weights))
    ]
    weight_stores = [
        pltpu.make_async_copy(source, target, weight_store.at[i])
        for i, (source, target) in enumerate(zip(weights, updated_hbm))
    ]
    moves = [
        pltpu.make_async_copy(source, target, store.at[i])
        for i, (source, target) in enumerate(
            [(part, out_hbm.at[m]) for m, part in enumerate(out_parts)]
            + [(back_hbm.at[done], last_back_ref), (matrix_hbm.at[done], last_matrix_ref)]
        )
    ]
    for item in jobs[0][0] + weight_loads:
        item.start()
    for later, _, _ in jobs[1:]:
        for item in later:
            item.start()
    for item in moves:
        item.start()
    jobs[0][1]()

    for item in weight_loads:
        item.wait()
    rows, width = weights[0].shape
    half = width // 2
    strip = min(rows, TILE // 2)
    own = table_ref[GROUP]
    for first in range(0, rows, strip):
        row_ids = first + lax.broadcasted_iota(jnp.int32, (strip, half), 0)
        used = row_ids < table_ref[STARTS + groups + own]
        down = slice(first, first + strip)
        for side in range(2):
            mine = (own & 1) == side
            here, there = own_ref[down, :], got_ref[down, :].astype(F32)
            columns = slice(side * half, (side + 1) * half)
            results = adamw_update(*(ref[down, columns] for ref in weights), jnp.where(mine, here, there), RATE_WEIGHT)
            for ref, result in zip(weights, results):
                ref[down, columns] = jnp.where(used, result, 0.0)
    for item in weight_stores:
        item.start()
    results = adamw_update(*(ref[...] for ref in biases), bias_grad_ref[...], RATE_BIAS)
    for ref, result in zip(bias_outs, results):
        ref[...] = result

    for _, work, _ in jobs[1:]:
        work()
    for item in weight_stores + moves:
        item.wait()
    for _, _, stores in jobs:
        for item in stores:
            item.wait()


def finish(table, groups, mine, other, bias_grad, biases, weights, outputs, backs, gots, scale, matrix, after=()):
    capacity, width = weights[0].shape
    nodes = outputs[0].array.shape[0]
    fixed = lambda i: (0, 0)
    scratch = [pltpu.VMEM((capacity, width), F32)] * 3 + [
        pltpu.SemaphoreType.DMA((3,)),
        pltpu.SemaphoreType.DMA((3,)),
        pltpu.SemaphoreType.DMA((MB + 2,)),
    ]
    for _ in gots:
        scratch += scatter_scratch(nodes, width)
    return launch(
        "finish", functools.partial(finish_kernel, groups), table,
        [(array, array.array.shape, fixed) for array in (mine, other)]
        + [(array, (1, width), fixed) for array in (bias_grad, *biases)]
        + [(array, None, None) for array in (*weights, *outputs, backs, *gots, scale, matrix)],
        [((capacity, width), F32, None, None)] * 3
        + [((1, width), F32, (1, width), fixed)] * 3
        + [((MB, nodes, width), BF16, None, None)] * 2
        + [((nodes, width), BF16, None, None, pltpu.VMEM), ((nodes, nodes), BF16, None, None, pltpu.VMEM)],
        after=after, scratch=scratch, vmem=32,
    )


def shards(
    features,
    neighbours,
    node_counts,
    row_counts,
    master_weight,
    weight_first,
    weight_second,
    master_bias,
    bias_first,
    bias_second,
    out_grad,
):
    groups = lax.axis_size("clus")
    capacity, width = master_weight.shape
    owner_ids = jnp.arange(groups, dtype=jnp.int32)
    starts = jnp.sum(jnp.where(owner_ids[None, :] < owner_ids[:, None], row_counts[None, :], 0), axis=1)
    table = jnp.concatenate(
        [
            jnp.stack([lax.axis_index("clus"), lax.axis_index("col")]).astype(jnp.int32),
            node_counts[:, 0],
            starts.astype(jnp.int32),
            row_counts,
        ]
    )
    bias_row, bias_first_row, bias_second_row = (
        array.reshape(1, width) for array in (master_bias, bias_first, bias_second)
    )

    picked = pick_first(features)
    picked = picked + pick(features, tuple(range(1, MB)), [Kept(picked[0])])
    far = [Kept(flip(array, "col", 2), None) for array in picked]

    matrix, scale, here, slots = front(
        table, groups, master_weight, jnp.swapaxes(neighbours, 1, 2), features, [picked[-1]]
    )
    scale = Kept(scale)
    weight, for_mate = (Kept(array) for array in place(table, slots))
    last = for_mate
    total, bias_sum = None, None
    outputs, pres, mates, away = [], [], [], []
    for m in range(MB):
        chunks = 2 if m == MB - 1 else 1
        out_m, pre_m, mate_m, *rest = batch(
            table, m, matrix, scale, far[m], here, weight, for_mate, out_grad, bias_row, total, bias_sum, chunks,
            [last],
        )
        outputs.append(Kept(out_m))
        pres.append(pre_m)
        mates.append(mate_m)
        away.append([Kept(flip(chunk, "col", 2), None) for chunk in rest[:chunks]])
        total, bias_sum = Kept(rest[chunks]), rest[-1]
        last = bias_sum

    mate_weight, keep, sent, bias_sum = rest[chunks:]
    mine, other, bias_total, backs = sum_over_owners(
        table, groups, capacity, keep, sent, bias_sum, weight, mate_weight, pres, mates, [last]
    )
    *updated, outputs, input_grads, last_back, last_matrix = finish(
        table, groups, Kept(mine, None), Kept(other, None), bias_total, (bias_row, bias_first_row, bias_second_row),
        (master_weight, weight_first, weight_second), outputs, backs, [part[0] for part in away[:-1]],
        scale, matrix, [bias_total],
    )
    for chunk, got in enumerate(away[-1]):
        input_grads = scatter(MB - 1, chunk, Kept(last_back), got, scale, Kept(last_matrix), input_grads)
    return (outputs, input_grads, *updated[:3], *(row.reshape(width) for row in updated[3:]))


def solution(mesh):
    in_specs = (
        P(None, "clus", "col"),
        P(None, "clus", None),
        P(None, "clus"),
        P(),
        P("clus", "col"),
        P("clus", "col"),
        P("clus", "col"),
        P("col"),
        P("col"),
        P("col"),
        P(None, "clus", "col"),
    )
    out_specs = (
        P(None, "clus", "col"),
        P(None, "clus", "col"),
        P("clus", "col"),
        P("clus", "col"),
        P("clus", "col"),
        P("col"),
        P("col"),
        P("col"),
    )
    return jax.shard_map(shards, mesh=mesh, in_specs=in_specs, out_specs=out_specs, check_vma=False)
```

```python
import functools

import jax
import jax.numpy as jnp
from jax import lax
from jax.experimental import pallas as pl
from jax.experimental.pallas import tpu as pltpu
from jax.sharding import PartitionSpec as P

D = 2048
MB = 3
STEP = 10

BETA_ONE = 0.9
BETA_TWO = 0.95
EPSILON = 1e-08
DECAY = 0.1
RATE_WEIGHT = 0.06
RATE_BIAS = 0.6

LANES = 128
DIGIT_BITS = 5
DIGITS = 6
STRIP = 32
SUBLANES = 8
TILE = 256
WIDE = 512
HALVES = 2
PIECES = 4
UNROLL = 3
CHUNKS = 8
MIB = 1024 * 1024
SMALL = 1 << 16

GROUP, COLUMN, LIMITS = 0, 1, 2
STARTS = LIMITS + MB

FRONT_ID, SUM_ID, BATCH_ID = 1, 2, 3

F32, BF16 = jnp.float32, jnp.bfloat16


class Kept:
    def __init__(self, array, space=pltpu.VMEM):
        self.array, self.space = array, space


def located(item):
    if isinstance(item, Kept):
        return pltpu.with_memory_space_constraint(item.array, item.space) if item.space else item.array
    return pltpu.with_memory_space_constraint(item, pltpu.HBM) if item.size > SMALL else item


def launch(name, body, table, ins, outs, grid=(1,), after=(), alias=None, scratch=(), barrier=None, vmem=16):
    tables = [] if table is None else [table]

    def spec(block, index):
        if block is None:
            return pl.BlockSpec(memory_space=pl.ANY)
        return pl.BlockSpec(block, lambda *a: index(*a[: len(grid)]))

    unread = ([alias[0]] if alias else []) + [array for array in after if alias is None or array is not alias[0]]

    def kernel(*refs):
        table_refs, refs = refs[: len(tables)], refs[len(tables) :]
        body(*table_refs, *refs[: len(ins)], *refs[len(ins) + len(unread) :])

    return pl.pallas_call(
        kernel,
        grid_spec=pltpu.PrefetchScalarGridSpec(
            num_scalar_prefetch=len(tables),
            grid=grid,
            in_specs=[spec(block, index) for _, block, index in ins]
            + [pl.BlockSpec(memory_space=pl.ANY)] * len(unread),
            out_specs=[spec(out[2], out[3]) for out in outs],
            scratch_shapes=list(scratch),
        ),
        out_shape=[
            (out[4] if len(out) > 4 else pltpu.HBM if out[2] is None else jax.ShapeDtypeStruct)(out[0], out[1])
            for out in outs
        ],
        input_output_aliases={len(tables) + len(ins): alias[1]} if alias else {},
        compiler_params=pltpu.CompilerParams(
            vmem_limit_bytes=vmem * MIB, collective_id=barrier, has_side_effects=barrier is not None
        ),
        cost_estimate=pl.CostEstimate(flops=1, bytes_accessed=1, transcendentals=0),
        name=name,
    )(*tables, *(located(item[0]) for item in ins), *(located(item) for item in unread))


def flip(values, axis, bit):
    size = lax.axis_size(axis)
    return lax.ppermute(values, axis, [(i, i ^ bit) for i in range(size)])


def partner(index, bit):
    return index + bit * (1 - 2 * ((index // bit) % 2))


def product(left, right):
    return jnp.dot(left, right, preferred_element_type=F32)


def product_back(left, right):
    return lax.dot_general(left, right, (((1,), (1,)), ((), ())), preferred_element_type=F32)


def product_rows(left, right):
    return lax.dot_general(left, right, (((0,), (0,)), ((), ())), preferred_element_type=F32)


def scaled(values, scale):
    return values * jnp.concatenate([scale] * (values.shape[1] // LANES), axis=1)


def put_rows(ref, first, rows):
    base = pl.multiple_of((first // SUBLANES) * SUBLANES, SUBLANES)
    offset = first - base
    moved = jnp.concatenate([rows, jnp.zeros((SUBLANES, rows.shape[1]), rows.dtype)], axis=0)
    wanted = jnp.broadcast_to(offset, moved.shape)
    for bit in (1, 2, 4):
        moved = jnp.where((wanted & bit) != 0, pltpu.roll(moved, bit, 0), moved)
    head = ref[pl.ds(base, SUBLANES), :]
    row_ids = lax.broadcasted_iota(jnp.int32, head.shape, 0)
    ref[pl.ds(base, SUBLANES), :] = jnp.where(row_ids < offset, head, moved[:SUBLANES])
    ref[pl.ds(pl.multiple_of(base + SUBLANES, SUBLANES), rows.shape[0]), :] = moved[SUBLANES:]


def take_rows(ref, first, count, largest):
    bit = 1 << (largest.bit_length() - 1)
    rows = ref[...]
    while bit:
        length = count + max(bit, SUBLANES)
        if bit >= SUBLANES:
            moved = rows[bit : bit + length]
            missing = length - moved.shape[0]
            if missing:
                moved = jnp.concatenate([moved, jnp.zeros((missing, rows.shape[1]), rows.dtype)], axis=0)
        else:
            moved = pltpu.roll(rows, length - bit, 0)
        chosen = (jnp.broadcast_to(first, (length, rows.shape[1])) & bit) != 0
        rows = jnp.where(chosen, moved, rows[:length])
        bit //= 2
    return rows[:count]


def relay(sources, targets, buffers, load, store):
    def piece(ref, i):
        rows = ref.shape[0] // PIECES
        return ref.at[pl.ds(i * rows, rows)]

    loads, stores = [], []
    for number, (source, target, buffer) in enumerate(zip(sources, targets, buffers)):
        for i in range(PIECES):
            place = number * PIECES + i
            loads.append(pltpu.make_async_copy(piece(source, i), piece(buffer, i), load.at[place]))
            stores.append(pltpu.make_async_copy(piece(buffer, i), piece(target, i), store.at[place]))
    return loads, stores


def first_kernel(source_hbm, target_ref, semaphore):
    copy = pltpu.make_async_copy(source_hbm.at[0], target_ref, semaphore)
    copy.start()
    copy.wait()


def pick_first(stacked):
    return launch(
        "first", first_kernel, None,
        [(stacked, None, None)], [(stacked.shape[1:], stacked.dtype, None, None, pltpu.VMEM)],
        scratch=[pltpu.SemaphoreType.DMA],
    )


def pick_kernel(batches, source_ref, *refs):
    targets, (buffer_ref, load, store) = refs[:-3], refs[-3:]
    loads, stores = relay(
        [source_ref.at[m] for m in batches], targets, [buffer_ref.at[i] for i in range(len(batches))], load, store
    )
    for item in loads:
        item.start()
    for item, onward in zip(loads, stores):
        item.wait()
        onward.start()
    for item in stores:
        item.wait()


def pick(stacked, batches, after=()):
    count = len(batches)
    return launch(
        f"pick{batches[0]}", functools.partial(pick_kernel, batches), None,
        [(stacked, None, None)], [(stacked.shape[1:], stacked.dtype, None, None)] * count,
        after=after,
        scratch=[
            pltpu.VMEM((count, *stacked.shape[1:]), stacked.dtype),
            pltpu.SemaphoreType.DMA((count * PIECES,)),
            pltpu.SemaphoreType.DMA((count * PIECES,)),
        ],
    )


def count_tile(limit, first, neighbour_ref, matrix_ref, scale_ref, lanes):
    nodes = matrix_ref.shape[1]
    words = -(-(nodes // LANES) // DIGITS)
    entries = neighbour_ref[0, :, lanes]
    node_ids = first + lax.broadcasted_iota(jnp.int32, entries.shape, 1)
    valid = (entries < limit) & (node_ids < limit)
    low = entries & (LANES - 1)
    high = entries >> 7
    digits = []
    for word in range(words):
        inside = valid & (high >= word * DIGITS) & (high < (word + 1) * DIGITS)
        shift = jnp.where(inside, (high - word * DIGITS) * DIGIT_BITS, 0)
        digits.append(jnp.where(inside, jnp.left_shift(1, shift), 0))
    for strip in range(LANES // STRIP):
        row_ids = strip * STRIP + lax.broadcasted_iota(jnp.int32, (STRIP, LANES), 0)
        sums = [jnp.zeros((STRIP, LANES), jnp.int32) for _ in range(words)]
        for entry in range(entries.shape[0]):
            hit = row_ids == low[entry : entry + 1, :]
            for word in range(words):
                sums[word] = sums[word] + jnp.where(hit, digits[word][entry : entry + 1, :], 0)
        for block in range(nodes // LANES):
            word, digit = block // DIGITS, block % DIGITS
            count = jnp.right_shift(sums[word], digit * DIGIT_BITS) & ((1 << DIGIT_BITS) - 1)
            rows = slice(block * LANES + strip * STRIP, block * LANES + (strip + 1) * STRIP)
            matrix_ref[0, rows, lanes] = count.astype(F32).astype(BF16)
    rows = pl.ds(pl.multiple_of(first, LANES), LANES)
    square = matrix_ref[0, rows, lanes].astype(F32)
    on_diagonal = lax.broadcasted_iota(jnp.int32, square.shape, 0) == lax.broadcasted_iota(jnp.int32, square.shape, 1)
    matrix_ref[0, rows, lanes] = jnp.where(on_diagonal, 2.0 * square + 2.0, square).astype(BF16)
    degree = 1.0 + jnp.sum(valid.astype(F32), axis=0, keepdims=True)
    factor = (node_ids[:1] < limit).astype(F32) / degree
    scale_ref[0, lanes, :] = jnp.transpose(jnp.broadcast_to(factor, (LANES, LANES)))


def front_kernel(
    groups, total, table_ref, master_ref, neighbour_ref, feature_ref, matrix_ref, scale_ref, mixed_ref, slots_ref,
    block_ref, local_semaphore, line_send, line_receive, pair_send, pair_receive,
):
    batch, tile_id = pl.program_id(0), pl.program_id(1)
    tiles = pl.num_programs(1)
    step = batch * tiles + tile_id
    own = lax.axis_index("clus")
    place, side = own // 2, own % 2
    pairs = groups // 2
    other = partner(own, 1)

    def rows_of(half):
        size = block_ref.shape[0] // HALVES
        return pl.ds(half * size, size)

    def remote(source, target, sent, received, device):
        return pltpu.make_async_remote_copy(
            src_ref=source,
            dst_ref=target,
            send_sem=sent,
            recv_sem=received,
            device_id={"clus": device},
            device_id_type=pl.DeviceIdType.MESH,
        )

    def origin_of(direction, hop):
        return place - 1 - hop if direction == 0 else place + 1 + hop

    def line_copy(direction, hop, half):
        slot = (place - hop if direction == 0 else place + hop) * 2 + side
        target = slots_ref.at[slot, rows_of(half)]
        return remote(
            block_ref.at[rows_of(half)] if hop == 0 else target, target,
            line_send.at[direction, hop, half], line_receive.at[direction, hop, half],
            own + 2 if direction == 0 else own - 2,
        )

    def sends(direction, hop):
        if direction == 0:
            return (place - hop >= 0) & (place + 1 < pairs)
        return (place + hop < pairs) & (place - 1 >= 0)

    def arrives(direction, hop):
        return place - 1 - hop >= 0 if direction == 0 else place + 1 + hop < pairs

    def arrival(direction, hop, half):
        target = slots_ref.at[origin_of(direction, hop) * 2 + side, rows_of(half)]
        return remote(
            target, target, line_send.at[direction, hop, half], line_receive.at[direction, hop, half], other
        )

    def pair_copy(direction, hop, half):
        slot = own if hop < 0 else origin_of(direction, hop) * 2 + side
        number = 0 if hop < 0 else 1 + 2 * hop + direction
        target = slots_ref.at[slot, rows_of(half)]
        return remote(
            block_ref.at[rows_of(half)] if hop < 0 else target, target,
            pair_send.at[number, half], pair_receive.at[number, half], other,
        )

    def pair_arrival(direction, hop, half):
        slot = other if hop < 0 else origin_of(direction, hop) * 2 + 1 - side
        number = 0 if hop < 0 else 1 + 2 * hop + direction
        target = slots_ref.at[slot, rows_of(half)]
        return remote(target, target, pair_send.at[number, half], pair_receive.at[number, half], other)

    local_copy = pltpu.make_async_copy(block_ref, slots_ref.at[own], local_semaphore)
    hops = pairs - 1

    @pl.when(step == 0)
    def _():
        barrier = pltpu.get_barrier_semaphore()

        def greet(index):
            pl.semaphore_signal(barrier, inc=1, device_id={"clus": index}, device_id_type=pl.DeviceIdType.MESH)

        greet(other)

        @pl.when(place + 1 < pairs)
        def _():
            greet(own + 2)

        @pl.when(place - 1 >= 0)
        def _():
            greet(own - 2)

        pl.semaphore_wait(barrier, 1 + jnp.where(place + 1 < pairs, 1, 0) + jnp.where(place - 1 >= 0, 1, 0))
        block_ref[...] = master_ref[...].astype(BF16)
        for half in range(HALVES):
            for direction in range(2):
                pl.when(sends(direction, 0))(line_copy(direction, 0, half).start)
            pair_copy(0, -1, half).start()
        local_copy.start()

    limit = table_ref[LIMITS + batch]
    tile = mixed_ref.shape[1]
    for part in range(tile // LANES):
        first = tile_id * tile + part * LANES
        count_tile(limit, first, neighbour_ref, matrix_ref, scale_ref, slice(part * LANES, (part + 1) * LANES))
    mixed_ref[0] = scaled(product_rows(matrix_ref[0], feature_ref[0]), scale_ref[0]).astype(BF16)

    for event in range(hops * HALVES):
        hop, half = event // HALVES, event % HALVES

        @pl.when(step == min(total - 1, ((event + 1) * total) // (hops * HALVES)))
        def _(hop=hop, half=half):
            for direction in range(2):

                @pl.when(arrives(direction, hop))
                def _(direction=direction):
                    arrival(direction, hop, half).wait_recv()
                    pair_copy(direction, hop, half).start()

                if hop + 1 < hops:
                    pl.when(sends(direction, hop + 1))(line_copy(direction, hop + 1, half).start)

    @pl.when(step == total - 1)
    def _():
        local_copy.wait()
        for half in range(HALVES):
            pair_copy(0, -1, half).wait_send()
            pair_arrival(0, -1, half).wait_recv()
            for hop in range(hops):
                for direction in range(2):
                    pl.when(sends(direction, hop))(line_copy(direction, hop, half).wait_send)

                    @pl.when(arrives(direction, hop))
                    def _(direction=direction, hop=hop, half=half):
                        pair_copy(direction, hop, half).wait_send()
                        pair_arrival(direction, hop, half).wait_recv()


def front(table, groups, master, neighbours, features, after=()):
    _, entries, nodes = neighbours.shape
    capacity, width = master.shape
    hops = groups // 2 - 1
    steps = MB * (nodes // TILE)
    return launch(
        "front", functools.partial(front_kernel, groups, steps), table,
        [
            (master, (capacity, width), lambda b, i: (0, 0)),
            (neighbours, (1, entries, TILE), lambda b, i: (b, 0, i)),
            (features, (1, nodes, width), lambda b, i: (b, 0, 0)),
        ],
        [
            ((MB, nodes, nodes), BF16, (1, nodes, TILE), lambda b, i: (b, 0, i), pltpu.HBM),
            ((MB, nodes, LANES), F32, (1, TILE, LANES), lambda b, i: (b, i, 0), pltpu.VMEM),
            ((MB, nodes, width), BF16, (1, TILE, width), lambda b, i: (b, i, 0), pltpu.HBM),
            ((groups, capacity, width), BF16, None, None),
        ],
        grid=(MB, nodes // TILE), after=after, barrier=FRONT_ID, vmem=20,
        scratch=[
            pltpu.VMEM((capacity, width), BF16),
            pltpu.SemaphoreType.DMA,
            pltpu.SemaphoreType.DMA((2, hops, HALVES)),
            pltpu.SemaphoreType.DMA((2, hops, HALVES)),
            pltpu.SemaphoreType.DMA((1 + 2 * hops, HALVES)),
            pltpu.SemaphoreType.DMA((1 + 2 * hops, HALVES)),
        ],
    )


def greet_mate(mate):
    barrier = pltpu.get_barrier_semaphore()
    pl.semaphore_signal(barrier, inc=1, device_id={"col": mate}, device_id_type=pl.DeviceIdType.MESH)
    pl.semaphore_wait(barrier, 1)


def place_kernel(groups, table_ref, slots_ref, weight_ref, mate_ref, rows_ref):
    owner = pl.program_id(0)

    @pl.when(owner == 0)
    def _():
        rows_ref[...] = jnp.zeros_like(rows_ref)

    put_rows(rows_ref, table_ref[STARTS + owner], slots_ref[0].astype(F32))

    @pl.when(owner == groups - 1)
    def _():
        width = weight_ref.shape[2]
        for block in range(weight_ref.shape[0]):
            source = pl.multiple_of((table_ref[COLUMN] ^ block) * width, width)
            rows = rows_ref[pl.ds(source, width), :].astype(BF16)
            weight_ref[block] = rows
            if block % 2:
                mate_ref[block // 2] = rows


def place(table, slots, after=()):
    groups, capacity, width = slots.shape
    blocks = D // width
    return launch(
        "place", functools.partial(place_kernel, groups), table,
        [(slots, (1, capacity, width), lambda i: (i, 0, 0))],
        [
            ((blocks, width, width), BF16, (blocks, width, width), lambda i: (0, 0, 0), pltpu.VMEM),
            ((blocks // 2, width, width), BF16, (blocks // 2, width, width), lambda i: (0, 0, 0), pltpu.VMEM),
        ],
        grid=(groups,), after=after, vmem=24, scratch=[pltpu.VMEM((D + capacity + SUBLANES, width), F32)],
    )


def batch_kernel(m, widths, table_ref, *refs):
    matrix_hbm, scale_hbm, far_hbm, here_hbm, weight_hbm, for_mate_hbm, grad_hbm, bias_ref = refs[:8]
    refs, chunks = refs[8:], len(widths)
    total_hbm, bias_sum_in = refs[:2] if m else (None, None)
    refs = refs[2:] if m else refs
    ended = m == MB - 1
    out_hbm, pre_hbm, mate_pre_hbm = refs[:3]
    away_hbm, refs = refs[3 : 3 + chunks], refs[3 + chunks :]
    mate_weight_hbm, refs = (refs[0], refs[1:]) if ended else (None, refs)
    results, refs = (refs[:2], refs[2:]) if ended else (refs[:1], refs[1:])
    bias_sum_ref, refs = refs[0], refs[1:]
    (
        matrix_ref, scale_ref, far_ref, mixed_ref, weight_ref, mate_weight_ref, grad_ref, out_ref, pre_ref, mate_pre_ref,
        away_ref, total_ref, load, store, send, receive,
    ) = refs[:16]
    parts = refs[16:]
    nodes, width = far_ref.shape
    wide, narrow = nodes // WIDE, nodes // TILE
    mate = partner(lax.axis_index("col"), 1)

    def at(index, size):
        return pl.ds(pl.multiple_of(index * size, size), size)

    def matrix_load(i):
        return pltpu.make_async_copy(
            matrix_hbm.at[m, :, at(i, WIDE)], matrix_ref.at[:, at(i, WIDE)], load.at[i]
        )

    loads = [
        pltpu.make_async_copy(source, target, load.at[wide + i])
        for i, (source, target) in enumerate(
            [
                (far_hbm, far_ref),
                (scale_hbm.at[m], scale_ref),
                (weight_hbm, weight_ref),
                (here_hbm.at[m], mixed_ref.at[0]),
                (grad_hbm.at[m], grad_ref),
            ]
            + ([(total_hbm, total_ref)] if m else [])
        )
    ]
    started = []

    def save(source, target):
        started.append(pltpu.make_async_copy(source, target, store.at[len(started)]))
        started[-1].start()

    def remote(source, target, number):
        return pltpu.make_async_remote_copy(
            src_ref=source,
            dst_ref=target,
            send_sem=send.at[number],
            recv_sem=receive.at[number],
            device_id={"col": mate},
            device_id_type=pl.DeviceIdType.MESH,
        )

    here_copy = remote(here_hbm.at[m], mixed_ref.at[1], 0)
    weight_copy = remote(for_mate_hbm, mate_weight_ref, 1)

    def there_copy(i):
        return remote(mixed_ref.at[2, at(i, WIDE)], mixed_ref.at[3, at(i, WIDE)], 2 + i)

    def pre_copy(i):
        return remote(pre_ref.at[at(i, TILE)], mate_pre_ref.at[at(i, TILE)], 2 + wide + i)

    loads[0].start()
    matrix_load(0).start()
    loads[1].start()
    for i in range(1, wide):
        matrix_load(i).start()
    for item in loads[2:]:
        item.start()
    greet_mate(mate)
    here_copy.start()
    loads[0].wait()
    loads[1].wait()

    @pl.loop(0, wide)
    def _(i):
        matrix_load(i).wait()
        rows = at(i, WIDE)
        there = product_rows(matrix_ref[:, rows], far_ref[...])
        mixed_ref[2, rows, :] = scaled(there, scale_ref[rows, :]).astype(BF16)
        there_copy(i).start()

    weight_copy.start()
    for item in loads[2:5]:
        item.wait()
    here_copy.wait_recv()
    bias_sum_ref[...] = bias_sum_in[...] if m else jnp.zeros_like(bias_sum_ref)
    for i in range(wide):
        there_copy(i).wait_recv()

    @pl.loop(0, narrow, unroll=UNROLL)
    def _(i):
        rows = at(i, TILE)
        preact = bias_ref[...]
        for block in range(4):
            preact = preact + product(mixed_ref[block, rows, :], weight_ref[block])
        row_ids = i * TILE + lax.broadcasted_iota(jnp.int32, preact.shape, 0)
        live = row_ids < table_ref[LIMITS + m]
        gate = jax.nn.sigmoid(preact)
        out_ref[rows, :] = jnp.where(live, preact * gate, 0.0).astype(BF16)
        slope = gate * (1.0 + preact * (1.0 - gate))
        grad_pre = jnp.where(live, grad_ref[rows, :].astype(F32) * slope, 0.0).astype(BF16)
        pre_ref[rows, :] = grad_pre
        pre_copy(i).start()
        bias_sum_ref[...] += jnp.sum(grad_pre.astype(F32), axis=0, keepdims=True)

    save(pre_ref, pre_hbm)
    save(out_ref, out_hbm)
    if m:
        loads[5].wait()

    @pl.loop(0, 4)
    def _(block):
        term = product_rows(mixed_ref[block], pre_ref[...])
        total_ref[block] = total_ref[block] + term if m else term

    if ended:
        half = width // 2
        upper = lax.axis_index("clus") % 2 == 1
        column = lax.axis_index("col")
        for block in range(4):
            source = partner(column, 1) if block % 2 else column
            source = partner(source, 2) if block >= 2 else source
            rows = at(source, width)
            low, high = total_ref[block, :, :half], total_ref[block, :, half:]
            parts[0][rows, :] = jnp.where(upper, high, low)
            parts[1][rows, :] = jnp.where(upper, low, high).astype(BF16)
        for part, result in zip(parts, results):
            save(part, result)
    else:
        save(total_ref, results[0])

    weight_copy.wait_recv()
    for i in range(narrow):
        pre_copy(i).wait_recv()
    save(mate_pre_ref, mate_pre_hbm)
    if ended:
        save(mate_weight_ref, mate_weight_hbm)
    for i in range(wide):
        rows = slice(i * WIDE, (i + 1) * WIDE)
        away = product_back(pre_ref[rows, :], weight_ref[2]) + product_back(mate_pre_ref[rows, :], mate_weight_ref[1])
        away_ref[rows, :] = away.astype(BF16)
        for chunk in range(chunks):
            columns = slice(sum(widths[:chunk]), sum(widths[: chunk + 1]))
            save(away_ref.at[rows, columns], away_hbm[chunk].at[rows])
    here_copy.wait_send()
    weight_copy.wait_send()
    for i in range(wide):
        there_copy(i).wait_send()
    for i in range(narrow):
        pre_copy(i).wait_send()
    for item in started:
        item.wait()


def batch(table, m, matrix, scale, far, here, weight, for_mate, out_grad, bias, total, bias_sum, widths, after=()):
    nodes, width = far.array.shape
    wide, narrow, chunks = nodes // WIDE, nodes // TILE, len(widths)
    flat = lambda i: (0, 0)
    ended = m == MB - 1
    parts = [((D, width // 2), F32), ((D, width // 2), BF16)] if ended else []
    results = [(*part, None, None) for part in parts]
    if not ended:
        results = [((4, width, width), F32, None, None, pltpu.VMEM)]
    return launch(
        f"batch{m}", functools.partial(batch_kernel, m, widths), table,
        [(array, None, None) for array in (matrix, scale, far, here, weight, for_mate, out_grad)]
        + [(bias, (1, width), flat)]
        + ([(total, None, None), (bias_sum, (1, width), flat)] if m else []),
        [((nodes, width), BF16, None, None, pltpu.VMEM)]
        + [((nodes, width), BF16, None, None)] * 2
        + [((nodes, columns), BF16, None, None) for columns in widths]
        + ([(for_mate.array.shape, BF16, None, None)] if ended else [])
        + results
        + [((1, width), F32, (1, width), flat)],
        after=after, barrier=BATCH_ID + m, vmem=34 if m == MB - 1 else 32,
        scratch=[
            pltpu.VMEM((nodes, nodes), BF16),
            pltpu.VMEM((nodes, LANES), F32),
            pltpu.VMEM((nodes, width), BF16),
            pltpu.VMEM((4, nodes, width), BF16),
            pltpu.VMEM(weight.array.shape, BF16),
            pltpu.VMEM(for_mate.array.shape, BF16),
            pltpu.VMEM((nodes, width), BF16),
            pltpu.VMEM((nodes, width), BF16),
            pltpu.VMEM((nodes, width), BF16),
            pltpu.VMEM((nodes, width), BF16),
            pltpu.VMEM((nodes, width), BF16),
            pltpu.VMEM((4, width, width), F32),
            pltpu.SemaphoreType.DMA((wide + 6,)),
            pltpu.SemaphoreType.DMA((6 + wide * chunks,)),
            pltpu.SemaphoreType.DMA((2 + wide + narrow,)),
            pltpu.SemaphoreType.DMA((2 + wide + narrow,)),
        ]
        + [pltpu.VMEM(*part) for part in parts],
    )


def scatter_job(m, tile, columns, own_source, got_source, scale_source, matrix_source, grads_hbm, scratch, semaphores):
    own_ref, got_ref, scale_ref, matrix_ref, sum_ref, grad_ref = scratch
    steps = matrix_ref.shape[0] // tile
    loads = [
        pltpu.make_async_copy(source, target, semaphores.at[i])
        for i, (source, target) in enumerate(
            [(own_source.at[:, columns], own_ref), (got_source, got_ref), (scale_source.at[m], scale_ref)]
        )
    ]
    tiles, stores = [], []
    for i in range(steps):
        rows = pl.ds(i * tile, tile)
        tiles.append(pltpu.make_async_copy(matrix_source.at[rows], matrix_ref.at[rows], semaphores.at[3 + i]))
        stores.append(
            pltpu.make_async_copy(grad_ref.at[rows], grads_hbm.at[m, rows, columns], semaphores.at[3 + steps + i])
        )

    def work():
        for item in loads:
            item.wait()
        grad_mixed = (own_ref[...].astype(F32) + got_ref[...].astype(F32)).astype(BF16)
        sum_ref[...] = scaled(grad_mixed.astype(F32), scale_ref[...]).astype(BF16)
        for i in range(steps):
            tiles[i].wait()
            rows = slice(i * tile, (i + 1) * tile)
            grad_ref[rows, :] = product(matrix_ref[rows, :], sum_ref[...]).astype(BF16)
            stores[i].start()

    return loads + tiles, work, stores


def scatter_scratch(nodes, width):
    return [
        pltpu.VMEM((nodes, width), BF16),
        pltpu.VMEM((nodes, width), BF16),
        pltpu.VMEM((nodes, LANES), F32),
        pltpu.VMEM((nodes, nodes), BF16),
        pltpu.VMEM((nodes, width), BF16),
        pltpu.VMEM((nodes, width), BF16),
        pltpu.SemaphoreType.DMA((3 + 2 * (nodes // WIDE),)),
    ]


def scatter_kernel(m, first, own_hbm, got_hbm, scale_hbm, matrix_hbm, grads_hbm, *refs):
    width = got_hbm.shape[1]
    loads, work, stores = scatter_job(
        m, own_hbm.shape[0], pl.ds(first, width), own_hbm, got_hbm, scale_hbm, matrix_hbm, grads_hbm, refs[:6], refs[6]
    )
    for item in loads:
        item.start()
    work()
    for item in stores:
        item.wait()


def scatter(m, first, own, got, scale, matrix, grads, after=()):
    nodes, width = own.array.shape
    return launch(
        f"scatter{m}_{first}", functools.partial(scatter_kernel, m, first), None,
        [(array, None, None) for array in (own, got, scale, matrix)],
        [((MB, nodes, width), BF16, None, None)],
        after=after, alias=(grads, 0), scratch=scatter_scratch(nodes, got.array.shape[1]),
    )[0]


def sum_kernel(groups, capacity, table_ref, *refs):
    keep_hbm, sent_hbm, bias_ref, weight_hbm, mate_weight_hbm = refs[:5]
    pre_hbm, mate_hbm, refs = refs[5 : 5 + MB], refs[5 + MB : 5 + 2 * MB], refs[5 + 2 * MB :]
    own_ref, got_ref, bias_out_ref, back_hbm, refs = *refs[:4], refs[4:]
    pre_ref, mate_ref, weights_ref, back_ref, load, store, refs = *refs[:6], refs[6:]
    keep_ref, pair_ref, land_ref, out_ref, total_ref, end_out_ref, end_in_ref, row_ref = refs[:8]
    pair_send, pair_receive, line_send, line_receive, row_send, row_receive = refs[8:]
    own = lax.axis_index("clus")
    place, pairs = own // 2, groups // 2
    other = partner(own, 1)
    rows = keep_ref.shape[0]
    size = rows // CHUNKS
    ahead, behind = place + 1 < pairs, place >= 1

    def remote(source, target, sent, received, device):
        return pltpu.make_async_remote_copy(
            src_ref=source,
            dst_ref=target,
            send_sem=sent,
            recv_sem=received,
            device_id={"clus": device},
            device_id_type=pl.DeviceIdType.MESH,
        )

    def part(chunk):
        return pl.ds(pl.multiple_of(chunk * size, size), size)

    def pair_copy(chunk):
        return remote(
            sent_hbm.at[part(chunk)], pair_ref.at[part(chunk)], pair_send.at[chunk], pair_receive.at[chunk], other
        )

    def line_copy(direction, chunk):
        return remote(
            out_ref.at[direction, part(chunk)], land_ref.at[direction, part(chunk)],
            line_send.at[direction, chunk], line_receive.at[direction, chunk],
            own + 2 if direction == 0 else own - 2,
        )

    def row_copy(number):
        device = (other, own + 2, own - 2)[number]
        return remote(row_ref.at[number], row_ref.at[3 + number], row_send.at[number], row_receive.at[number], device)

    end_copy = remote(end_out_ref, end_in_ref, pair_send.at[CHUNKS], pair_receive.at[CHUNKS], other)

    nodes = pre_ref.shape[1]
    tiles = nodes // WIDE
    loads = [
        pltpu.make_async_copy(source, target, load.at[i])
        for i, (source, target) in enumerate(
            [(keep_hbm, keep_ref), (weight_hbm.at[0], weights_ref.at[0]), (mate_weight_hbm.at[0], weights_ref.at[1])]
            + [(source, pre_ref.at[m]) for m, source in enumerate(pre_hbm)]
            + [(source, mate_ref.at[m]) for m, source in enumerate(mate_hbm)]
        )
    ]
    stores = [pltpu.make_async_copy(back_ref.at[m], back_hbm.at[m], store.at[m]) for m in range(MB)]

    def back(number):
        m, i = number // tiles, number % tiles
        if i == 0:
            loads[3 + m].wait()
            loads[3 + MB + m].wait()
        down = slice(i * WIDE, (i + 1) * WIDE)
        term = product_back(pre_ref[m, down, :], weights_ref[0]) + product_back(mate_ref[m, down, :], weights_ref[1])
        back_ref[m, down, :] = term.astype(BF16)
        if i == tiles - 1:
            stores[m].start()

    land_ref[...] = jnp.zeros_like(land_ref)
    row_ref[...] = jnp.zeros_like(row_ref)
    row_ref[0] = bias_ref[...]
    for item in loads:
        item.start()
    barrier = pltpu.get_barrier_semaphore()

    def greet(index):
        pl.semaphore_signal(barrier, inc=1, device_id={"clus": index}, device_id_type=pl.DeviceIdType.MESH)

    greet(other)

    @pl.when(ahead)
    def _():
        greet(own + 2)

    @pl.when(behind)
    def _():
        greet(own - 2)

    pl.semaphore_wait(barrier, 1 + jnp.where(ahead, 1, 0) + jnp.where(behind, 1, 0))
    row_copy(0).start()
    for chunk in range(CHUNKS):
        pair_copy(chunk).start()
    for item in loads[:3]:
        item.wait()

    def pass_on(direction, chunk, first):
        sums = keep_ref[part(chunk), :]
        if not first:
            sums = sums + land_ref[direction, part(chunk), :].astype(F32)
        out_ref[direction, part(chunk), :] = sums.astype(BF16)
        line_copy(direction, chunk).start()

    def pass_row(direction, first):
        row_ref[1 + direction] = row_ref[0] if first else row_ref[0] + row_ref[4 + direction]
        row_copy(1 + direction).start()

    steps = CHUNKS + pairs - 1
    for step in range(steps):
        if step < CHUNKS:
            pair_copy(step).wait_recv()
            keep_ref[part(step), :] += pair_ref[part(step), :].astype(F32)
            if step == 0:
                row_copy(0).wait()
                row_ref[0] += row_ref[3]
            for direction, (here, there) in enumerate(((behind, ahead), (ahead, behind))):

                @pl.when(jnp.logical_not(here) & there)
                def _(direction=direction, step=step):
                    pass_on(direction, step, True)
                    if step == 0:
                        pass_row(direction, True)

        for direction, (here, there) in enumerate(((behind, ahead), (ahead, behind))):
            chunk = step - (place if direction == 0 else pairs - 1 - place)

            @pl.when(here & (chunk >= 0) & (chunk < CHUNKS))
            def _(direction=direction, chunk=chunk, there=there):
                line_copy(direction, chunk).wait_recv()

                @pl.when(there)
                def _():
                    pass_on(direction, chunk, False)

                @pl.when(chunk == 0)
                def _():
                    row_copy(1 + direction).wait_recv()

                    @pl.when(there)
                    def _():
                        pass_row(direction, False)

        for number in range(step * MB * tiles // steps, (step + 1) * MB * tiles // steps):
            back(number)

    total_ref[:rows, :] = keep_ref[...] + (land_ref[0].astype(F32) + land_ref[1].astype(F32))
    total_ref[rows:, :] = jnp.zeros((capacity + SUBLANES, keep_ref.shape[1]), F32)
    end_out_ref[...] = take_rows(total_ref, table_ref[STARTS + other], capacity, rows - 1).astype(BF16)
    end_copy.start()
    own_ref[...] = take_rows(total_ref, table_ref[STARTS + own], capacity, rows - 1)
    bias_out_ref[...] = row_ref[0] + (row_ref[4] + row_ref[5])
    end_copy.wait()
    got_ref[...] = end_in_ref[...]
    for chunk in range(CHUNKS):
        pair_copy(chunk).wait_send()
    for direction, there in enumerate((ahead, behind)):

        @pl.when(there)
        def _(direction=direction):
            row_copy(1 + direction).wait_send()
            for chunk in range(CHUNKS):
                line_copy(direction, chunk).wait_send()

    for item in stores:
        item.wait()


def sum_over_owners(table, groups, capacity, keep, sent, bias, weight, mate_weight, pres, mates, after=()):
    rows, half = keep.shape
    nodes, width = pres[0].shape
    flat = lambda i: (0, 0)
    shape = (capacity, half)
    return launch(
        "sum", functools.partial(sum_kernel, groups, capacity), table,
        [(array, None, None) for array in (keep, sent)]
        + [(bias, bias.shape, flat)]
        + [(array, None, None) for array in (weight, mate_weight, *pres, *mates)],
        [
            (shape, F32, shape, flat),
            (shape, BF16, shape, flat),
            (bias.shape, F32, bias.shape, flat),
            ((MB, nodes, width), BF16, None, None),
        ],
        after=after, barrier=SUM_ID, vmem=34,
        scratch=[
            pltpu.VMEM((MB, nodes, width), BF16),
            pltpu.VMEM((MB, nodes, width), BF16),
            pltpu.VMEM((2, width, width), BF16),
            pltpu.VMEM((MB, nodes, width), BF16),
            pltpu.SemaphoreType.DMA((3 + 2 * MB,)),
            pltpu.SemaphoreType.DMA((MB,)),
            pltpu.VMEM((rows, half), F32),
            pltpu.VMEM((rows, half), BF16),
            pltpu.VMEM((2, rows, half), BF16),
            pltpu.VMEM((2, rows, half), BF16),
            pltpu.VMEM((rows + capacity + SUBLANES, half), F32),
            pltpu.VMEM(shape, BF16),
            pltpu.VMEM(shape, BF16),
            pltpu.VMEM((6, 1, width), F32),
            pltpu.SemaphoreType.DMA((CHUNKS + 1,)),
            pltpu.SemaphoreType.DMA((CHUNKS + 1,)),
            pltpu.SemaphoreType.DMA((2, CHUNKS)),
            pltpu.SemaphoreType.DMA((2, CHUNKS)),
            pltpu.SemaphoreType.DMA((3,)),
            pltpu.SemaphoreType.DMA((3,)),
        ],
    )


def adamw_update(current, first_moment, second_moment, gradient, step_rate):
    first_new = BETA_ONE * first_moment + (1.0 - BETA_ONE) * gradient
    second_new = BETA_TWO * second_moment + (1.0 - BETA_TWO) * gradient * gradient
    fixed_first = first_new / (1.0 - BETA_ONE**STEP)
    fixed_second = second_new / (1.0 - BETA_TWO**STEP)
    updated = current - step_rate * (
        fixed_first / (jnp.sqrt(fixed_second) + EPSILON) + DECAY * current
    )
    return (updated, first_new, second_new)


def finish_kernel(groups, table_ref, *refs):
    done = MB - 1
    own_ref, got_ref, bias_grad_ref, biases = refs[0], refs[1], refs[2], refs[3:6]
    weights_hbm, out_parts, refs = refs[6:9], refs[9 : 9 + MB], refs[9 + MB :]
    back_hbm, gots, (scale_hbm, matrix_hbm), refs = refs[0], refs[1 : 1 + done], refs[1 + done : 3 + done], refs[3 + done :]
    updated_hbm, bias_outs, (out_hbm, grads_hbm, last_back_ref, last_matrix_ref), refs = refs[:3], refs[3:6], refs[6:10], refs[10:]
    weights, (weight_load, weight_store, store), refs = refs[:3], refs[3:6], refs[6:]
    jobs = [
        scatter_job(
            m, WIDE, pl.ds(0, back_hbm.shape[2]), back_hbm.at[m], gots[m], scale_hbm, matrix_hbm.at[m], grads_hbm,
            refs[7 * m : 7 * m + 6], refs[7 * m + 6],
        )
        for m in range(done)
    ]
    weight_loads = [
        pltpu.make_async_copy(source, target, weight_load.at[i])
        for i, (source, target) in enumerate(zip(weights_hbm, weights))
    ]
    weight_stores = [
        pltpu.make_async_copy(source, target, weight_store.at[i])
        for i, (source, target) in enumerate(zip(weights, updated_hbm))
    ]
    moves = [
        pltpu.make_async_copy(source, target, store.at[i])
        for i, (source, target) in enumerate(
            [(part, out_hbm.at[m]) for m, part in enumerate(out_parts)]
            + [(back_hbm.at[done], last_back_ref), (matrix_hbm.at[done], last_matrix_ref)]
        )
    ]
    for item in jobs[0][0] + weight_loads:
        item.start()
    for later, _, _ in jobs[1:]:
        for item in later:
            item.start()
    for item in moves:
        item.start()
    jobs[0][1]()

    for item in weight_loads:
        item.wait()
    rows, width = weights[0].shape
    half = width // 2
    strip = min(rows, TILE // 2)
    own = table_ref[GROUP]
    for first in range(0, rows, strip):
        row_ids = first + lax.broadcasted_iota(jnp.int32, (strip, half), 0)
        used = row_ids < table_ref[STARTS + groups + own]
        down = slice(first, first + strip)
        for side in range(2):
            mine = (own & 1) == side
            here, there = own_ref[down, :], got_ref[down, :].astype(F32)
            columns = slice(side * half, (side + 1) * half)
            results = adamw_update(*(ref[down, columns] for ref in weights), jnp.where(mine, here, there), RATE_WEIGHT)
            for ref, result in zip(weights, results):
                ref[down, columns] = jnp.where(used, result, 0.0)
    for item in weight_stores:
        item.start()
    results = adamw_update(*(ref[...] for ref in biases), bias_grad_ref[...], RATE_BIAS)
    for ref, result in zip(bias_outs, results):
        ref[...] = result

    for _, work, _ in jobs[1:]:
        work()
    for item in weight_stores + moves:
        item.wait()
    for _, _, stores in jobs:
        for item in stores:
            item.wait()


def finish(table, groups, mine, other, bias_grad, biases, weights, outputs, backs, gots, scale, matrix, after=()):
    capacity, width = weights[0].shape
    nodes = outputs[0].array.shape[0]
    fixed = lambda i: (0, 0)
    scratch = [pltpu.VMEM((capacity, width), F32)] * 3 + [
        pltpu.SemaphoreType.DMA((3,)),
        pltpu.SemaphoreType.DMA((3,)),
        pltpu.SemaphoreType.DMA((MB + 2,)),
    ]
    for _ in gots:
        scratch += scatter_scratch(nodes, width)
    return launch(
        "finish", functools.partial(finish_kernel, groups), table,
        [(array, array.array.shape, fixed) for array in (mine, other)]
        + [(array, (1, width), fixed) for array in (bias_grad, *biases)]
        + [(array, None, None) for array in (*weights, *outputs, backs, *gots, scale, matrix)],
        [((capacity, width), F32, None, None)] * 3
        + [((1, width), F32, (1, width), fixed)] * 3
        + [((MB, nodes, width), BF16, None, None)] * 2
        + [((nodes, width), BF16, None, None, pltpu.VMEM), ((nodes, nodes), BF16, None, None, pltpu.VMEM)],
        after=after, scratch=scratch, vmem=32,
    )


def shards(
    features,
    neighbours,
    node_counts,
    row_counts,
    master_weight,
    weight_first,
    weight_second,
    master_bias,
    bias_first,
    bias_second,
    out_grad,
):
    groups = lax.axis_size("clus")
    capacity, width = master_weight.shape
    owner_ids = jnp.arange(groups, dtype=jnp.int32)
    starts = jnp.sum(jnp.where(owner_ids[None, :] < owner_ids[:, None], row_counts[None, :], 0), axis=1)
    table = jnp.concatenate(
        [
            jnp.stack([lax.axis_index("clus"), lax.axis_index("col")]).astype(jnp.int32),
            node_counts[:, 0],
            starts.astype(jnp.int32),
            row_counts,
        ]
    )
    bias_row, bias_first_row, bias_second_row = (
        array.reshape(1, width) for array in (master_bias, bias_first, bias_second)
    )

    picked = pick_first(features)
    picked = picked + pick(features, tuple(range(1, MB)), [Kept(picked[0])])
    far = [Kept(flip(array, "col", 2), None) for array in picked]

    matrix, scale, here, slots = front(
        table, groups, master_weight, jnp.swapaxes(neighbours, 1, 2), features, [picked[-1]]
    )
    scale = Kept(scale)
    weight, for_mate = (Kept(array) for array in place(table, slots))
    last = for_mate
    total, bias_sum = None, None
    outputs, pres, mates, away = [], [], [], []
    for m in range(MB):
        widths = (width - width // 4, width // 4) if m == MB - 1 else (width,)
        chunks = len(widths)
        out_m, pre_m, mate_m, *rest = batch(
            table, m, matrix, scale, far[m], here, weight, for_mate, out_grad, bias_row, total, bias_sum, widths,
            [last],
        )
        outputs.append(Kept(out_m))
        pres.append(pre_m)
        mates.append(mate_m)
        away.append([Kept(flip(chunk, "col", 2), None) for chunk in rest[:chunks]])
        total, bias_sum = Kept(rest[chunks]), rest[-1]
        last = bias_sum

    mate_weight, keep, sent, bias_sum = rest[chunks:]
    mine, other, bias_total, backs = sum_over_owners(
        table, groups, capacity, keep, sent, bias_sum, weight, mate_weight, pres, mates, [last]
    )
    *updated, outputs, input_grads, last_back, last_matrix = finish(
        table, groups, Kept(mine, None), Kept(other, None), bias_total, (bias_row, bias_first_row, bias_second_row),
        (master_weight, weight_first, weight_second), outputs, backs, [part[0] for part in away[:-1]],
        scale, matrix, [bias_total],
    )
    for chunk, got in enumerate(away[-1]):
        input_grads = scatter(MB - 1, sum(widths[:chunk]), Kept(last_back), got, scale, Kept(last_matrix), input_grads)
    return (outputs, input_grads, *updated[:3], *(row.reshape(width) for row in updated[3:]))


def solution(mesh):
    in_specs = (
        P(None, "clus", "col"),
        P(None, "clus", None),
        P(None, "clus"),
        P(),
        P("clus", "col"),
        P("clus", "col"),
        P("clus", "col"),
        P("col"),
        P("col"),
        P("col"),
        P(None, "clus", "col"),
    )
    out_specs = (
        P(None, "clus", "col"),
        P(None, "clus", "col"),
        P("clus", "col"),
        P("clus", "col"),
        P("clus", "col"),
        P("col"),
        P("col"),
        P("col"),
    )
    return jax.shard_map(shards, mesh=mesh, in_specs=in_specs, out_specs=out_specs, check_vma=False)
```

```python
import functools

import jax
import jax.numpy as jnp
from jax import lax
from jax.experimental import pallas as pl
from jax.experimental.pallas import tpu as pltpu
from jax.sharding import PartitionSpec as P

D = 2048
MB = 3
STEP = 10

BETA_ONE = 0.9
BETA_TWO = 0.95
EPSILON = 1e-08
DECAY = 0.1
RATE_WEIGHT = 0.06
RATE_BIAS = 0.6

LANES = 128
DIGIT_BITS = 5
DIGITS = 6
STRIP = 32
SUBLANES = 8
TILE = 256
WIDE = 512
HALVES = 2
PIECES = 4
UNROLL = 3
CHUNKS = 8
MIB = 1024 * 1024
SMALL = 1 << 16

GROUP, COLUMN, LIMITS = 0, 1, 2
STARTS = LIMITS + MB

FRONT_ID, SUM_ID, BATCH_ID = 1, 2, 3

F32, BF16 = jnp.float32, jnp.bfloat16


class Kept:
    def __init__(self, array, space=pltpu.VMEM):
        self.array, self.space = array, space


def located(item):
    if isinstance(item, Kept):
        return pltpu.with_memory_space_constraint(item.array, item.space) if item.space else item.array
    return pltpu.with_memory_space_constraint(item, pltpu.HBM) if item.size > SMALL else item


def launch(name, body, table, ins, outs, grid=(1,), after=(), alias=None, scratch=(), barrier=None, vmem=16):
    tables = [] if table is None else [table]

    def spec(block, index):
        if block is None:
            return pl.BlockSpec(memory_space=pl.ANY)
        return pl.BlockSpec(block, lambda *a: index(*a[: len(grid)]))

    unread = ([alias[0]] if alias else []) + [array for array in after if alias is None or array is not alias[0]]

    def kernel(*refs):
        table_refs, refs = refs[: len(tables)], refs[len(tables) :]
        body(*table_refs, *refs[: len(ins)], *refs[len(ins) + len(unread) :])

    return pl.pallas_call(
        kernel,
        grid_spec=pltpu.PrefetchScalarGridSpec(
            num_scalar_prefetch=len(tables),
            grid=grid,
            in_specs=[spec(block, index) for _, block, index in ins]
            + [pl.BlockSpec(memory_space=pl.ANY)] * len(unread),
            out_specs=[spec(out[2], out[3]) for out in outs],
            scratch_shapes=list(scratch),
        ),
        out_shape=[
            (out[4] if len(out) > 4 else pltpu.HBM if out[2] is None else jax.ShapeDtypeStruct)(out[0], out[1])
            for out in outs
        ],
        input_output_aliases={len(tables) + len(ins): alias[1]} if alias else {},
        compiler_params=pltpu.CompilerParams(
            vmem_limit_bytes=vmem * MIB, collective_id=barrier, has_side_effects=barrier is not None
        ),
        cost_estimate=pl.CostEstimate(flops=1, bytes_accessed=1, transcendentals=0),
        name=name,
    )(*tables, *(located(item[0]) for item in ins), *(located(item) for item in unread))


def flip(values, axis, bit):
    size = lax.axis_size(axis)
    return lax.ppermute(values, axis, [(i, i ^ bit) for i in range(size)])


def partner(index, bit):
    return index + bit * (1 - 2 * ((index // bit) % 2))


def product(left, right):
    return jnp.dot(left, right, preferred_element_type=F32)


def product_back(left, right):
    return lax.dot_general(left, right, (((1,), (1,)), ((), ())), preferred_element_type=F32)


def product_rows(left, right):
    return lax.dot_general(left, right, (((0,), (0,)), ((), ())), preferred_element_type=F32)


def scaled(values, scale):
    return values * jnp.concatenate([scale] * (values.shape[1] // LANES), axis=1)


def put_rows(ref, first, rows):
    base = pl.multiple_of((first // SUBLANES) * SUBLANES, SUBLANES)
    offset = first - base
    moved = jnp.concatenate([rows, jnp.zeros((SUBLANES, rows.shape[1]), rows.dtype)], axis=0)
    wanted = jnp.broadcast_to(offset, moved.shape)
    for bit in (1, 2, 4):
        moved = jnp.where((wanted & bit) != 0, pltpu.roll(moved, bit, 0), moved)
    head = ref[pl.ds(base, SUBLANES), :]
    row_ids = lax.broadcasted_iota(jnp.int32, head.shape, 0)
    ref[pl.ds(base, SUBLANES), :] = jnp.where(row_ids < offset, head, moved[:SUBLANES])
    ref[pl.ds(pl.multiple_of(base + SUBLANES, SUBLANES), rows.shape[0]), :] = moved[SUBLANES:]


def take_rows(ref, first, count, largest):
    bit = 1 << (largest.bit_length() - 1)
    rows = ref[...]
    while bit:
        length = count + max(bit, SUBLANES)
        if bit >= SUBLANES:
            moved = rows[bit : bit + length]
            missing = length - moved.shape[0]
            if missing:
                moved = jnp.concatenate([moved, jnp.zeros((missing, rows.shape[1]), rows.dtype)], axis=0)
        else:
            moved = pltpu.roll(rows, length - bit, 0)
        chosen = (jnp.broadcast_to(first, (length, rows.shape[1])) & bit) != 0
        rows = jnp.where(chosen, moved, rows[:length])
        bit //= 2
    return rows[:count]


def relay(sources, targets, buffers, load, store):
    def piece(ref, i):
        rows = ref.shape[0] // PIECES
        return ref.at[pl.ds(i * rows, rows)]

    loads, stores = [], []
    for number, (source, target, buffer) in enumerate(zip(sources, targets, buffers)):
        for i in range(PIECES):
            place = number * PIECES + i
            loads.append(pltpu.make_async_copy(piece(source, i), piece(buffer, i), load.at[place]))
            stores.append(pltpu.make_async_copy(piece(buffer, i), piece(target, i), store.at[place]))
    return loads, stores


def pick_kernel(batches, source_ref, *refs):
    targets, (buffer_ref, load, store) = refs[:-3], refs[-3:]
    loads, stores = relay(
        [source_ref.at[m] for m in batches], targets, [buffer_ref.at[i] for i in range(len(batches))], load, store
    )
    for item in loads:
        item.start()
    for item, onward in zip(loads, stores):
        item.wait()
        onward.start()
    for item in stores:
        item.wait()


def pick(stacked, batches, after=()):
    count = len(batches)
    return launch(
        f"pick{batches[0]}", functools.partial(pick_kernel, batches), None,
        [(stacked, None, None)], [(stacked.shape[1:], stacked.dtype, None, None)] * count,
        after=after,
        scratch=[
            pltpu.VMEM((count, *stacked.shape[1:]), stacked.dtype),
            pltpu.SemaphoreType.DMA((count * PIECES,)),
            pltpu.SemaphoreType.DMA((count * PIECES,)),
        ],
    )


def count_tile(limit, first, neighbour_ref, matrix_ref, scale_ref, lanes):
    nodes = matrix_ref.shape[1]
    words = -(-(nodes // LANES) // DIGITS)
    entries = neighbour_ref[0, :, lanes]
    node_ids = first + lax.broadcasted_iota(jnp.int32, entries.shape, 1)
    valid = (entries < limit) & (node_ids < limit)
    low = entries & (LANES - 1)
    high = entries >> 7
    digits = []
    for word in range(words):
        inside = valid & (high >= word * DIGITS) & (high < (word + 1) * DIGITS)
        shift = jnp.where(inside, (high - word * DIGITS) * DIGIT_BITS, 0)
        digits.append(jnp.where(inside, jnp.left_shift(1, shift), 0))
    for strip in range(LANES // STRIP):
        row_ids = strip * STRIP + lax.broadcasted_iota(jnp.int32, (STRIP, LANES), 0)
        sums = [jnp.zeros((STRIP, LANES), jnp.int32) for _ in range(words)]
        for entry in range(entries.shape[0]):
            hit = row_ids == low[entry : entry + 1, :]
            for word in range(words):
                sums[word] = sums[word] + jnp.where(hit, digits[word][entry : entry + 1, :], 0)
        for block in range(nodes // LANES):
            word, digit = block // DIGITS, block % DIGITS
            count = jnp.right_shift(sums[word], digit * DIGIT_BITS) & ((1 << DIGIT_BITS) - 1)
            rows = slice(block * LANES + strip * STRIP, block * LANES + (strip + 1) * STRIP)
            matrix_ref[0, rows, lanes] = count.astype(F32).astype(BF16)
    rows = pl.ds(pl.multiple_of(first, LANES), LANES)
    square = matrix_ref[0, rows, lanes].astype(F32)
    on_diagonal = lax.broadcasted_iota(jnp.int32, square.shape, 0) == lax.broadcasted_iota(jnp.int32, square.shape, 1)
    matrix_ref[0, rows, lanes] = jnp.where(on_diagonal, 2.0 * square + 2.0, square).astype(BF16)
    degree = 1.0 + jnp.sum(valid.astype(F32), axis=0, keepdims=True)
    factor = (node_ids[:1] < limit).astype(F32) / degree
    scale_ref[0, lanes, :] = jnp.transpose(jnp.broadcast_to(factor, (LANES, LANES)))


def front_kernel(
    groups, total, table_ref, master_ref, neighbour_ref, feature_ref, matrix_ref, scale_ref, mixed_ref, slots_ref,
    block_ref, local_semaphore, line_send, line_receive, pair_send, pair_receive,
):
    batch, tile_id = pl.program_id(0), pl.program_id(1)
    tiles = pl.num_programs(1)
    step = batch * tiles + tile_id
    own = lax.axis_index("clus")
    place, side = own // 2, own % 2
    pairs = groups // 2
    other = partner(own, 1)

    def rows_of(half):
        size = block_ref.shape[0] // HALVES
        return pl.ds(half * size, size)

    def remote(source, target, sent, received, device):
        return pltpu.make_async_remote_copy(
            src_ref=source,
            dst_ref=target,
            send_sem=sent,
            recv_sem=received,
            device_id={"clus": device},
            device_id_type=pl.DeviceIdType.MESH,
        )

    def origin_of(direction, hop):
        return place - 1 - hop if direction == 0 else place + 1 + hop

    def line_copy(direction, hop, half):
        slot = (place - hop if direction == 0 else place + hop) * 2 + side
        target = slots_ref.at[slot, rows_of(half)]
        return remote(
            block_ref.at[rows_of(half)] if hop == 0 else target, target,
            line_send.at[direction, hop, half], line_receive.at[direction, hop, half],
            own + 2 if direction == 0 else own - 2,
        )

    def sends(direction, hop):
        if direction == 0:
            return (place - hop >= 0) & (place + 1 < pairs)
        return (place + hop < pairs) & (place - 1 >= 0)

    def arrives(direction, hop):
        return place - 1 - hop >= 0 if direction == 0 else place + 1 + hop < pairs

    def arrival(direction, hop, half):
        target = slots_ref.at[origin_of(direction, hop) * 2 + side, rows_of(half)]
        return remote(
            target, target, line_send.at[direction, hop, half], line_receive.at[direction, hop, half], other
        )

    def pair_copy(direction, hop, half):
        slot = own if hop < 0 else origin_of(direction, hop) * 2 + side
        number = 0 if hop < 0 else 1 + 2 * hop + direction
        target = slots_ref.at[slot, rows_of(half)]
        return remote(
            block_ref.at[rows_of(half)] if hop < 0 else target, target,
            pair_send.at[number, half], pair_receive.at[number, half], other,
        )

    def pair_arrival(direction, hop, half):
        slot = other if hop < 0 else origin_of(direction, hop) * 2 + 1 - side
        number = 0 if hop < 0 else 1 + 2 * hop + direction
        target = slots_ref.at[slot, rows_of(half)]
        return remote(target, target, pair_send.at[number, half], pair_receive.at[number, half], other)

    local_copy = pltpu.make_async_copy(block_ref, slots_ref.at[own], local_semaphore)
    hops = pairs - 1

    @pl.when(step == 0)
    def _():
        barrier = pltpu.get_barrier_semaphore()

        def greet(index):
            pl.semaphore_signal(barrier, inc=1, device_id={"clus": index}, device_id_type=pl.DeviceIdType.MESH)

        greet(other)

        @pl.when(place + 1 < pairs)
        def _():
            greet(own + 2)

        @pl.when(place - 1 >= 0)
        def _():
            greet(own - 2)

        pl.semaphore_wait(barrier, 1 + jnp.where(place + 1 < pairs, 1, 0) + jnp.where(place - 1 >= 0, 1, 0))
        block_ref[...] = master_ref[...].astype(BF16)
        for half in range(HALVES):
            for direction in range(2):
                pl.when(sends(direction, 0))(line_copy(direction, 0, half).start)
            pair_copy(0, -1, half).start()
        local_copy.start()

    limit = table_ref[LIMITS + batch]
    tile = mixed_ref.shape[1]
    for part in range(tile // LANES):
        first = tile_id * tile + part * LANES
        count_tile(limit, first, neighbour_ref, matrix_ref, scale_ref, slice(part * LANES, (part + 1) * LANES))
    mixed_ref[0] = scaled(product_rows(matrix_ref[0], feature_ref[0]), scale_ref[0]).astype(BF16)

    for event in range(hops * HALVES):
        hop, half = event // HALVES, event % HALVES

        @pl.when(step == min(total - 1, ((event + 1) * total) // (hops * HALVES)))
        def _(hop=hop, half=half):
            for direction in range(2):

                @pl.when(arrives(direction, hop))
                def _(direction=direction):
                    arrival(direction, hop, half).wait_recv()
                    pair_copy(direction, hop, half).start()

                if hop + 1 < hops:
                    pl.when(sends(direction, hop + 1))(line_copy(direction, hop + 1, half).start)

    @pl.when(step == total - 1)
    def _():
        local_copy.wait()
        for half in range(HALVES):
            pair_copy(0, -1, half).wait_send()
            pair_arrival(0, -1, half).wait_recv()
            for hop in range(hops):
                for direction in range(2):
                    pl.when(sends(direction, hop))(line_copy(direction, hop, half).wait_send)

                    @pl.when(arrives(direction, hop))
                    def _(direction=direction, hop=hop, half=half):
                        pair_copy(direction, hop, half).wait_send()
                        pair_arrival(direction, hop, half).wait_recv()


def front(table, groups, master, neighbours, features, after=()):
    _, entries, nodes = neighbours.shape
    capacity, width = master.shape
    hops = groups // 2 - 1
    steps = MB * (nodes // TILE)
    return launch(
        "front", functools.partial(front_kernel, groups, steps), table,
        [
            (master, (capacity, width), lambda b, i: (0, 0)),
            (neighbours, (1, entries, TILE), lambda b, i: (b, 0, i)),
            (features, (1, nodes, width), lambda b, i: (b, 0, 0)),
        ],
        [
            ((MB, nodes, nodes), BF16, (1, nodes, TILE), lambda b, i: (b, 0, i), pltpu.HBM),
            ((MB, nodes, LANES), F32, (1, TILE, LANES), lambda b, i: (b, i, 0), pltpu.VMEM),
            ((MB, nodes, width), BF16, (1, TILE, width), lambda b, i: (b, i, 0), pltpu.HBM),
            ((groups, capacity, width), BF16, None, None),
        ],
        grid=(MB, nodes // TILE), after=after, barrier=FRONT_ID, vmem=20,
        scratch=[
            pltpu.VMEM((capacity, width), BF16),
            pltpu.SemaphoreType.DMA,
            pltpu.SemaphoreType.DMA((2, hops, HALVES)),
            pltpu.SemaphoreType.DMA((2, hops, HALVES)),
            pltpu.SemaphoreType.DMA((1 + 2 * hops, HALVES)),
            pltpu.SemaphoreType.DMA((1 + 2 * hops, HALVES)),
        ],
    )


def greet_mate(mate):
    barrier = pltpu.get_barrier_semaphore()
    pl.semaphore_signal(barrier, inc=1, device_id={"col": mate}, device_id_type=pl.DeviceIdType.MESH)
    pl.semaphore_wait(barrier, 1)


def place_kernel(groups, table_ref, slots_ref, weight_ref, mate_ref, rows_ref):
    owner = pl.program_id(0)

    @pl.when(owner == 0)
    def _():
        rows_ref[...] = jnp.zeros_like(rows_ref)

    put_rows(rows_ref, table_ref[STARTS + owner], slots_ref[0].astype(F32))

    @pl.when(owner == groups - 1)
    def _():
        width = weight_ref.shape[2]
        for block in range(weight_ref.shape[0]):
            source = pl.multiple_of((table_ref[COLUMN] ^ block) * width, width)
            rows = rows_ref[pl.ds(source, width), :].astype(BF16)
            weight_ref[block] = rows
            if block % 2:
                mate_ref[block // 2] = rows


def place(table, slots, after=()):
    groups, capacity, width = slots.shape
    blocks = D // width
    return launch(
        "place", functools.partial(place_kernel, groups), table,
        [(slots, (1, capacity, width), lambda i: (i, 0, 0))],
        [
            ((blocks, width, width), BF16, (blocks, width, width), lambda i: (0, 0, 0), pltpu.VMEM),
            ((blocks // 2, width, width), BF16, (blocks // 2, width, width), lambda i: (0, 0, 0), pltpu.VMEM),
        ],
        grid=(groups,), after=after, vmem=24, scratch=[pltpu.VMEM((D + capacity + SUBLANES, width), F32)],
    )


def batch_kernel(m, widths, table_ref, *refs):
    matrix_hbm, scale_hbm, far_hbm, here_hbm, weight_hbm, for_mate_hbm, grad_hbm, bias_ref = refs[:8]
    refs, chunks = refs[8:], len(widths)
    total_hbm, bias_sum_in = refs[:2] if m else (None, None)
    refs = refs[2:] if m else refs
    ended = m == MB - 1
    out_hbm, pre_hbm, mate_pre_hbm = refs[:3]
    away_hbm, refs = refs[3 : 3 + chunks], refs[3 + chunks :]
    mate_weight_hbm, refs = (refs[0], refs[1:]) if ended else (None, refs)
    results, refs = (refs[:2], refs[2:]) if ended else (refs[:1], refs[1:])
    bias_sum_ref, refs = refs[0], refs[1:]
    (
        matrix_ref, scale_ref, far_ref, mixed_ref, weight_ref, mate_weight_ref, grad_ref, out_ref, pre_ref, mate_pre_ref,
        away_ref, total_ref, load, store, send, receive,
    ) = refs[:16]
    parts = refs[16:]
    nodes, width = far_ref.shape
    wide, narrow = nodes // WIDE, nodes // TILE
    mate = partner(lax.axis_index("col"), 1)

    def at(index, size):
        return pl.ds(pl.multiple_of(index * size, size), size)

    def matrix_load(i):
        return pltpu.make_async_copy(
            matrix_hbm.at[m, :, at(i, WIDE)], matrix_ref.at[:, at(i, WIDE)], load.at[i]
        )

    loads = [
        pltpu.make_async_copy(source, target, load.at[wide + i])
        for i, (source, target) in enumerate(
            [
                (far_hbm, far_ref),
                (scale_hbm.at[m], scale_ref),
                (weight_hbm, weight_ref),
                (here_hbm.at[m], mixed_ref.at[0]),
                (grad_hbm.at[m], grad_ref),
            ]
            + ([(total_hbm, total_ref)] if m else [])
        )
    ]
    started = []

    def save(source, target):
        started.append(pltpu.make_async_copy(source, target, store.at[len(started)]))
        started[-1].start()

    def remote(source, target, number):
        return pltpu.make_async_remote_copy(
            src_ref=source,
            dst_ref=target,
            send_sem=send.at[number],
            recv_sem=receive.at[number],
            device_id={"col": mate},
            device_id_type=pl.DeviceIdType.MESH,
        )

    here_copy = remote(here_hbm.at[m], mixed_ref.at[1], 0)
    weight_copy = remote(for_mate_hbm, mate_weight_ref, 1)

    def there_copy(i):
        return remote(mixed_ref.at[2, at(i, WIDE)], mixed_ref.at[3, at(i, WIDE)], 2 + i)

    def pre_copy(i):
        return remote(pre_ref.at[at(i, TILE)], mate_pre_ref.at[at(i, TILE)], 2 + wide + i)

    loads[0].start()
    matrix_load(0).start()
    loads[1].start()
    for i in range(1, wide):
        matrix_load(i).start()
    for item in loads[2:]:
        item.start()
    greet_mate(mate)
    here_copy.start()
    loads[0].wait()
    loads[1].wait()

    @pl.loop(0, wide)
    def _(i):
        matrix_load(i).wait()
        rows = at(i, WIDE)
        there = product_rows(matrix_ref[:, rows], far_ref[...])
        mixed_ref[2, rows, :] = scaled(there, scale_ref[rows, :]).astype(BF16)
        there_copy(i).start()

    weight_copy.start()
    for item in loads[2:5]:
        item.wait()
    here_copy.wait_recv()
    bias_sum_ref[...] = bias_sum_in[...] if m else jnp.zeros_like(bias_sum_ref)
    for i in range(wide):
        there_copy(i).wait_recv()

    @pl.loop(0, narrow, unroll=UNROLL)
    def _(i):
        rows = at(i, TILE)
        preact = bias_ref[...]
        for block in range(4):
            preact = preact + product(mixed_ref[block, rows, :], weight_ref[block])
        row_ids = i * TILE + lax.broadcasted_iota(jnp.int32, preact.shape, 0)
        live = row_ids < table_ref[LIMITS + m]
        gate = jax.nn.sigmoid(preact)
        out_ref[rows, :] = jnp.where(live, preact * gate, 0.0).astype(BF16)
        slope = gate * (1.0 + preact * (1.0 - gate))
        grad_pre = jnp.where(live, grad_ref[rows, :].astype(F32) * slope, 0.0).astype(BF16)
        pre_ref[rows, :] = grad_pre
        pre_copy(i).start()
        bias_sum_ref[...] += jnp.sum(grad_pre.astype(F32), axis=0, keepdims=True)

    save(pre_ref, pre_hbm)
    save(out_ref, out_hbm)
    if m:
        loads[5].wait()

    @pl.loop(0, 4)
    def _(block):
        term = product_rows(mixed_ref[block], pre_ref[...])
        total_ref[block] = total_ref[block] + term if m else term

    if ended:
        half = width // 2
        upper = lax.axis_index("clus") % 2 == 1
        column = lax.axis_index("col")
        for block in range(4):
            source = partner(column, 1) if block % 2 else column
            source = partner(source, 2) if block >= 2 else source
            rows = at(source, width)
            low, high = total_ref[block, :, :half], total_ref[block, :, half:]
            parts[0][rows, :] = jnp.where(upper, high, low)
            parts[1][rows, :] = jnp.where(upper, low, high).astype(BF16)
        for part, result in zip(parts, results):
            save(part, result)
    else:
        save(total_ref, results[0])

    weight_copy.wait_recv()
    for i in range(narrow):
        pre_copy(i).wait_recv()
    save(mate_pre_ref, mate_pre_hbm)
    if ended:
        save(mate_weight_ref, mate_weight_hbm)
    for i in range(wide):
        rows = slice(i * WIDE, (i + 1) * WIDE)
        away = product_back(pre_ref[rows, :], weight_ref[2]) + product_back(mate_pre_ref[rows, :], mate_weight_ref[1])
        away_ref[rows, :] = away.astype(BF16)
        for chunk in range(chunks):
            columns = slice(sum(widths[:chunk]), sum(widths[: chunk + 1]))
            save(away_ref.at[rows, columns], away_hbm[chunk].at[rows])
    here_copy.wait_send()
    weight_copy.wait_send()
    for i in range(wide):
        there_copy(i).wait_send()
    for i in range(narrow):
        pre_copy(i).wait_send()
    for item in started:
        item.wait()


def batch(table, m, matrix, scale, far, here, weight, for_mate, out_grad, bias, total, bias_sum, widths, after=()):
    nodes, width = far.array.shape
    wide, narrow, chunks = nodes // WIDE, nodes // TILE, len(widths)
    flat = lambda i: (0, 0)
    ended = m == MB - 1
    parts = [((D, width // 2), F32), ((D, width // 2), BF16)] if ended else []
    results = [(*part, None, None) for part in parts]
    if not ended:
        results = [((4, width, width), F32, None, None, pltpu.VMEM)]
    return launch(
        f"batch{m}", functools.partial(batch_kernel, m, widths), table,
        [(array, None, None) for array in (matrix, scale, far, here, weight, for_mate, out_grad)]
        + [(bias, (1, width), flat)]
        + ([(total, None, None), (bias_sum, (1, width), flat)] if m else []),
        [((nodes, width), BF16, None, None, pltpu.VMEM)]
        + [((nodes, width), BF16, None, None)] * 2
        + [((nodes, columns), BF16, None, None) for columns in widths]
        + ([(for_mate.array.shape, BF16, None, None)] if ended else [])
        + results
        + [((1, width), F32, (1, width), flat)],
        after=after, barrier=BATCH_ID + m, vmem=34 if m == MB - 1 else 32,
        scratch=[
            pltpu.VMEM((nodes, nodes), BF16),
            pltpu.VMEM((nodes, LANES), F32),
            pltpu.VMEM((nodes, width), BF16),
            pltpu.VMEM((4, nodes, width), BF16),
            pltpu.VMEM(weight.array.shape, BF16),
            pltpu.VMEM(for_mate.array.shape, BF16),
            pltpu.VMEM((nodes, width), BF16),
            pltpu.VMEM((nodes, width), BF16),
            pltpu.VMEM((nodes, width), BF16),
            pltpu.VMEM((nodes, width), BF16),
            pltpu.VMEM((nodes, width), BF16),
            pltpu.VMEM((4, width, width), F32),
            pltpu.SemaphoreType.DMA((wide + 6,)),
            pltpu.SemaphoreType.DMA((6 + wide * chunks,)),
            pltpu.SemaphoreType.DMA((2 + wide + narrow,)),
            pltpu.SemaphoreType.DMA((2 + wide + narrow,)),
        ]
        + [pltpu.VMEM(*part) for part in parts],
    )


def scatter_job(m, tile, columns, own_source, got_source, scale_source, matrix_source, grads_hbm, scratch, semaphores):
    own_ref, got_ref, scale_ref, matrix_ref, sum_ref, grad_ref = scratch
    steps = matrix_ref.shape[0] // tile
    loads = [
        pltpu.make_async_copy(source, target, semaphores.at[i])
        for i, (source, target) in enumerate(
            [(own_source.at[:, columns], own_ref), (got_source, got_ref), (scale_source.at[m], scale_ref)]
        )
    ]
    tiles, stores = [], []
    for i in range(steps):
        rows = pl.ds(i * tile, tile)
        tiles.append(pltpu.make_async_copy(matrix_source.at[rows], matrix_ref.at[rows], semaphores.at[3 + i]))
        stores.append(
            pltpu.make_async_copy(grad_ref.at[rows], grads_hbm.at[m, rows, columns], semaphores.at[3 + steps + i])
        )

    def work():
        for item in loads:
            item.wait()
        grad_mixed = (own_ref[...].astype(F32) + got_ref[...].astype(F32)).astype(BF16)
        sum_ref[...] = scaled(grad_mixed.astype(F32), scale_ref[...]).astype(BF16)
        for i in range(steps):
            tiles[i].wait()
            rows = slice(i * tile, (i + 1) * tile)
            grad_ref[rows, :] = product(matrix_ref[rows, :], sum_ref[...]).astype(BF16)
            stores[i].start()

    return loads + tiles, work, stores


def scatter_scratch(nodes, width):
    return [
        pltpu.VMEM((nodes, width), BF16),
        pltpu.VMEM((nodes, width), BF16),
        pltpu.VMEM((nodes, LANES), F32),
        pltpu.VMEM((nodes, nodes), BF16),
        pltpu.VMEM((nodes, width), BF16),
        pltpu.VMEM((nodes, width), BF16),
        pltpu.SemaphoreType.DMA((3 + 2 * (nodes // WIDE),)),
    ]


def scatter_kernel(m, first, own_hbm, got_hbm, scale_hbm, matrix_hbm, grads_hbm, *refs):
    width = got_hbm.shape[1]
    loads, work, stores = scatter_job(
        m, own_hbm.shape[0], pl.ds(first, width), own_hbm, got_hbm, scale_hbm, matrix_hbm, grads_hbm, refs[:6], refs[6]
    )
    for item in loads:
        item.start()
    work()
    for item in stores:
        item.wait()


def scatter(m, first, own, got, scale, matrix, grads, after=()):
    nodes, width = own.array.shape
    return launch(
        f"scatter{m}_{first}", functools.partial(scatter_kernel, m, first), None,
        [(array, None, None) for array in (own, got, scale, matrix)],
        [((MB, nodes, width), BF16, None, None)],
        after=after, alias=(grads, 0), scratch=scatter_scratch(nodes, got.array.shape[1]),
    )[0]


def sum_kernel(groups, capacity, table_ref, *refs):
    keep_hbm, sent_hbm, bias_ref, weight_hbm, mate_weight_hbm = refs[:5]
    pre_hbm, mate_hbm, refs = refs[5 : 5 + MB], refs[5 + MB : 5 + 2 * MB], refs[5 + 2 * MB :]
    own_ref, got_ref, bias_out_ref, back_hbm, refs = *refs[:4], refs[4:]
    pre_ref, mate_ref, weights_ref, back_ref, load, store, refs = *refs[:6], refs[6:]
    keep_ref, pair_ref, land_ref, out_ref, total_ref, end_out_ref, end_in_ref, row_ref = refs[:8]
    pair_send, pair_receive, line_send, line_receive, row_send, row_receive = refs[8:]
    own = lax.axis_index("clus")
    place, pairs = own // 2, groups // 2
    other = partner(own, 1)
    rows = keep_ref.shape[0]
    size = rows // CHUNKS
    ahead, behind = place + 1 < pairs, place >= 1

    def remote(source, target, sent, received, device):
        return pltpu.make_async_remote_copy(
            src_ref=source,
            dst_ref=target,
            send_sem=sent,
            recv_sem=received,
            device_id={"clus": device},
            device_id_type=pl.DeviceIdType.MESH,
        )

    def part(chunk):
        return pl.ds(pl.multiple_of(chunk * size, size), size)

    def pair_copy(chunk):
        return remote(
            sent_hbm.at[part(chunk)], pair_ref.at[part(chunk)], pair_send.at[chunk], pair_receive.at[chunk], other
        )

    def line_copy(direction, chunk):
        return remote(
            out_ref.at[direction, part(chunk)], land_ref.at[direction, part(chunk)],
            line_send.at[direction, chunk], line_receive.at[direction, chunk],
            own + 2 if direction == 0 else own - 2,
        )

    def row_copy(number):
        device = (other, own + 2, own - 2)[number]
        return remote(row_ref.at[number], row_ref.at[3 + number], row_send.at[number], row_receive.at[number], device)

    end_copy = remote(end_out_ref, end_in_ref, pair_send.at[CHUNKS], pair_receive.at[CHUNKS], other)

    nodes = pre_ref.shape[1]
    tiles = nodes // WIDE
    loads = [
        pltpu.make_async_copy(source, target, load.at[i])
        for i, (source, target) in enumerate(
            [(keep_hbm, keep_ref), (weight_hbm.at[0], weights_ref.at[0]), (mate_weight_hbm.at[0], weights_ref.at[1])]
            + [(source, pre_ref.at[m]) for m, source in enumerate(pre_hbm)]
            + [(source, mate_ref.at[m]) for m, source in enumerate(mate_hbm)]
        )
    ]
    stores = [pltpu.make_async_copy(back_ref.at[m], back_hbm.at[m], store.at[m]) for m in range(MB)]

    def back(number):
        m, i = number // tiles, number % tiles
        if i == 0:
            loads[3 + m].wait()
            loads[3 + MB + m].wait()
        down = slice(i * WIDE, (i + 1) * WIDE)
        term = product_back(pre_ref[m, down, :], weights_ref[0]) + product_back(mate_ref[m, down, :], weights_ref[1])
        back_ref[m, down, :] = term.astype(BF16)
        if i == tiles - 1:
            stores[m].start()

    land_ref[...] = jnp.zeros_like(land_ref)
    row_ref[...] = jnp.zeros_like(row_ref)
    row_ref[0] = bias_ref[...]
    for item in loads:
        item.start()
    barrier = pltpu.get_barrier_semaphore()

    def greet(index):
        pl.semaphore_signal(barrier, inc=1, device_id={"clus": index}, device_id_type=pl.DeviceIdType.MESH)

    greet(other)

    @pl.when(ahead)
    def _():
        greet(own + 2)

    @pl.when(behind)
    def _():
        greet(own - 2)

    pl.semaphore_wait(barrier, 1 + jnp.where(ahead, 1, 0) + jnp.where(behind, 1, 0))
    row_copy(0).start()
    for chunk in range(CHUNKS):
        pair_copy(chunk).start()
    for item in loads[:3]:
        item.wait()

    def pass_on(direction, chunk, first):
        sums = keep_ref[part(chunk), :]
        if not first:
            sums = sums + land_ref[direction, part(chunk), :].astype(F32)
        out_ref[direction, part(chunk), :] = sums.astype(BF16)
        line_copy(direction, chunk).start()

    def pass_row(direction, first):
        row_ref[1 + direction] = row_ref[0] if first else row_ref[0] + row_ref[4 + direction]
        row_copy(1 + direction).start()

    steps = CHUNKS + pairs - 1
    for step in range(steps):
        if step < CHUNKS:
            pair_copy(step).wait_recv()
            keep_ref[part(step), :] += pair_ref[part(step), :].astype(F32)
            if step == 0:
                row_copy(0).wait()
                row_ref[0] += row_ref[3]
            for direction, (here, there) in enumerate(((behind, ahead), (ahead, behind))):

                @pl.when(jnp.logical_not(here) & there)
                def _(direction=direction, step=step):
                    pass_on(direction, step, True)
                    if step == 0:
                        pass_row(direction, True)

        for direction, (here, there) in enumerate(((behind, ahead), (ahead, behind))):
            chunk = step - (place if direction == 0 else pairs - 1 - place)

            @pl.when(here & (chunk >= 0) & (chunk < CHUNKS))
            def _(direction=direction, chunk=chunk, there=there):
                line_copy(direction, chunk).wait_recv()

                @pl.when(there)
                def _():
                    pass_on(direction, chunk, False)

                @pl.when(chunk == 0)
                def _():
                    row_copy(1 + direction).wait_recv()

                    @pl.when(there)
                    def _():
                        pass_row(direction, False)

        for number in range(step * MB * tiles // steps, (step + 1) * MB * tiles // steps):
            back(number)

    total_ref[:rows, :] = keep_ref[...] + (land_ref[0].astype(F32) + land_ref[1].astype(F32))
    total_ref[rows:, :] = jnp.zeros((capacity + SUBLANES, keep_ref.shape[1]), F32)
    end_out_ref[...] = take_rows(total_ref, table_ref[STARTS + other], capacity, rows - 1).astype(BF16)
    end_copy.start()
    own_ref[...] = take_rows(total_ref, table_ref[STARTS + own], capacity, rows - 1)
    bias_out_ref[...] = row_ref[0] + (row_ref[4] + row_ref[5])
    end_copy.wait()
    got_ref[...] = end_in_ref[...]
    for chunk in range(CHUNKS):
        pair_copy(chunk).wait_send()
    for direction, there in enumerate((ahead, behind)):

        @pl.when(there)
        def _(direction=direction):
            row_copy(1 + direction).wait_send()
            for chunk in range(CHUNKS):
                line_copy(direction, chunk).wait_send()

    for item in stores:
        item.wait()


def sum_over_owners(table, groups, capacity, keep, sent, bias, weight, mate_weight, pres, mates, after=()):
    rows, half = keep.shape
    nodes, width = pres[0].shape
    flat = lambda i: (0, 0)
    shape = (capacity, half)
    return launch(
        "sum", functools.partial(sum_kernel, groups, capacity), table,
        [(array, None, None) for array in (keep, sent)]
        + [(bias, bias.shape, flat)]
        + [(array, None, None) for array in (weight, mate_weight, *pres, *mates)],
        [
            (shape, F32, shape, flat),
            (shape, BF16, shape, flat),
            (bias.shape, F32, bias.shape, flat),
            ((MB, nodes, width), BF16, None, None),
        ],
        after=after, barrier=SUM_ID, vmem=34,
        scratch=[
            pltpu.VMEM((MB, nodes, width), BF16),
            pltpu.VMEM((MB, nodes, width), BF16),
            pltpu.VMEM((2, width, width), BF16),
            pltpu.VMEM((MB, nodes, width), BF16),
            pltpu.SemaphoreType.DMA((3 + 2 * MB,)),
            pltpu.SemaphoreType.DMA((MB,)),
            pltpu.VMEM((rows, half), F32),
            pltpu.VMEM((rows, half), BF16),
            pltpu.VMEM((2, rows, half), BF16),
            pltpu.VMEM((2, rows, half), BF16),
            pltpu.VMEM((rows + capacity + SUBLANES, half), F32),
            pltpu.VMEM(shape, BF16),
            pltpu.VMEM(shape, BF16),
            pltpu.VMEM((6, 1, width), F32),
            pltpu.SemaphoreType.DMA((CHUNKS + 1,)),
            pltpu.SemaphoreType.DMA((CHUNKS + 1,)),
            pltpu.SemaphoreType.DMA((2, CHUNKS)),
            pltpu.SemaphoreType.DMA((2, CHUNKS)),
            pltpu.SemaphoreType.DMA((3,)),
            pltpu.SemaphoreType.DMA((3,)),
        ],
    )


def adamw_update(current, first_moment, second_moment, gradient, step_rate):
    first_new = BETA_ONE * first_moment + (1.0 - BETA_ONE) * gradient
    second_new = BETA_TWO * second_moment + (1.0 - BETA_TWO) * gradient * gradient
    fixed_first = first_new / (1.0 - BETA_ONE**STEP)
    fixed_second = second_new / (1.0 - BETA_TWO**STEP)
    updated = current - step_rate * (
        fixed_first / (jnp.sqrt(fixed_second) + EPSILON) + DECAY * current
    )
    return (updated, first_new, second_new)


def finish_kernel(groups, table_ref, *refs):
    done = MB - 1
    own_ref, got_ref, bias_grad_ref, biases = refs[0], refs[1], refs[2], refs[3:6]
    weights_hbm, out_parts, refs = refs[6:9], refs[9 : 9 + MB], refs[9 + MB :]
    back_hbm, gots, (scale_hbm, matrix_hbm), refs = refs[0], refs[1 : 1 + done], refs[1 + done : 3 + done], refs[3 + done :]
    updated_hbm, bias_outs, (out_hbm, grads_hbm, last_back_ref, last_matrix_ref), refs = refs[:3], refs[3:6], refs[6:10], refs[10:]
    weights, (weight_load, weight_store, store), refs = refs[:3], refs[3:6], refs[6:]
    jobs = [
        scatter_job(
            m, WIDE, pl.ds(0, back_hbm.shape[2]), back_hbm.at[m], gots[m], scale_hbm, matrix_hbm.at[m], grads_hbm,
            refs[7 * m : 7 * m + 6], refs[7 * m + 6],
        )
        for m in range(done)
    ]
    weight_loads = [
        pltpu.make_async_copy(source, target, weight_load.at[i])
        for i, (source, target) in enumerate(zip(weights_hbm, weights))
    ]
    weight_stores = [
        pltpu.make_async_copy(source, target, weight_store.at[i])
        for i, (source, target) in enumerate(zip(weights, updated_hbm))
    ]
    moves = [
        pltpu.make_async_copy(source, target, store.at[i])
        for i, (source, target) in enumerate(
            [(part, out_hbm.at[m]) for m, part in enumerate(out_parts)]
            + [(back_hbm.at[done], last_back_ref), (matrix_hbm.at[done], last_matrix_ref)]
        )
    ]
    for item in jobs[0][0] + weight_loads:
        item.start()
    for later, _, _ in jobs[1:]:
        for item in later:
            item.start()
    for item in moves:
        item.start()
    jobs[0][1]()

    for item in weight_loads:
        item.wait()
    rows, width = weights[0].shape
    half = width // 2
    strip = min(rows, TILE // 2)
    own = table_ref[GROUP]
    for first in range(0, rows, strip):
        row_ids = first + lax.broadcasted_iota(jnp.int32, (strip, half), 0)
        used = row_ids < table_ref[STARTS + groups + own]
        down = slice(first, first + strip)
        for side in range(2):
            mine = (own & 1) == side
            here, there = own_ref[down, :], got_ref[down, :].astype(F32)
            columns = slice(side * half, (side + 1) * half)
            results = adamw_update(*(ref[down, columns] for ref in weights), jnp.where(mine, here, there), RATE_WEIGHT)
            for ref, result in zip(weights, results):
                ref[down, columns] = jnp.where(used, result, 0.0)
    for item in weight_stores:
        item.start()
    results = adamw_update(*(ref[...] for ref in biases), bias_grad_ref[...], RATE_BIAS)
    for ref, result in zip(bias_outs, results):
        ref[...] = result

    for _, work, _ in jobs[1:]:
        work()
    for item in weight_stores + moves:
        item.wait()
    for _, _, stores in jobs:
        for item in stores:
            item.wait()


def finish(table, groups, mine, other, bias_grad, biases, weights, outputs, backs, gots, scale, matrix, after=()):
    capacity, width = weights[0].shape
    nodes = outputs[0].array.shape[0]
    fixed = lambda i: (0, 0)
    scratch = [pltpu.VMEM((capacity, width), F32)] * 3 + [
        pltpu.SemaphoreType.DMA((3,)),
        pltpu.SemaphoreType.DMA((3,)),
        pltpu.SemaphoreType.DMA((MB + 2,)),
    ]
    for _ in gots:
        scratch += scatter_scratch(nodes, width)
    return launch(
        "finish", functools.partial(finish_kernel, groups), table,
        [(array, array.array.shape, fixed) for array in (mine, other)]
        + [(array, (1, width), fixed) for array in (bias_grad, *biases)]
        + [(array, None, None) for array in (*weights, *outputs, backs, *gots, scale, matrix)],
        [((capacity, width), F32, None, None)] * 3
        + [((1, width), F32, (1, width), fixed)] * 3
        + [((MB, nodes, width), BF16, None, None)] * 2
        + [((nodes, width), BF16, None, None, pltpu.VMEM), ((nodes, nodes), BF16, None, None, pltpu.VMEM)],
        after=after, scratch=scratch, vmem=32,
    )


def shards(
    features,
    neighbours,
    node_counts,
    row_counts,
    master_weight,
    weight_first,
    weight_second,
    master_bias,
    bias_first,
    bias_second,
    out_grad,
):
    groups = lax.axis_size("clus")
    capacity, width = master_weight.shape
    owner_ids = jnp.arange(groups, dtype=jnp.int32)
    starts = jnp.sum(jnp.where(owner_ids[None, :] < owner_ids[:, None], row_counts[None, :], 0), axis=1)
    table = jnp.concatenate(
        [
            jnp.stack([lax.axis_index("clus"), lax.axis_index("col")]).astype(jnp.int32),
            node_counts[:, 0],
            starts.astype(jnp.int32),
            row_counts,
        ]
    )
    bias_row, bias_first_row, bias_second_row = (
        array.reshape(1, width) for array in (master_bias, bias_first, bias_second)
    )

    lead = features[0]
    picked = [lead, *pick(features, tuple(range(1, MB)), [Kept(lead, None)])]
    far = [Kept(flip(array, "col", 2), None) for array in picked]

    matrix, scale, here, slots = front(
        table, groups, master_weight, jnp.swapaxes(neighbours, 1, 2), features, [picked[-1]]
    )
    scale = Kept(scale)
    weight, for_mate = (Kept(array) for array in place(table, slots))
    last = for_mate
    total, bias_sum = None, None
    outputs, pres, mates, away = [], [], [], []
    for m in range(MB):
        widths = (width - width // 4, width // 4) if m == MB - 1 else (width,)
        chunks = len(widths)
        out_m, pre_m, mate_m, *rest = batch(
            table, m, matrix, scale, far[m], here, weight, for_mate, out_grad, bias_row, total, bias_sum, widths,
            [last],
        )
        outputs.append(Kept(out_m))
        pres.append(pre_m)
        mates.append(mate_m)
        away.append([Kept(flip(chunk, "col", 2), None) for chunk in rest[:chunks]])
        total, bias_sum = Kept(rest[chunks]), rest[-1]
        last = bias_sum

    mate_weight, keep, sent, bias_sum = rest[chunks:]
    mine, other, bias_total, backs = sum_over_owners(
        table, groups, capacity, keep, sent, bias_sum, weight, mate_weight, pres, mates, [last]
    )
    *updated, outputs, input_grads, last_back, last_matrix = finish(
        table, groups, Kept(mine, None), Kept(other, None), bias_total, (bias_row, bias_first_row, bias_second_row),
        (master_weight, weight_first, weight_second), outputs, backs, [part[0] for part in away[:-1]],
        scale, matrix, [bias_total],
    )
    for chunk, got in enumerate(away[-1]):
        input_grads = scatter(MB - 1, sum(widths[:chunk]), Kept(last_back), got, scale, Kept(last_matrix), input_grads)
    return (outputs, input_grads, *updated[:3], *(row.reshape(width) for row in updated[3:]))


def solution(mesh):
    in_specs = (
        P(None, "clus", "col"),
        P(None, "clus", None),
        P(None, "clus"),
        P(),
        P("clus", "col"),
        P("clus", "col"),
        P("clus", "col"),
        P("col"),
        P("col"),
        P("col"),
        P(None, "clus", "col"),
    )
    out_specs = (
        P(None, "clus", "col"),
        P(None, "clus", "col"),
        P("clus", "col"),
        P("clus", "col"),
        P("clus", "col"),
        P("col"),
        P("col"),
        P("col"),
    )
    return jax.shard_map(shards, mesh=mesh, in_specs=in_specs, out_specs=out_specs, check_vma=False)
```
